32 devices in a mesh: dp: 8 (over z, y), tensor: 4 (over x, core).
Axes of the slice: x: 2, y: 2, z: 4, core: 2. Of those that a mesh axis runs over, the one named last changes fastest.
Arguments:
- tokens: bfloat16 [16384, 768], P(('dp', 'tensor')), may hold values from -6 to 6
- lengths: int32 [16, 8], P('dp'), may hold values from 1 to 256, 1024 in all within a row
- cotangent: bfloat16 [16384, 768], P(('dp', 'tensor')), may hold values from -6 to 6
- query_weight: bfloat16 [768, 768], P(None, 'tensor'), may hold values from -0.21875 to 0.21875
- query_bias: float32 [768], P('tensor'), may hold values from -3 to 3
- key_weight: bfloat16 [768, 768], P(None, 'tensor'), may hold values from -0.21875 to 0.21875
- value_weight: bfloat16 [768, 768], P(None, 'tensor'), may hold values from -0.21875 to 0.21875
- value_bias: float32 [768], P('tensor'), may hold values from -3 to 3
- out_weight: bfloat16 [768, 768], P('tensor'), may hold values from -1.25 to 1.25
- out_bias: float32 [768], replicated, may hold values from -3 to 3
- gain_one: float32 [768], replicated, may hold values from 0.25 to 1.75
- shift_one: float32 [768], replicated, may hold values from -3 to 3
- up_weight: bfloat16 [768, 3072], P(None, 'tensor'), may hold values from -0.21875 to 0.21875
- up_bias: float32 [3072], P('tensor'), may hold values from -3 to 3
- down_weight: bfloat16 [3072, 768], P('tensor'), may hold values from -0.109375 to 0.109375
- down_bias: float32 [768], replicated, may hold values from -3 to 3
- gain_two: float32 [768], replicated, may hold values from 0.25 to 1.75
- shift_two: float32 [768], replicated, may hold values from -3 to 3
Outputs:
- layer_output: bfloat16 [16384, 768], P(('dp', 'tensor'))
- tokens_grad: float32 [16384, 768], P(('dp', 'tensor'))
- query_weight_grad: float32 [768, 768], P(None, 'tensor')
- query_bias_grad: float32 [768], P('tensor')
- key_weight_grad: float32 [768, 768], P(None, 'tensor')
- value_weight_grad: float32 [768, 768], P(None, 'tensor')
- value_bias_grad: float32 [768], P('tensor')
- out_weight_grad: float32 [768, 768], P('tensor')
- out_bias_grad: float32 [768], replicated
- gain_one_grad: float32 [768], replicated
- shift_one_grad: float32 [768], replicated
- up_weight_grad: float32 [768, 3072], P(None, 'tensor')
- up_bias_grad: float32 [3072], P('tensor')
- down_weight_grad: float32 [3072, 768], P('tensor')
- down_bias_grad: float32 [768], replicated
- gain_two_grad: float32 [768], replicated
- shift_two_grad: float32 [768], replicated
The draws below stay inside these ranges and needn't reach their ends.
Inputs may be any that keep to these rules, and one draw needn't show every extreme that they name: Each row of lengths sums to 1024, and its largest entry is 256.
All inputs are finite; a program needn't handle non-finite values.
Results may differ from the reference program's by a relative error of at most 0.02.
Values may be sent and summed in bfloat16 or wider, within the bound.
No kernel may reach another device: no remote copies, remote signals or barrier semaphores. Data moves between devices by JAX's collectives and lax.ppermute only.
A program may use at most 128 MiB of HBM per device.

```python
import math
import jax
import jax.numpy as jnp
import numpy as np
from jax import lax

D = 768
HEADS = 12
HEAD_DIM = 64
FF = 3072
SEQ_LEN = 1024
NSEG = 8
MOST = 256
SEQS = 16
TOKENS = 16384


def levels(rng, extent, split, smallest, top_value):
    level = 1.0
    for axis_at, shards_of in split:
        heights = jax.random.uniform(jax.random.fold_in(jax.random.fold_in(rng, 6), axis_at), (shards_of,), jnp.float32, smallest / len(split), top_value / len(split))
        level = level * jnp.repeat(jnp.exp(heights), extent[axis_at] // shards_of).reshape((-1,) + (1,) * (len(extent) - 1 - axis_at))
    return level


def profile(amount, total, reach, slope):
    portions = [(1 << 20) // math.isqrt(grade ** slope) + 1 for grade in range(2, amount + 1)]
    surplus, given = total - reach - (amount - 1), [1] * (amount - 1)
    while surplus > 0:
        candidates = [i for i in range(amount - 1) if given[i] < reach]
        whole, budget = sum([portions[i] for i in candidates]), surplus
        for i in candidates:
            more = min(reach - given[i], max(1, budget * portions[i] // whole), surplus)
            given[i] = given[i] + more
            surplus = surplus - more
    return np.array([reach] + given)


def ragged_sizes(own_key, amount, total, most, skew):
    if amount == 2:
        one = jax.random.randint(own_key, (), max(1, total - most), min(most, total - 1) + 1)
        return jnp.stack([one, total - one])
    sizes = jnp.asarray(profile(amount, total, most, skew), jnp.int32)
    twos = (amount - 1) // 2
    giver, sink = sizes[1:1 + 2 * twos:2], sizes[2:2 + 2 * twos:2]
    room = jnp.minimum(giver - 1, most - sink)
    moved = jax.random.randint(jax.random.fold_in(own_key, 1), (twos,), 0, 1 << 20) % (room + 1)
    sizes = sizes.at[1:1 + 2 * twos:2].set(giver - moved).at[2:2 + 2 * twos:2].set(sink + moved)
    return sizes[jax.random.permutation(jax.random.fold_in(own_key, 2), amount)]


def normal_values(key, dims, spread, reach, split=(), held_as=jnp.bfloat16):
    level = levels(key, dims, split, -0.22, 0.18) if split else 1.0
    result = jax.random.normal(key, dims, jnp.float32) * spread * level
    return jnp.minimum(jnp.maximum(result, -reach), reach).astype(held_as)


def setup_inputs(seed: int = 0) -> dict:
    seeds = jax.random.split(jax.random.key(seed), 19)
    return {
        "tokens": normal_values(seeds[0], (TOKENS, D), 1.0, 6.0, ((0, 32),)),
        "lengths": jax.vmap(lambda own: ragged_sizes(own, NSEG, SEQ_LEN, MOST, 1))(jax.random.split(seeds[1], SEQS)).reshape((SEQS, NSEG)).astype(jnp.int32),
        "cotangent": normal_values(seeds[2], (TOKENS, D), 1.0, 6.0, ((0, 32),)),
        "query_weight": normal_values(seeds[3], (D, D), D ** -0.5, 0.21875, ((1, 4),)),
        "query_bias": normal_values(seeds[4], (D,), 0.5, 3.0, ((0, 4),), jnp.float32),
        "key_weight": normal_values(seeds[5], (D, D), D ** -0.5, 0.21875, ((1, 4),)),
        "value_weight": normal_values(seeds[6], (D, D), D ** -0.5, 0.21875, ((1, 4),)),
        "value_bias": normal_values(seeds[7], (D,), 0.5, 3.0, ((0, 4),), jnp.float32),
        "out_weight": normal_values(seeds[8], (D, D), (D // 32) ** -0.5, 1.25, ((0, 4),)),
        "out_bias": normal_values(seeds[9], (D,), 0.5, 3.0, (), jnp.float32),
        "gain_one": jnp.clip(1.0 + 0.15 * jax.random.normal(seeds[10], (D,), jnp.float32), 0.25, 1.75),
        "shift_one": normal_values(seeds[11], (D,), 0.5, 3.0, (), jnp.float32),
        "up_weight": normal_values(seeds[12], (D, FF), D ** -0.5, 0.21875, ((1, 4),)),
        "up_bias": normal_values(seeds[13], (FF,), 0.5, 3.0, ((0, 4),), jnp.float32),
        "down_weight": normal_values(seeds[14], (FF, D), FF ** -0.5, 0.109375, ((0, 4),)),
        "down_bias": normal_values(seeds[15], (D,), 0.5, 3.0, (), jnp.float32),
        "gain_two": jnp.clip(1.0 + 0.15 * jax.random.normal(seeds[16], (D,), jnp.float32), 0.25, 1.75),
        "shift_two": normal_values(seeds[17], (D,), 0.5, 3.0, (), jnp.float32),
    }


@jax.custom_vjp
def low(v):
    return lax.optimization_barrier(v.astype(jnp.bfloat16)).astype(jnp.float32)

@jax.custom_vjp
def low_back(v):
    return v

def low_keep(v):
    return (low(v), None)

def low_pass(kept, grad):
    return (grad,)

def back_keep(v):
    return (v, None)

def back_low(kept, grad):
    return (low(grad),)
low.defvjp(low_keep, low_pass)
low_back.defvjp(back_keep, back_low)

def matmul(left_side, right_side):
    return jnp.dot(left_side, right_side, precision=lax.Precision.HIGHEST, preferred_element_type=jnp.float32)

def layer_norm(values_in, gain, shift):
    row_mean = lax.optimization_barrier(jnp.mean(values_in, axis=-1, keepdims=True))
    centered = values_in - row_mean
    row_var = lax.optimization_barrier(jnp.mean(centered * centered, axis=-1, keepdims=True))
    return centered * lax.rsqrt(row_var + 1e-05) * gain + shift

def doc_mask(lengths, row_count):
    doc_ends = jnp.cumsum(lengths).astype(jnp.int32)
    places = jnp.arange(row_count, dtype=jnp.int32)
    segment = lax.optimization_barrier(jnp.sum((places[:, None] >= doc_ends[None, :]).astype(jnp.int32), axis=1)).astype(jnp.int32)
    return segment[:, None] == segment[None, :]

def one_sequence(params, inputs_one, lengths):
    query_weight, query_bias, key_weight, value_weight, value_bias, out_weight, out_bias, gain_one, shift_one, up_weight, up_bias, down_weight, down_bias, gain_two, shift_two = params
    row_count = inputs_one.shape[0]
    same_doc = doc_mask(lengths, row_count)
    low_tokens = low(inputs_one)
    queries = low(low_back(matmul(low_tokens, query_weight) + query_bias)).reshape(row_count, HEADS, HEAD_DIM)
    key_rows = low(low_back(matmul(low_tokens, key_weight))).reshape(row_count, HEADS, HEAD_DIM)
    value_rows = low(low_back(matmul(low_tokens, value_weight) + value_bias)).reshape(row_count, HEADS, HEAD_DIM)
    scores = jnp.einsum('qhd,khd->hqk', queries, key_rows, precision=lax.Precision.HIGHEST) * HEAD_DIM ** (-0.5)
    scores = low_back(jnp.where(same_doc[None], scores, -1e+30))
    row_top = lax.optimization_barrier(jnp.max(scores, axis=-1, keepdims=True))
    weights = jnp.exp(scores - row_top)
    prob_rows = low(weights / lax.optimization_barrier(jnp.sum(weights, axis=-1, keepdims=True)))
    context = jnp.einsum('hqk,khd->qhd', prob_rows, value_rows, precision=lax.Precision.HIGHEST)
    context = low(low_back(context.reshape(row_count, HEADS * HEAD_DIM)))
    attended = low_back(matmul(context, out_weight))
    hidden = layer_norm(inputs_one + attended + out_bias, gain_one, shift_one)
    pre_up = low_back(matmul(low(hidden), up_weight) + up_bias)
    active = low(jax.nn.gelu(pre_up, approximate=False))
    branch = low_back(matmul(active, down_weight))
    return layer_norm(hidden + branch + down_bias, gain_two, shift_two)

def reference(tokens, lengths, cotangent, query_weight, query_bias, key_weight, value_weight, value_bias, out_weight, out_bias, gain_one, shift_one, up_weight, up_bias, down_weight, down_bias, gain_two, shift_two):
    params = tuple((member.astype(jnp.float32) for member in (query_weight, query_bias, key_weight, value_weight, value_bias, out_weight, out_bias, gain_one, shift_one, up_weight, up_bias, down_weight, down_bias, gain_two, shift_two)))
    inputs = tokens.astype(jnp.float32).reshape(SEQS, SEQ_LEN, D)

    def forward(inputs_all, params_all):

        def single(pair):
            return one_sequence(params_all, pair[0], pair[1])
        return lax.map(jax.checkpoint(single), (inputs_all, lengths))
    outputs, pullback = jax.vjp(forward, inputs, params)
    grad_inputs, grads = pullback(cotangent.astype(jnp.float32).reshape(SEQS, SEQ_LEN, D))
    return (outputs.reshape(SEQS * SEQ_LEN, D).astype(jnp.bfloat16), grad_inputs.reshape(SEQS * SEQ_LEN, D), grads[0], grads[1], grads[2], grads[3], grads[4], grads[5], grads[6], grads[7], grads[8], grads[9], grads[10], grads[11], grads[12], grads[13], grads[14])
```

```python
import functools

import jax
import jax.numpy as jnp
from jax import lax
from jax.experimental import pallas as pl
from jax.experimental.pallas import tpu as pltpu
from jax.sharding import PartitionSpec as P

HEAD_DIM = 64
MOST = 256
EPSILON = 1e-05
MASKED = -1e30
QUERY_BLOCK = 256
UNIT_BLOCK = 256
EXTRA = 64
VMEM_LIMIT = 48 * 1024 * 1024

TAIL_SCALE = 0.425
TAIL = (
    0.23966740682492862,
    0.24201181237516,
    0.19964184258583956,
    0.2585875675603689,
    -0.10985333090134082,
    0.4147788772153898,
    -0.3173079260911745,
    0.07247363954140279,
)

BF16 = jnp.bfloat16
F32 = jnp.float32


def product(left_side, right_side):
    return jnp.dot(left_side, right_side, preferred_element_type=F32)


def rows_product(left_side, right_side):
    return lax.dot_general(
        left_side, right_side, (((0,), (0,)), ((), ())), preferred_element_type=F32
    )


def cols_product(left_side, right_side):
    return lax.dot_general(
        left_side, right_side, (((1,), (1,)), ((), ())), preferred_element_type=F32
    )


def norm_forward(values_in, gain, shift):
    row_mean = jnp.mean(values_in, axis=-1, keepdims=True)
    centered = values_in - row_mean
    row_var = jnp.mean(centered * centered, axis=-1, keepdims=True)
    inverse = lax.rsqrt(row_var + EPSILON)
    normal = centered * inverse
    return (normal * gain + shift, normal, inverse)


def norm_backward(upstream, normal, inverse, gain):
    scaled = upstream * gain
    first_mean = jnp.mean(scaled, axis=-1, keepdims=True)
    second_mean = jnp.mean(scaled * normal, axis=-1, keepdims=True)
    grad_in = inverse * (scaled - first_mean - normal * second_mean)
    return (grad_in, jnp.sum(upstream * normal, axis=0), jnp.sum(upstream, axis=0))


def normal_parts(z):
    size = jnp.abs(z)
    t = 1.0 / (1.0 + (TAIL_SCALE * 0.7071067811865476) * size)
    series = TAIL[-1]
    for factor in TAIL[-2::-1]:
        series = series * t + factor
    bell = jnp.exp(-0.5 * z * z)
    tail = (0.5 * bell) * (series * t)
    return jnp.where(z >= 0.0, 1.0 - tail, tail), bell * 0.3989422804014327


def attend_kernel(q_ref, kv_ref, seg_k_ref, seg_q_ref, context_ref, log_ref):
    width = context_ref.shape[1]
    bias = jnp.where(seg_k_ref[...] == seg_q_ref[...], 0.0, MASKED).astype(F32)
    for h in range(width // HEAD_DIM):
        low, high = h * HEAD_DIM, (h + 1) * HEAD_DIM
        queries = q_ref[:, low:high] * BF16(HEAD_DIM**-0.5)
        key_rows = kv_ref[:, width + low : width + high]
        value_rows = kv_ref[:, 2 * width + low : 2 * width + high]
        scores = cols_product(key_rows, queries) + bias
        top = jnp.max(scores, axis=0, keepdims=True)
        weights = jnp.exp(scores - top)
        total = jnp.sum(weights, axis=0, keepdims=True)
        low_probs = (weights * (1.0 / total)).astype(BF16)
        context = rows_product(value_rows, low_probs)
        context_ref[:, low:high] = context.T.astype(BF16)
        log_ref[h : h + 1, :] = top + jnp.log(total)


def attend(qkv, seg_k, seg_q, own):
    rows, columns = qkv.shape
    width = columns // 3
    heads = width // HEAD_DIM
    block = min(QUERY_BLOCK, own)
    return pl.pallas_call(
        attend_kernel,
        grid=(own // block,),
        in_specs=[
            pl.BlockSpec((block, columns), lambda i: (i, 0)),
            pl.BlockSpec((rows, columns), lambda i: (0, 0)),
            pl.BlockSpec((rows, 1), lambda i: (0, 0)),
            pl.BlockSpec((1, block), lambda i: (0, i)),
        ],
        out_specs=[
            pl.BlockSpec((block, width), lambda i: (i, 0)),
            pl.BlockSpec((8, block), lambda i: (0, i)),
        ],
        out_shape=[
            jax.ShapeDtypeStruct((own, width), BF16),
            jax.ShapeDtypeStruct((8, own), F32),
        ],
        compiler_params=pltpu.CompilerParams(vmem_limit_bytes=VMEM_LIMIT),
        cost_estimate=pl.CostEstimate(
            flops=16 * rows * own * width, bytes_accessed=4 * rows * columns, transcendentals=0
        ),
    )(qkv, qkv, seg_k, seg_q)


def attend_back_kernel(
    q_ref, kv_ref, seg_k_ref, seg_q_ref, log_ref, grad_ref, out_ref, keys_ref, values_ref
):
    step, steps = pl.program_id(0), pl.num_programs(0)
    rows, columns = out_ref.shape
    width = columns // 3
    block = q_ref.shape[0]

    @pl.when(step == 0)
    def start():
        keys_ref[...] = jnp.zeros_like(keys_ref)
        values_ref[...] = jnp.zeros_like(values_ref)
        out_ref[:, :width] = jnp.zeros((rows, width), BF16)

    bias = jnp.where(seg_k_ref[...] == seg_q_ref[...], 0.0, MASKED).astype(F32)
    grad_queries = []
    for h in range(width // HEAD_DIM):
        low, high = h * HEAD_DIM, (h + 1) * HEAD_DIM
        queries = q_ref[:, low:high] * BF16(HEAD_DIM**-0.5)
        key_rows = kv_ref[:, width + low : width + high]
        value_rows = kv_ref[:, 2 * width + low : 2 * width + high]
        grads = grad_ref[:, low:high]
        scores = cols_product(key_rows, queries) + bias
        probs = jnp.exp(scores - log_ref[h : h + 1, :])
        values_ref[:, low:high] += product(probs.astype(BF16), grads)
        grad_probs = cols_product(value_rows, grads)
        inner = jnp.sum(probs * grad_probs, axis=0, keepdims=True)
        grad_scores = (probs * (grad_probs - inner)).astype(BF16)
        keys_ref[:, low:high] += product(grad_scores, queries)
        grad_queries.append(rows_product(key_rows, grad_scores).T)
    here = pl.multiple_of(step * block, block)
    joined = jnp.concatenate(grad_queries, axis=1) * (HEAD_DIM**-0.5)
    out_ref[pl.ds(here, block), :width] = joined.astype(BF16)

    @pl.when(step == steps - 1)
    def finish():
        out_ref[:, width : 2 * width] = keys_ref[...].astype(BF16)
        out_ref[:, 2 * width :] = values_ref[...].astype(BF16)


def attend_back(qkv, seg_k, seg_q, log_total, grad_context, own):
    rows, columns = qkv.shape
    width = columns // 3
    block = min(QUERY_BLOCK, own)
    return pl.pallas_call(
        attend_back_kernel,
        grid=(own // block,),
        in_specs=[
            pl.BlockSpec((block, columns), lambda i: (i, 0)),
            pl.BlockSpec((rows, columns), lambda i: (0, 0)),
            pl.BlockSpec((rows, 1), lambda i: (0, 0)),
            pl.BlockSpec((1, block), lambda i: (0, i)),
            pl.BlockSpec((8, block), lambda i: (0, i)),
            pl.BlockSpec((block, width), lambda i: (i, 0)),
        ],
        out_specs=pl.BlockSpec((rows, columns), lambda i: (0, 0)),
        out_shape=jax.ShapeDtypeStruct((rows, columns), BF16),
        scratch_shapes=[pltpu.VMEM((rows, width), F32), pltpu.VMEM((rows, width), F32)],
        compiler_params=pltpu.CompilerParams(vmem_limit_bytes=VMEM_LIMIT),
        cost_estimate=pl.CostEstimate(
            flops=40 * rows * own * width, bytes_accessed=6 * rows * columns, transcendentals=0
        ),
    )(qkv, qkv, seg_k, seg_q, log_total, grad_context)


def feed_kernel(hidden_ref, up_ref, bias_ref, down_ref, sum_ref, active_ref, slope_ref, out_ref):
    @pl.when(pl.program_id(0) == 0)
    def start():
        out_ref[...] = sum_ref[...]

    pre_up = product(hidden_ref[...], up_ref[...]) + bias_ref[...]
    cumulative, density = normal_parts(pre_up)
    active = (pre_up * cumulative).astype(BF16)
    active_ref[...] = active
    slope_ref[...] = cumulative + pre_up * density
    out_ref[...] += product(active, down_ref[...])


def feed(hidden, up, bias, down, running):
    rows, model = hidden.shape
    units = up.shape[1]
    block = min(UNIT_BLOCK, units)
    return pl.pallas_call(
        feed_kernel,
        grid=(units // block,),
        in_specs=[
            pl.BlockSpec((rows, model), lambda i: (0, 0)),
            pl.BlockSpec((model, block), lambda i: (0, i)),
            pl.BlockSpec((1, block), lambda i: (0, i)),
            pl.BlockSpec((block, model), lambda i: (i, 0)),
            pl.BlockSpec((rows, model), lambda i: (0, 0)),
        ],
        out_specs=[
            pl.BlockSpec((rows, block), lambda i: (0, i)),
            pl.BlockSpec((rows, block), lambda i: (0, i)),
            pl.BlockSpec((rows, model), lambda i: (0, 0)),
        ],
        out_shape=[
            jax.ShapeDtypeStruct((rows, units), BF16),
            jax.ShapeDtypeStruct((rows, units), F32),
            jax.ShapeDtypeStruct((rows, model), F32),
        ],
        compiler_params=pltpu.CompilerParams(vmem_limit_bytes=VMEM_LIMIT),
        cost_estimate=pl.CostEstimate(
            flops=6 * rows * model * units, bytes_accessed=8 * rows * units, transcendentals=0
        ),
    )(hidden, up, bias, down, running)


def body(
    dp_size,
    tokens,
    lengths,
    cotangent,
    query_weight,
    query_bias,
    key_weight,
    value_weight,
    value_bias,
    out_weight,
    out_bias,
    gain_one,
    shift_one,
    up_weight,
    up_bias,
    down_weight,
    down_bias,
    gain_two,
    shift_two,
):
    own, model = tokens.shape
    width = query_weight.shape[1]
    units = up_weight.shape[1]
    place = lax.axis_index("tensor")
    replica = lax.axis_index("dp")
    half_row = place % 2

    def swap_core(values_in):
        return lax.ppermute(values_in, "tensor", [(i, i ^ 1) for i in range(4)])

    def swap_chip(values_in):
        return lax.ppermute(values_in, "tensor", [(i, i ^ 2) for i in range(4)])

    def swap_replica(values_in, bit):
        return lax.ppermute(values_in, "dp", [(i, i ^ (1 << bit)) for i in range(dp_size)])

    def spread(values_in):
        second = swap_core(values_in)
        third = swap_chip(values_in)
        fourth = swap_core(third)
        return (values_in, second, third, fourth)

    halo = swap_core(jnp.where(half_row == 0, tokens[own - MOST :], tokens[:MOST]))
    inputs_full = jnp.concatenate([tokens, halo], axis=0)
    total_rows = own + MOST
    doc_ends = jnp.cumsum(lax.dynamic_index_in_dim(lengths, place // 2, 0, keepdims=False))
    spot = jnp.arange(total_rows, dtype=jnp.int32)
    base = jnp.where(half_row == 0, 0, own)
    halo_base = jnp.where(half_row == 0, own, own - MOST)
    spot = jnp.where(spot < own, base + spot, halo_base + spot - own)
    segment = jnp.sum((spot[:, None] >= doc_ends[None, :]).astype(jnp.int32), axis=1)
    seg_k = segment[:, None]
    seg_q = segment[None, :own]

    biases = jnp.concatenate([query_bias, value_bias, up_bias]).reshape(-1, 128)
    biases = [b.reshape(-1) for b in spread(biases)]
    query_biases = [b[:width] for b in biases]
    value_biases = [b[width : 2 * width] for b in biases]
    up_biases = [b[2 * width :] for b in biases]
    projections = spread(jnp.concatenate([query_weight, key_weight, value_weight], axis=1))
    out_weights = spread(out_weight)
    ups = spread(up_weight)
    downs = spread(down_weight)

    mix_one = tokens.astype(F32) + out_bias
    saved = []
    for j in range(4):
        bias = jnp.concatenate([query_biases[j], jnp.zeros((width,), F32), value_biases[j]])
        qkv = (product(inputs_full, projections[j]) + bias).astype(BF16)
        context, log_total = attend(qkv, seg_k, seg_q, own)
        mix_one = mix_one + product(context, out_weights[j])
        saved.append((qkv, context, log_total))
    hidden, normal_one, inverse_one = norm_forward(mix_one, gain_one, shift_one)
    low_hidden = hidden.astype(BF16)

    mix_two = hidden + down_bias
    actives, slopes = [], []
    for j in range(4):
        active, slope, mix_two = feed(low_hidden, ups[j], up_biases[j][None], downs[j], mix_two)
        actives.append(active)
        slopes.append(slope)
    layer_output, normal_two, inverse_two = norm_forward(mix_two, gain_two, shift_two)
    grad_two, gain_two_grad, shift_two_grad = norm_backward(
        cotangent.astype(F32), normal_two, inverse_two, gain_two
    )
    down_bias_grad = jnp.sum(grad_two, axis=0)
    low_grad_two = grad_two.astype(BF16)

    def reduce_tensor(parts):
        mine = (parts[0].astype(F32) + swap_core(parts[1]).astype(F32)).astype(BF16)
        theirs = (parts[2].astype(F32) + swap_core(parts[3]).astype(F32)).astype(BF16)
        mine = lax.optimization_barrier(mine)
        return (mine.astype(F32) + swap_chip(theirs).astype(F32)).astype(BF16)

    def reduce_replicas(values_in):
        bits = dp_size.bit_length() - 1
        now = values_in
        for bit in range(bits):
            upper = (replica >> bit) & 1
            half = now.shape[0] // 2
            send = lax.dynamic_slice_in_dim(now, (1 - upper) * half, half, 0)
            keep = lax.dynamic_slice_in_dim(now, upper * half, half, 0)
            now = (keep.astype(F32) + swap_replica(send, bit).astype(F32)).astype(BF16)
        for bit in range(bits - 1, -1, -1):
            upper = (replica >> bit) & 1
            other = swap_replica(now, bit)
            now = jnp.where(
                upper == 1,
                jnp.concatenate([other, now], axis=0),
                jnp.concatenate([now, other], axis=0),
            )
        return now.astype(F32)

    grad_hidden = grad_two
    down_grads, up_grads, up_bias_grads = [None] * 4, [None] * 4, [None] * 4
    for j in (1, 3, 2, 0):
        grad_pre = (slopes[j] * cols_product(low_grad_two, downs[j])).astype(BF16)
        down_grads[j] = rows_product(actives[j], low_grad_two).astype(BF16)
        up_grads[j] = rows_product(low_hidden, grad_pre).astype(BF16)
        up_bias_grads[j] = jnp.sum(grad_pre, axis=0, dtype=F32)
        grad_hidden = grad_hidden + cols_product(grad_pre, ups[j])
    down_weight_grad = reduce_replicas(reduce_tensor(down_grads))
    grad_one, gain_one_grad, shift_one_grad = norm_backward(
        grad_hidden, normal_one, inverse_one, gain_one
    )
    out_bias_grad = jnp.sum(grad_one, axis=0)
    low_grad_one = grad_one.astype(BF16)

    out_grads = [rows_product(saved[j][1], low_grad_one).astype(BF16) for j in range(4)]
    packed = [jnp.concatenate([up_grads[j], out_grads[j]], axis=0) for j in range(4)]
    packed = reduce_replicas(reduce_tensor(packed))
    up_weight_grad, out_weight_grad = packed[:model], packed[model:]

    shared = [out_bias_grad, gain_one_grad, shift_one_grad, down_bias_grad, gain_two_grad, shift_two_grad]
    tokens_sum = jnp.zeros((total_rows, model), F32)
    last = [None] * 4
    for j in (1, 3, 2, 0):
        qkv, context, log_total = saved[j]
        grad_context = cols_product(low_grad_one, out_weights[j]).astype(BF16)
        grad_qkv = attend_back(qkv, seg_k, seg_q, log_total, grad_context, own)
        sums = jnp.sum(grad_qkv, axis=0, dtype=F32)
        row = jnp.concatenate(
            [sums[:width], sums[2 * width :], jnp.zeros((model - 2 * width,), F32)]
        )
        extras = jnp.stack(shared + [up_bias_grads[j], row], axis=1).astype(BF16)
        extras = jnp.pad(extras, ((0, 0), (0, EXTRA - extras.shape[1])))
        last[j] = jnp.concatenate(
            [rows_product(inputs_full, grad_qkv).astype(BF16), extras], axis=1
        )
        tokens_sum = tokens_sum + cols_product(grad_qkv, projections[j])
    last = reduce_replicas(reduce_tensor(last))
    from_halo = swap_core(tokens_sum[own:].astype(BF16)).astype(F32)
    tokens_grad = grad_one + tokens_sum[:own]
    blank = jnp.zeros((own - MOST, model), F32)
    tokens_grad = tokens_grad + jnp.where(
        half_row == 0,
        jnp.concatenate([blank, from_halo], axis=0),
        jnp.concatenate([from_halo, blank], axis=0),
    )
    vectors = last[:, 3 * width : 3 * width + 8].T
    return (
        layer_output.astype(BF16),
        tokens_grad,
        last[:, :width],
        vectors[7, :width],
        last[:, width : 2 * width],
        last[:, 2 * width : 3 * width],
        vectors[7, width : 2 * width],
        out_weight_grad,
        vectors[0],
        vectors[1],
        vectors[2],
        up_weight_grad,
        vectors[6],
        down_weight_grad,
        vectors[3],
        vectors[4],
        vectors[5],
    )


def solution(mesh):
    placed = (
        P(("dp", "tensor"), None),
        P("dp", None),
        P(("dp", "tensor"), None),
        P(None, "tensor"),
        P("tensor"),
        P(None, "tensor"),
        P(None, "tensor"),
        P("tensor"),
        P("tensor", None),
        P(),
        P(),
        P(),
        P(None, "tensor"),
        P("tensor"),
        P("tensor", None),
        P(),
        P(),
        P(),
    )
    return jax.shard_map(
        functools.partial(body, mesh.shape["dp"]),
        mesh=mesh,
        in_specs=placed,
        out_specs=(
            P(("dp", "tensor"), None),
            P(("dp", "tensor"), None),
            P(None, "tensor"),
            P("tensor"),
            P(None, "tensor"),
            P(None, "tensor"),
            P("tensor"),
            P("tensor", None),
            P(),
            P(),
            P(),
            P(None, "tensor"),
            P("tensor"),
            P("tensor", None),
            P(),
            P(),
            P(),
        ),
        check_vma=False,
    )
```

```python
import functools

import jax
import jax.numpy as jnp
from jax import lax
from jax.experimental import pallas as pl
from jax.experimental.pallas import tpu as pltpu
from jax.sharding import PartitionSpec as P

HEAD_DIM = 64
MOST = 256
EPSILON = 1e-05
MASKED = -1e30
BLOCK = 256
STRIP = 64
BIAS_ROWS = 16
VMEM_LIMIT = 16 * 1024 * 1024
PACK_LIMIT = 60 * 1024 * 1024
COST = 3.6e6
TAIL_SCALE = 0.425
TAIL = (
    0.23966740682492862,
    0.24201181237516,
    0.19964184258583956,
    0.2585875675603689,
    -0.10985333090134082,
    0.4147788772153898,
    -0.3173079260911745,
    0.07247363954140279,
)

BF16 = jnp.bfloat16
F32 = jnp.float32


def product(left_side, right_side):
    return jnp.dot(left_side, right_side, preferred_element_type=F32)


def rows_product(left_side, right_side):
    return lax.dot_general(
        left_side, right_side, (((0,), (0,)), ((), ())), preferred_element_type=F32
    )


def cols_product(left_side, right_side):
    return lax.dot_general(
        left_side, right_side, (((1,), (1,)), ((), ())), preferred_element_type=F32
    )


def normal_parts(z):
    size = jnp.abs(z)
    t = 1.0 / (1.0 + (TAIL_SCALE * 0.7071067811865476) * size)
    series = TAIL[-1]
    for factor in TAIL[-2::-1]:
        series = series * t + factor
    bell = jnp.exp(-0.5 * z * z)
    tail = (0.5 * bell) * (series * t)
    return jnp.where(z >= 0.0, 1.0 - tail, tail), bell * 0.3989422804014327


def call(kernel, outs, args, scalars=0, scratch=(), cost=1.0, far=()):
    specs = [pl.BlockSpec(memory_space=pltpu.SMEM)] * scalars
    specs += [pl.BlockSpec(memory_space=pltpu.VMEM)] * (len(args) + len(outs) - scalars)
    for i in far:
        specs[i] = pl.BlockSpec(memory_space=pl.ANY)
    outputs = pl.pallas_call(
        kernel,
        in_specs=specs[: len(args)],
        out_specs=specs[len(args) :],
        out_shape=[jax.ShapeDtypeStruct(shape, dtype) for shape, dtype in outs],
        scratch_shapes=list(scratch),
        compiler_params=pltpu.CompilerParams(vmem_limit_bytes=VMEM_LIMIT),
        cost_estimate=pl.CostEstimate(
            flops=1, bytes_accessed=int(cost * COST), transcendentals=0
        ),
    )(*args)
    return list(outputs)


def piece(index, size):
    return pl.ds(pl.multiple_of(index * size, 16), size)


def assemble(flags_ref, refs, out_ref):
    size = refs[0].shape[0]
    side = flags_ref[0] * 2
    for ref, index in zip(refs, (side, side + 1, 2 - side, 3 - side)):
        out_ref[piece(index, size), :] = ref[...]


def pack_kernel(
    flags_ref, query_b_ref, value_b_ref, up_b_ref, query_ref, key_ref, value_ref, out_w_ref, tokens_ref, up_ref, down_ref,
    pack_ref, pack_a, pack_b, up_a, up_b, down_a, down_b, halo_ref,
    weights, pack_near, up_near, down_near, halo_near, sems,
):
    side, half_row = flags_ref[0], flags_ref[1]
    width, model = query_ref.shape
    size = width + BIAS_ROWS
    quarter = up_a.shape[0]
    copies = []

    def move(source, target):
        copies.append(pltpu.make_async_copy(source, target, sems.at[len(copies)]))
        copies[-1].start()

    for i, ref in enumerate((query_ref, key_ref, value_ref, out_w_ref)):
        move(ref, weights.at[i * width : (i + 1) * width])
    both = pl.ds(pl.multiple_of(side * 2 * quarter, 128), 2 * quarter)
    start = pl.multiple_of((1 - half_row) * (tokens_ref.shape[0] - MOST), 128)
    move(tokens_ref.at[pl.ds(start, MOST)], halo_near)
    move(up_ref.at[both], up_near)
    move(down_ref.at[both], down_near)
    blank = jnp.zeros((1, model - 2 * width), F32)
    rows = []
    for row in (up_b_ref[...], jnp.concatenate([query_b_ref[...], value_b_ref[...], blank], axis=1)):
        for _ in range(3):
            rows.append(row.astype(BF16).astype(F32))
            row = row - rows[-1]
    rows.append(jnp.zeros((BIAS_ROWS - 6, model), F32))
    biases = jnp.concatenate(rows, axis=0).astype(BF16)
    for i in range(4):
        copies[i].wait()
        pack_near[i * size + width : (i + 1) * size, :] = biases
        pack_near[i * size : i * size + width, :] = weights[i * width : (i + 1) * width, :]
    for index, out in ((0, pack_a), (1, pack_b)):
        move(pack_near.at[piece(side * 2 + index, size)], out)
    move(pack_near, pack_ref)
    copies[4].wait()
    move(halo_near, halo_ref)
    for i, near, outs in ((5, up_near, (up_a, up_b)), (6, down_near, (down_a, down_b))):
        copies[i].wait()
        for index, out in enumerate(outs):
            move(near.at[index * quarter : (index + 1) * quarter], out)
    for copy in copies[7:]:
        copy.wait()


def segments(flags_ref, lengths_ref, spot):
    ends = 0
    segment = jnp.zeros_like(spot)
    for d in range(lengths_ref.shape[1]):
        ends = ends + lengths_ref[flags_ref[2], d]
        segment = segment + (spot >= ends).astype(jnp.int32)
    return segment


def masks(flags_ref, lengths_ref, own, rows):
    half_row = flags_ref[1]
    spot = lax.broadcasted_iota(jnp.int32, (rows, 1), 0)
    halo = jnp.where(half_row == 0, spot, spot - MOST)
    keys = jnp.where(spot < own, spot + half_row * own, halo)
    queries = lax.broadcasted_iota(jnp.int32, (1, own), 1) + half_row * own
    return segments(flags_ref, lengths_ref, keys), segments(flags_ref, lengths_ref, queries)


def attend_kernel(given, first, flags_ref, lengths_ref, *refs):
    w_refs, refs = refs[:given], refs[given:]
    if first:
        tokens_ref, halo_ref, x_ref, refs = refs[0], refs[1], refs[2], refs[3:]
        x_ref[: tokens_ref.shape[0], :] = tokens_ref[...]
        x_ref[tokens_ref.shape[0] :, :] = halo_ref[...]
    else:
        x_ref, refs = refs[0], refs[1:]
    if given > 1:
        w_ref, refs = refs[0], refs[1:]
        assemble(flags_ref, w_refs, w_ref)
    else:
        w_ref = w_refs[0]
    qkv_ref, context_ref, turned_ref, log_ref, bias_ref, seg_ref = refs
    rows, model = x_ref.shape
    own, width = context_ref.shape
    size = width + BIAS_ROWS
    parts = w_ref[width : width + 6, :].astype(F32)
    bias_ref[0:1, :] = parts[0:1] + parts[1:2] + parts[2:3]
    mixed = parts[3:4] + parts[4:5] + parts[5:6]
    for i, bias in enumerate((mixed[:, :width], None, mixed[:, width : 2 * width])):
        weights = w_ref[i * size : i * size + width, :]
        for r in range(0, rows, BLOCK):
            total = cols_product(x_ref[r : r + BLOCK, :], weights)
            if bias is not None:
                total = total + bias
            qkv_ref[r : r + BLOCK, i * width : (i + 1) * width] = total.astype(BF16)
    seg_k, seg_q = masks(flags_ref, lengths_ref, own, rows)
    seg_ref[...] = seg_q

    def one_block(i, carry):
        here = pl.ds(pl.multiple_of(i * BLOCK, BLOCK), BLOCK)
        bias = jnp.where(seg_k == seg_ref[:, here], 0.0, MASKED).astype(F32)
        contexts = []
        for h in range(width // HEAD_DIM):
            low, high = h * HEAD_DIM, (h + 1) * HEAD_DIM
            queries = qkv_ref[here, low:high] * BF16(HEAD_DIM**-0.5)
            key_rows = qkv_ref[:, width + low : width + high]
            value_rows = qkv_ref[:, 2 * width + low : 2 * width + high]
            scores = cols_product(key_rows, queries) + bias
            top = jnp.max(scores, axis=0, keepdims=True)
            weights = jnp.exp(scores - top)
            total = jnp.sum(weights, axis=0, keepdims=True)
            low_probs = (weights * (1.0 / total)).astype(BF16)
            context = rows_product(value_rows, low_probs)
            turned_ref[low:high, here] = context.astype(BF16)
            contexts.append(context.T)
            log_ref[h : h + 1, here] = top + jnp.log(total)
        context_ref[here, :] = jnp.concatenate(contexts, axis=1).astype(BF16)
        return carry

    lax.fori_loop(0, own // BLOCK, one_block, 0)


def mid_kernel(tokens_ref, *refs):
    contexts, shards, refs = refs[:4], refs[4:8], refs[8:]
    out_b_ref, gain_ref, shift_ref, normal_ref, inverse_ref, hidden_ref, turned_ref, mix_ref = refs
    own, model = tokens_ref.shape
    width = contexts[0].shape[1]
    size = width + BIAS_ROWS
    mix_ref[...] = tokens_ref[...].astype(F32) + out_b_ref[...]
    for context_ref, ref in zip(contexts, shards):
        mix_ref[...] += product(context_ref[...], ref[3 * size : 3 * size + width, :])

    def strip(i, carry):
        here = pl.ds(pl.multiple_of(i * STRIP, STRIP), STRIP)
        values = mix_ref[here, :]
        centered = values - jnp.mean(values, axis=1, keepdims=True)
        inverse = lax.rsqrt(jnp.mean(centered * centered, axis=1, keepdims=True) + EPSILON)
        normal = centered * inverse
        normal_ref[here, :] = normal
        inverse_ref[here, :] = inverse
        hidden_ref[here, :] = (normal * gain_ref[...] + shift_ref[...]).astype(BF16)
        return carry

    lax.fori_loop(0, own // STRIP, strip, 0, unroll=2)
    turned_ref[...] = hidden_ref[...].T


def feed_units(hidden_ref, up_ref, down_ref, bias_ref, active_ref, slope_ref, sum_ref, first):
    units = bias_ref.shape[1]
    for u in range(0, units, BLOCK):
        pre_up = bias_ref[0:1, u : u + BLOCK] + product(hidden_ref[...], up_ref[:, u : u + BLOCK])
        cumulative, density = normal_parts(pre_up)
        active = (pre_up * cumulative).astype(BF16)
        active_ref[u : u + BLOCK, :] = active.T
        slope_ref[:, u : u + BLOCK] = (cumulative + pre_up * density).astype(BF16)
        now = product(active, down_ref[u : u + BLOCK, :])
        if first and u == 0:
            sum_ref[...] = now
        else:
            sum_ref[...] += now


def feed_kernel(hidden_ref, up_a, up_b, down_a, down_b, bias_a, bias_b, act_a, act_b, slope_a, slope_b, sum_ref):
    feed_units(hidden_ref, up_a, down_a, bias_a, act_a, slope_a, sum_ref, True)
    feed_units(hidden_ref, up_b, down_b, bias_b, act_b, slope_b, sum_ref, False)


def feed_last_kernel(flags_ref, hidden_ref, *refs):
    pieces, refs = refs[:16], refs[16:]
    (
        bias_a, bias_b, partial_ref,
        normal_ref, gain_one_ref, shift_one_ref, down_b_ref, gain_ref, shift_ref, cotangent_ref,
        act_a, act_b, slope_a, slope_b, out_ref, grad_ref, low_ref, vector_ref, up_a, up_b, down_a, down_b, sum_ref,
    ) = refs
    own, model = hidden_ref.shape
    for i, ref in enumerate((up_a, up_b, down_a, down_b)):
        assemble(flags_ref, pieces[4 * i : 4 * i + 4], ref)
    feed_units(hidden_ref, up_a, down_a, bias_a, act_a, slope_a, sum_ref, True)
    feed_units(hidden_ref, up_b, down_b, bias_b, act_b, slope_b, sum_ref, False)
    vector_ref[...] = jnp.zeros_like(vector_ref)

    def strip(i, carry):
        here = pl.ds(pl.multiple_of(i * STRIP, STRIP), STRIP)
        values = sum_ref[here, :] + partial_ref[here, :] + down_b_ref[...]
        values = values + (normal_ref[here, :] * gain_one_ref[...] + shift_one_ref[...])
        centered = values - jnp.mean(values, axis=1, keepdims=True)
        inverse = lax.rsqrt(jnp.mean(centered * centered, axis=1, keepdims=True) + EPSILON)
        normal = centered * inverse
        out_ref[here, :] = (normal * gain_ref[...] + shift_ref[...]).astype(BF16)
        upstream = cotangent_ref[here, :].astype(F32)
        scaled = upstream * gain_ref[...]
        first = jnp.mean(scaled, axis=1, keepdims=True)
        second = jnp.mean(scaled * normal, axis=1, keepdims=True)
        grad = inverse * (scaled - first - normal * second)
        grad_ref[here, :] = grad
        low_ref[here, :] = grad.astype(BF16)
        vector_ref[0:1, :] += jnp.sum(upstream * normal, axis=0, keepdims=True)
        vector_ref[1:2, :] += jnp.sum(upstream, axis=0, keepdims=True)
        vector_ref[2:3, :] += jnp.sum(grad, axis=0, keepdims=True)
        return carry

    lax.fori_loop(0, own // STRIP, strip, 0, unroll=2)


def quarters(flags_ref, size):
    return [pl.ds(pl.multiple_of(jnp.bitwise_xor(flags_ref[4], i) * size, 16), size) for i in range(4)]


def feed_back_kernel(received, last, flags_ref, grad_ref, active_ref, slope_ref, hidden_ref, up_ref, down_ref, *refs):
    if received:
        got, refs = refs[:2], refs[2:]
    sum_in, refs = refs[0], refs[1:]
    if last:
        normal_ref, inverse_ref, gain_ref = refs[:3]
        refs = refs[3:]
    up_grad_ref, down_grad_ref, bias_grad_ref, sum_ref = refs[:4]
    refs = refs[4:]
    own, model = grad_ref.shape
    units = slope_ref.shape[1]
    grad_pre_ref = refs[-1]
    up_rows, down_rows = quarters(flags_ref, model // 4), quarters(flags_ref, units // 4)
    for i in range(4):
        value = product(active_ref[i * (units // 4) : (i + 1) * (units // 4), :], grad_ref[...])
        if received:
            value = value + got[1][down_rows[i], :].astype(F32)
        down_grad_ref[down_rows[i], :] = value.astype(BF16)
    for u in range(0, units, BLOCK):
        here = slice(u, u + BLOCK)
        grad_active = cols_product(grad_ref[...], down_ref[here, :])
        grad_pre = (slope_ref[:, here].astype(F32) * grad_active).astype(BF16)
        grad_pre_ref[:, here] = grad_pre
        bias_grad_ref[0:1, here] = jnp.sum(grad_pre.astype(F32), axis=0, keepdims=True)
    for i in range(4):
        value = product(hidden_ref[i * (model // 4) : (i + 1) * (model // 4), :], grad_pre_ref[...])
        if received:
            value = value + got[0][up_rows[i], :].astype(F32)
        up_grad_ref[up_rows[i], :] = value.astype(BF16)
    sum_ref[...] = sum_in[...] + cols_product(grad_pre_ref[...], up_ref[...])
    if not last:
        return
    low_ref, vector_ref = refs[:2]
    vector_ref[...] = jnp.zeros_like(vector_ref)

    def strip(i, carry):
        here = pl.ds(pl.multiple_of(i * STRIP, STRIP), STRIP)
        upstream, normal = sum_ref[here, :], normal_ref[here, :]
        scaled = upstream * gain_ref[...]
        first = jnp.mean(scaled, axis=1, keepdims=True)
        second = jnp.mean(scaled * normal, axis=1, keepdims=True)
        grad = inverse_ref[here, :] * (scaled - first - normal * second)
        sum_ref[here, :] = grad
        low_ref[here, :] = grad.astype(BF16)
        vector_ref[0:1, :] += jnp.sum(grad, axis=0, keepdims=True)
        vector_ref[1:2, :] += jnp.sum(upstream * normal, axis=0, keepdims=True)
        vector_ref[2:3, :] += jnp.sum(upstream, axis=0, keepdims=True)
        return carry

    lax.fori_loop(0, own // STRIP, strip, 0, unroll=2)


def attend_back_kernel(received, flags_ref, lengths_ref, *refs):
    x_ref, grad_ref, qkv_ref, context_ref, log_ref, w_ref, refs = *refs[:6], refs[6:]
    if received:
        got, refs = refs[0], refs[1:]
    out_ref, plain_ref, bias_ref = refs[:3]
    grad_context_ref, turned_ref, keys_ref, values_ref, seg_ref = refs[3:]
    rows, model = x_ref.shape
    own = grad_ref.shape[0]
    width = qkv_ref.shape[1] // 3
    size = width + BIAS_ROWS
    grad_context_ref[...] = cols_product(grad_ref[...], w_ref[3 * size : 3 * size + width, :]).astype(BF16)
    keys_ref[...] = jnp.zeros_like(keys_ref)
    values_ref[...] = jnp.zeros_like(values_ref)
    plain_ref[own:, :width] = jnp.zeros((rows - own, width), BF16)
    turned_ref[:width, own:] = jnp.zeros((width, rows - own), BF16)
    seg_k, seg_q = masks(flags_ref, lengths_ref, own, rows)
    seg_ref[...] = seg_q

    def one_block(i, carry):
        here = pl.ds(pl.multiple_of(i * BLOCK, BLOCK), BLOCK)
        bias = jnp.where(seg_k == seg_ref[:, here], 0.0, MASKED).astype(F32)
        for h in range(width // HEAD_DIM):
            low, high = h * HEAD_DIM, (h + 1) * HEAD_DIM
            queries = qkv_ref[here, low:high] * BF16(HEAD_DIM**-0.5)
            key_rows = qkv_ref[:, width + low : width + high]
            value_rows = qkv_ref[:, 2 * width + low : 2 * width + high]
            grads = grad_context_ref[here, low:high]
            scores = cols_product(key_rows, queries) + bias
            probs = jnp.exp(scores - log_ref[h : h + 1, here])
            values_ref[:, low:high] += product(probs.astype(BF16), grads)
            grad_probs = cols_product(value_rows, grads)
            inner = jnp.sum(probs * grad_probs, axis=0, keepdims=True)
            grad_scores = (probs * (grad_probs - inner)).astype(BF16)
            keys_ref[:, low:high] += product(grad_scores, queries)
            grad_queries = rows_product(key_rows, grad_scores) * (HEAD_DIM**-0.5)
            turned_ref[low:high, here] = grad_queries.astype(BF16)
        return carry

    lax.fori_loop(0, own // BLOCK, one_block, 0)
    plain_ref[:own, :width] = turned_ref[:width, :own].T
    plain_ref[:, width : 2 * width] = keys_ref[...].astype(BF16)
    plain_ref[:, 2 * width :] = values_ref[...].astype(BF16)
    turned_ref[width:, :] = plain_ref[:, width:].T
    bias_ref[0:1, :] = jnp.sum(plain_ref[...].astype(F32), axis=0, keepdims=True)
    for i, here in enumerate(quarters(flags_ref, width)):
        if i < 3:
            grad = product(turned_ref[i * width : (i + 1) * width, :], x_ref[...])
        else:
            grad = product(context_ref[...], grad_ref[...])
        if received:
            grad = grad + got[here, :].astype(F32)
        out_ref[here, :] = grad.astype(BF16)


def tokens_kernel(flags_ref, grad_ref, *refs):
    plains, shards, out_ref, halo_ref = refs[:4], refs[4:8], refs[8], refs[9]
    own, model = grad_ref.shape
    rows, columns = plains[0].shape
    width = columns // 3
    size = width + BIAS_ROWS
    for r in range(0, rows, BLOCK):
        total = grad_ref[r : r + BLOCK, :] if r < own else 0.0
        for plain, shard in zip(plains, shards):
            for i in range(3):
                total = total + product(
                    plain[r : r + BLOCK, i * width : (i + 1) * width], shard[i * size : i * size + width, :]
                )
        if r < own:
            out_ref[r : r + BLOCK, :] = total
        else:
            halo_ref[r - own : r - own + BLOCK, :] = total.astype(BF16)


def last_kernel(flags_ref, total_ref, halo_ref, out_ref):
    out_ref[...] = total_ref[...]
    start = pl.multiple_of((1 - flags_ref[1]) * (total_ref.shape[0] - MOST), 128)
    out_ref[pl.ds(start, MOST), :] += halo_ref[...].astype(F32)


def vectors_kernel(place_ref, one_ref, two_ref, *refs):
    ups, qkvs, out_ref = refs[:4], refs[4:8], refs[8]
    model = one_ref.shape[1]
    width = qkvs[0].shape[1] // 3
    out_ref[0:3, :] = one_ref[0:3, :]
    out_ref[3:6, :] = two_ref[0:3, :]
    out_ref[14:16, :] = jnp.zeros((2, model), F32)
    blank = jnp.zeros((1, model - 2 * width), F32)
    for j in range(4):
        spot = jnp.bitwise_xor(place_ref[3], j)
        out_ref[pl.ds(6 + spot, 1), :] = ups[j][0:1, :]
        row = [qkvs[j][0:1, :width], qkvs[j][0:1, 2 * width :], blank]
        out_ref[pl.ds(10 + spot, 1), :] = jnp.concatenate(row, axis=1)


def tie(*arrays):
    return lax.optimization_barrier(arrays)


def add(*members):
    members = [m.astype(F32) for m in members]
    while len(members) > 1:
        members = [a + b for a, b in zip(members[::2], members[1::2])]
    return members[0].astype(BF16)


class Swaps:
    def __init__(self, dp_size, replica):
        self.dp_size, self.near = dp_size, replica & 3

    def core(self, values_in):
        return lax.ppermute(values_in, "tensor", [(i, i ^ 1) for i in range(4)])

    def chip(self, values_in):
        return lax.ppermute(values_in, "tensor", [(i, i ^ 2) for i in range(4)])

    def replica(self, values_in, mask):
        return lax.ppermute(values_in, "dp", [(i, i ^ mask) for i in range(self.dp_size)])

    def scatter(self, parts):
        return [self.replica(parts[m], m) for m in (1, 2, 3)]

    def far(self, value, mask):
        return self.replica(value, mask)

    def gather(self, value):
        return [self.replica(value, m) for m in (1, 2, 3)]

    @property
    def far_masks(self):
        return [1 << b for b in range(2, self.dp_size.bit_length() - 1)]

    def placed(self, members):
        return [lax.select_n(self.near, *[members[i ^ p] for p in range(4)]) for i in range(4)]


def cut(value):
    size = value.shape[0] // 4
    return [value[i * size : (i + 1) * size] for i in range(4)]


def first_call(
    flags, query_bias, value_bias, up_bias, query_weight, key_weight, value_weight, out_weight,
    tokens, up_weight, down_weight, whole, quarter,
):
    model = tokens.shape[1]
    size = whole[0] // 4
    width = size - BIAS_ROWS
    outs = [whole] + [(size, model)] * 2 + [quarter] * 4 + [(MOST, model)]
    far, vmem = pl.BlockSpec(memory_space=pl.ANY), pl.BlockSpec(memory_space=pltpu.VMEM)
    near = [(4 * width, model), whole, (2 * quarter[0], model), (2 * quarter[0], model), (MOST, model)]
    return pl.pallas_call(
        pack_kernel,
        in_specs=[pl.BlockSpec(memory_space=pltpu.SMEM)] + [vmem] * 3 + [far] * 7,
        out_specs=[far] * 8,
        out_shape=[jax.ShapeDtypeStruct(s, BF16) for s in outs],
        scratch_shapes=[pltpu.VMEM(s, BF16) for s in near] + [pltpu.SemaphoreType.DMA((16,))],
        compiler_params=pltpu.CompilerParams(vmem_limit_bytes=PACK_LIMIT),
        cost_estimate=pl.CostEstimate(flops=1, bytes_accessed=7_000_000, transcendentals=0),
    )(
        flags, query_bias[None], value_bias[None], up_bias[None],
        query_weight.T, key_weight.T, value_weight.T, out_weight, tokens, up_weight, down_weight,
    )


def body(
    dp_size,
    tokens,
    lengths,
    cotangent,
    query_weight,
    query_bias,
    key_weight,
    value_weight,
    value_bias,
    out_weight,
    out_bias,
    gain_one,
    shift_one,
    up_weight,
    up_bias,
    down_weight,
    down_bias,
    gain_two,
    shift_two,
):
    own, model = tokens.shape
    width = query_weight.shape[1]
    units = up_weight.shape[1]
    total_rows = own + MOST
    size = width + BIAS_ROWS
    place = lax.axis_index("tensor")
    replica = lax.axis_index("dp")
    side = (replica ^ (replica >> 1)) & 1
    flags = jnp.stack([side, place % 2, place // 2, place, replica & 3]).astype(jnp.int32)
    swaps = Swaps(dp_size, replica)
    swap_core, swap_chip, swap_replica = swaps.core, swaps.chip, swaps.replica

    whole, quarter = (4 * size, model), (units // 4, model)
    pack, pack_a, pack_b, up_a, up_b, down_a, down_b, halo = first_call(
        flags, query_bias, value_bias, up_bias, query_weight, key_weight, value_weight, out_weight,
        tokens, up_weight, down_weight, whole, quarter,
    )

    def attend(j, shard, inputs):
        first, made = len(inputs) == 2, len(shard) > 1
        outs = [((total_rows, model), BF16)] * first + [(whole, BF16)] * made
        outs += [
            ((total_rows, 3 * width), BF16), ((own, width), BF16), ((width, own), BF16),
            ((8, own), F32), ((8, model), F32),
        ]
        return call(
            functools.partial(attend_kernel, len(shard), first),
            outs,
            (flags, lengths, *shard, *inputs),
            scalars=2,
            scratch=[pltpu.VMEM((1, own), jnp.int32)],
            cost=5.5,
        )

    packs = [pack, swap_core(pack), None, None]
    saved = [None] * 4
    direct = [swap_chip(pack_a), swap_chip(pack_b)]
    halo = swap_core(halo)
    inputs_full, *saved[0] = attend(0, [pack], (tokens, halo))
    up_a, up_b, inputs_full = tie(up_a, up_b, inputs_full)
    up_direct = [swap_chip(up_a), swap_chip(up_b)]
    *direct, inputs_full, down_a, down_b = tie(*direct, inputs_full, down_a, down_b)
    around = [swap_replica(direct[0], 1), swap_replica(direct[1], 2)]
    down_direct = [swap_chip(down_a), swap_chip(down_b)]
    saved[1] = attend(1, packs[1:2], (inputs_full,))
    saved[1][1], inputs_full, *held = tie(saved[1][1], inputs_full, *around, *up_direct)
    around, up_direct = held[:2], held[2:]
    others = [swap_core(v) for v in direct + around]
    up_around = [swap_replica(up_direct[0], 1), swap_replica(up_direct[1], 2)]
    packs[2], *saved[2] = attend(2, direct + around, (inputs_full,))
    saved[2][1], inputs_full, up_own, down_own, *down_direct = tie(
        saved[2][1], inputs_full, up_weight, down_weight, *down_direct
    )
    down_around = [swap_replica(down_direct[0], 1), swap_replica(down_direct[1], 2)]
    ups = [up_weight, swap_core(up_own)]
    downs = [down_weight, swap_core(down_own)]
    packs[3], *saved[3] = attend(3, others, (inputs_full,))
    biases = [kept[4] for kept in saved]
    normal_one, inverse_one, low_hidden, turned_hidden = call(
        mid_kernel,
        [((own, model), F32), ((own, 1), F32), ((own, model), BF16), ((model, own), BF16)],
        (
            tokens, *[kept[1] for kept in saved], *packs,
            out_bias[None], gain_one[None], shift_one[None],
        ),
        scratch=[pltpu.VMEM((own, model), F32)],
        cost=3.0,
    )

    kept_shapes = [((units, own), BF16)] * 2 + [((own, units), BF16)] * 2
    active_0, active_1, slope_0, slope_1, partial = call(
        feed_kernel,
        kept_shapes + [((own, model), F32)],
        (low_hidden, *ups, *downs, biases[0], biases[1]),
        cost=7.0,
    )
    partial, *held = tie(partial, *up_direct, *up_around, *down_direct, *down_around)
    up_pieces, down_pieces = held[:4], held[4:]
    up_others = [swap_core(v) for v in up_pieces]
    down_others = [swap_core(v) for v in down_pieces]
    (
        active_2, active_3, slope_2, slope_3, layer_output, grad_two, low_grad_two, vector_two, *assembled,
    ) = call(
        feed_last_kernel,
        kept_shapes + [((own, model), BF16), ((own, model), F32), ((own, model), BF16), ((8, model), F32)]
        + [((model, units), BF16)] * 2 + [((units, model), BF16)] * 2,
        (
            flags, low_hidden, *up_pieces, *up_others, *down_pieces, *down_others, biases[2], biases[3], partial,
            normal_one, gain_one[None], shift_one[None], down_bias[None], gain_two[None], shift_two[None], cotangent,
        ),
        scalars=1,
        scratch=[pltpu.VMEM((own, model), F32)],
        cost=11.0,
    )
    ups += assembled[:2]
    downs += assembled[2:]
    actives = [active_0, active_1, active_2, active_3]
    slopes = [slope_0, slope_1, slope_2, slope_3]

    def feed_back(j, running, got=(), last=False):
        outs = [((model, units), BF16), ((units, model), BF16), ((8, units), F32), ((own, model), F32)]
        extra = ()
        if last:
            outs += [((own, model), BF16), ((8, model), F32)]
            extra = (normal_one, inverse_one, gain_one[None])
        return call(
            functools.partial(feed_back_kernel, bool(got), last),
            outs,
            (flags, low_grad_two, actives[j], slopes[j], turned_hidden, ups[j], downs[j], *got, running, *extra),
            scalars=1,
            scratch=[pltpu.VMEM((own, units), BF16)],
            cost=5.5,
        )

    up_3, down_3, up_sum_3, running = feed_back(3, grad_two)
    up_3, down_3, running = tie(up_3, down_3, running)
    up_3, down_3 = swap_core(up_3), swap_core(down_3)
    up_1, down_1, up_sum_1, running = feed_back(1, running)
    up_1, down_1, running = tie(up_1, down_1, running)
    up_1, down_1 = swap_core(up_1), swap_core(down_1)
    up_2, down_2, up_sum_2, running = feed_back(2, running, (up_3, down_3))
    up_2, down_2, running = tie(up_2, down_2, running)
    down_chip = swap_chip(down_2)
    up_0, down_0, up_sum_0, grad_one, low_grad_one, vector_one = feed_back(0, running, (up_1, down_1), True)
    up_0, up_2, low_grad_one = tie(up_0, up_2, low_grad_one)
    up_mine, up_theirs = cut(up_0), cut(up_2)
    up_got = swaps.scatter(up_mine) + swaps.scatter(up_theirs)

    def attend_back(j, low_grad_one, got=()):
        qkv, _, turned, log_total, _ = saved[j]
        return call(
            functools.partial(attend_back_kernel, bool(got)),
            [((4 * width, model), BF16), ((total_rows, 3 * width), BF16), ((8, 3 * width), F32)],
            (
                flags, lengths, inputs_full, low_grad_one, qkv, turned, log_total, packs[j], *got,
            ),
            scalars=2,
            scratch=[
                pltpu.VMEM((own, width), BF16), pltpu.VMEM((3 * width, total_rows), BF16),
                pltpu.VMEM((total_rows, width), F32), pltpu.VMEM((total_rows, width), F32),
                pltpu.VMEM((1, own), jnp.int32),
            ],
            cost=8.5,
        )

    plains, sums = [None] * 4, [None] * 4
    pack_3, plains[3], sums[3] = attend_back(3, low_grad_one)
    pack_3, low_grad_one = tie(pack_3, low_grad_one)
    pack_3 = swap_core(pack_3)
    pack_1, plains[1], sums[1] = attend_back(1, low_grad_one)
    pack_1, low_grad_one = tie(pack_1, low_grad_one)
    pack_1 = swap_core(pack_1)
    pack_2, plains[2], sums[2] = attend_back(2, low_grad_one, (pack_3,))
    pack_2, down_chip, low_grad_one = tie(pack_2, down_chip, low_grad_one)
    pack_chip = swap_chip(pack_2)
    down_parts = [add(m, t) for m, t in zip(cut(down_0), cut(down_chip))]
    *down_parts, low_grad_one = tie(*down_parts, low_grad_one)
    down_got = swaps.scatter(down_parts)
    pack_0, plains[0], sums[0] = attend_back(0, low_grad_one, (pack_1,))
    pack_0, *held = tie(pack_0, *down_got, *up_got)
    down_got, up_got = held[:3], held[3:]
    down_now = add(down_parts[0], *down_got)
    up_now, up_theirs = add(up_mine[0], *up_got[:3]), add(up_theirs[0], *up_got[3:])
    down_now, up_now, up_theirs = tie(down_now, up_now, up_theirs)
    up_chip = swap_chip(up_theirs)

    (vectors,) = call(
        vectors_kernel,
        [((16, model), F32)],
        (flags, vector_one, vector_two, up_sum_0, up_sum_1, up_sum_2, up_sum_3, *sums),
        scalars=1,
    )
    vectors = vectors + swap_core(vectors)
    far_masks = swaps.far_masks
    down_far = swaps.far(down_now, far_masks[0])
    pack_chip, vectors, pack_0 = tie(pack_chip, vectors, pack_0)
    pack_parts = [add(m, t) for m, t in zip(cut(pack_0), cut(pack_chip))]
    pack_got = swaps.scatter(pack_parts)
    other_vectors = swap_chip(vectors)
    tokens_total, to_halo = call(
        tokens_kernel,
        [((own, model), F32), ((MOST, model), BF16)],
        (flags, grad_one, *plains, *packs),
        scalars=1,
        cost=6.0,
    )
    up_now = add(up_now, up_chip)
    down_now = add(down_now, down_far)
    for mask in far_masks[1:]:
        down_now = add(down_now, swaps.far(down_now, mask))
    up_now, down_now = tie(up_now, down_now)
    up_far = swaps.far(up_now, far_masks[0])
    down_all = [down_now] + swaps.gather(down_now)
    *pack_got, other_vectors, tokens_total = tie(*pack_got, other_vectors, tokens_total)
    pack_now = add(pack_parts[0], *pack_got)
    vectors = vectors + other_vectors
    pack_now, vectors = tie(pack_now, vectors)
    pack_far = swaps.far(pack_now, far_masks[0])
    others = swaps.gather(vectors)
    (tokens_grad,) = call(
        last_kernel, [((own, model), F32)], (flags, tokens_total, swap_core(to_halo)), scalars=1, cost=2.0
    )
    up_now = add(up_now, up_far)
    for mask in far_masks[1:]:
        up_now = add(up_now, swaps.far(up_now, mask))
    *down_all, up_now = tie(*down_all, up_now)
    up_all = [up_now] + swaps.gather(up_now)
    pack_far, others[0], others[1], others[2], tokens_grad = tie(pack_far, *others, tokens_grad)
    pack_now = add(pack_now, pack_far)
    vectors = (vectors + others[0]) + (others[1] + others[2])
    for mask in far_masks[1:]:
        pack_now = add(pack_now, swaps.far(pack_now, mask))
    pack_now, vectors, *up_all = tie(pack_now, vectors, *up_all)
    pack_all = [pack_now] + swaps.gather(pack_now)
    for mask in far_masks:
        vectors = vectors + swap_replica(vectors, mask)
    down_weight_grad = jnp.concatenate(swaps.placed(down_all), axis=0).astype(F32)
    up_weight_grad = jnp.concatenate(swaps.placed(up_all), axis=0).astype(F32)
    query_grad, key_grad, value_grad, out_grad = [v.astype(F32) for v in swaps.placed(pack_all)]
    up_bias_row = lax.dynamic_index_in_dim(vectors, 6 + place, 0, keepdims=False)
    bias_row = lax.dynamic_index_in_dim(vectors, 10 + place, 0, keepdims=False)
    return (
        layer_output,
        tokens_grad,
        query_grad.T,
        bias_row[:width],
        key_grad.T,
        value_grad.T,
        bias_row[width : 2 * width],
        out_grad,
        vectors[0],
        vectors[1],
        vectors[2],
        up_weight_grad,
        up_bias_row,
        down_weight_grad,
        vectors[5],
        vectors[3],
        vectors[4],
    )


def solution(mesh):
    placed = (
        P(("dp", "tensor"), None),
        P("dp", None),
        P(("dp", "tensor"), None),
        P(None, "tensor"),
        P("tensor"),
        P(None, "tensor"),
        P(None, "tensor"),
        P("tensor"),
        P("tensor", None),
        P(),
        P(),
        P(),
        P(None, "tensor"),
        P("tensor"),
        P("tensor", None),
        P(),
        P(),
        P(),
    )
    return jax.shard_map(
        functools.partial(body, mesh.shape["dp"]),
        mesh=mesh,
        in_specs=placed,
        out_specs=(
            P(("dp", "tensor"), None),
            P(("dp", "tensor"), None),
            P(None, "tensor"),
            P("tensor"),
            P(None, "tensor"),
            P(None, "tensor"),
            P("tensor"),
            P("tensor", None),
            P(),
            P(),
            P(),
            P(None, "tensor"),
            P("tensor"),
            P("tensor", None),
            P(),
            P(),
            P(),
        ),
        check_vma=False,
    )
```

```python
import functools

import jax
import jax.numpy as jnp
from jax import lax
from jax.experimental import pallas as pl
from jax.experimental.pallas import tpu as pltpu
from jax.sharding import PartitionSpec as P

HEAD_DIM = 64
MOST = 256
EPSILON = 1e-05
MASKED = -1e30
BLOCK = 256
STRIP = 64
BIAS_ROWS = 16
VMEM_LIMIT = 16 * 1024 * 1024
PACK_LIMIT = 60 * 1024 * 1024
TAIL_SCALE = 0.425
TAIL = (
    0.23966740682492862,
    0.24201181237516,
    0.19964184258583956,
    0.2585875675603689,
    -0.10985333090134082,
    0.4147788772153898,
    -0.3173079260911745,
    0.07247363954140279,
)

BF16 = jnp.bfloat16
F32 = jnp.float32


def product(left_side, right_side):
    return jnp.dot(left_side, right_side, preferred_element_type=F32)


def rows_product(left_side, right_side):
    return lax.dot_general(
        left_side, right_side, (((0,), (0,)), ((), ())), preferred_element_type=F32
    )


def cols_product(left_side, right_side):
    return lax.dot_general(
        left_side, right_side, (((1,), (1,)), ((), ())), preferred_element_type=F32
    )


def normal_parts(z):
    size = jnp.abs(z)
    t = 1.0 / (1.0 + (TAIL_SCALE * 0.7071067811865476) * size)
    series = TAIL[-1]
    for factor in TAIL[-2::-1]:
        series = series * t + factor
    bell = jnp.exp(-0.5 * z * z)
    tail = (0.5 * bell) * (series * t)
    return jnp.where(z >= 0.0, 1.0 - tail, tail), bell * 0.3989422804014327


def call(kernel, outs, args, scalars=0, scratch=(), cost=1.0, far=()):
    specs = [pl.BlockSpec(memory_space=pltpu.SMEM)] * scalars
    specs += [pl.BlockSpec(memory_space=pltpu.VMEM)] * (len(args) + len(outs) - scalars)
    for i in far:
        specs[i] = pl.BlockSpec(memory_space=pl.ANY)
    outputs = pl.pallas_call(
        kernel,
        in_specs=specs[: len(args)],
        out_specs=specs[len(args) :],
        out_shape=[jax.ShapeDtypeStruct(shape, dtype) for shape, dtype in outs],
        scratch_shapes=list(scratch),
        compiler_params=pltpu.CompilerParams(vmem_limit_bytes=VMEM_LIMIT),
        cost_estimate=pl.CostEstimate(
            flops=0, bytes_accessed=0, transcendentals=0
        ),
    )(*args)
    return list(outputs)


def piece(index, size):
    return pl.ds(pl.multiple_of(index * size, 16), size)


def assemble(side, refs, out_ref):
    size, count = refs[0].shape[0], len(refs) // 2
    for i, ref in enumerate(refs):
        first = side if i < count else 1 - side
        out_ref[piece(first * count + i % count, size), :] = ref[...]


def join(flags_ref, own_ref, other_ref, out_ref):
    size = own_ref.shape[0]
    out_ref[piece(flags_ref[1], size), :] = own_ref[...]
    out_ref[piece(1 - flags_ref[1], size), :] = other_ref[...]


def pack_kernel(
    flags_ref, query_b_ref, value_b_ref, up_b_ref, query_ref, key_ref, value_ref, out_w_ref, up_ref, down_ref,
    pack_ref, pack_a, pack_b, up_out, down_out, weights, pack_near, up_near, down_near, sems,
):
    width, model = query_ref.shape
    size = width + BIAS_ROWS
    half = up_out.shape[0]
    copies = []

    def move(source, target):
        copies.append(pltpu.make_async_copy(source, target, sems.at[len(copies)]))
        copies[-1].start()

    for i, ref in enumerate((query_ref, key_ref, value_ref, out_w_ref)):
        move(ref, weights.at[i * width : (i + 1) * width])
    move(up_ref.at[piece(flags_ref[5], half)], up_near)
    move(down_ref.at[piece(flags_ref[6], half)], down_near)
    blank = jnp.zeros((1, model - 2 * width), F32)
    rows = []
    for row in (up_b_ref[...], jnp.concatenate([query_b_ref[...], value_b_ref[...], blank], axis=1)):
        for _ in range(3):
            rows.append(row.astype(BF16).astype(F32))
            row = row - rows[-1]
    rows.append(jnp.zeros((BIAS_ROWS - 6, model), F32))
    biases = jnp.concatenate(rows, axis=0).astype(BF16)
    for i in range(4):
        copies[i].wait()
        pack_near[i * size + width : (i + 1) * size, :] = biases
        pack_near[i * size : i * size + width, :] = weights[i * width : (i + 1) * width, :]
    for index, out in enumerate((pack_a, pack_b)):
        move(pack_near.at[piece(flags_ref[0] * 2 + index, size)], out)
    move(pack_near, pack_ref)
    copies[4].wait()
    move(up_near, up_out)
    copies[5].wait()
    move(down_near, down_out)
    for copy in copies[6:]:
        copy.wait()


def masks(flags_ref, lengths_ref, rows):
    found = []
    for shape, axis in (((rows, 1), 0), ((1, rows), 1)):
        spot = lax.broadcasted_iota(jnp.int32, shape, axis)
        ends = 0
        segment = jnp.zeros_like(spot)
        for d in range(lengths_ref.shape[1]):
            ends = ends + lengths_ref[flags_ref[2], d]
            segment = segment + (spot >= ends).astype(jnp.int32)
        found.append(segment)
    return found


def window(i, rows):
    last = max(rows // BLOCK - 3, 0)
    count = min(3, rows // BLOCK)
    return pl.ds(pl.multiple_of(jnp.clip(i - 1, 0, last) * BLOCK, BLOCK), count * BLOCK)


def attend_units(flags_ref, lengths_ref, x_ref, w_ref, qkv_ref, context_ref, turned_ref, log_ref, bias_ref, seg_k_ref, seg_q_ref):
    rows, model = x_ref.shape
    width = context_ref.shape[1]
    size = width + BIAS_ROWS
    parts = w_ref[width : width + 6, :].astype(F32)
    bias_ref[0:1, :] = parts[0:1] + parts[1:2] + parts[2:3]
    mixed = parts[3:4] + parts[4:5] + parts[5:6]
    for i, bias in enumerate((mixed[:, :width], None, mixed[:, width : 2 * width])):
        weights = w_ref[i * size : i * size + width, :]
        for r in range(0, rows, BLOCK):
            total = cols_product(x_ref[r : r + BLOCK, :], weights)
            if bias is not None:
                total = total + bias
            qkv_ref[r : r + BLOCK, i * width : (i + 1) * width] = total.astype(BF16)
    seg_k_ref[...], seg_q_ref[...] = masks(flags_ref, lengths_ref, rows)

    def one_block(i, carry):
        here = pl.ds(pl.multiple_of(i * BLOCK, BLOCK), BLOCK)
        seen = window(i, rows)
        bias = jnp.where(seg_k_ref[seen, :] == seg_q_ref[:, here], 0.0, MASKED).astype(F32)
        contexts = []
        for h in range(width // HEAD_DIM):
            low, high = h * HEAD_DIM, (h + 1) * HEAD_DIM
            queries = qkv_ref[here, low:high] * BF16(HEAD_DIM**-0.5)
            key_rows = qkv_ref[seen, width + low : width + high]
            value_rows = qkv_ref[seen, 2 * width + low : 2 * width + high]
            scores = cols_product(key_rows, queries) + bias
            top = jnp.max(scores, axis=0, keepdims=True)
            weights = jnp.exp(scores - top)
            total = jnp.sum(weights, axis=0, keepdims=True)
            low_probs = (weights * (1.0 / total)).astype(BF16)
            context = rows_product(value_rows, low_probs)
            turned_ref[low:high, here] = context.astype(BF16)
            contexts.append(context.T)
            log_ref[h : h + 1, here] = top + jnp.log(total)
        context_ref[here, :] = jnp.concatenate(contexts, axis=1).astype(BF16)
        return carry

    lax.fori_loop(0, rows // BLOCK, one_block, 0)


def attend_kernel(
    flags_ref, lengths_ref, w_ref, tokens_ref, other_ref,
    x_ref, qkv_ref, context_ref, turned_ref, log_ref, bias_ref, seg_k_ref, seg_q_ref,
):
    join(flags_ref, tokens_ref, other_ref, x_ref)
    attend_units(
        flags_ref, lengths_ref, x_ref, w_ref, qkv_ref, context_ref, turned_ref, log_ref, bias_ref, seg_k_ref, seg_q_ref
    )


def share(flags_ref, total_ref, keep_ref, *send_refs):
    size = keep_ref.shape[0]
    keep_ref[...] = total_ref[piece(flags_ref[1], size), :]
    part = size // len(send_refs)
    for i, send_ref in enumerate(send_refs):
        send_ref[...] = total_ref[piece((1 - flags_ref[1]) * len(send_refs) + i, part), :].astype(BF16)


def attend_last_kernel(
    flags_ref, lengths_ref, w_0, w_1, w_2, w_3, x_ref, before_ref, w_before,
    w_ref, qkv_ref, turned_ref, log_ref, bias_ref, keep_ref, send_ref, seg_k_ref, seg_q_ref, context_ref, mix_ref,
):
    assemble(flags_ref[0], (w_0, w_1, w_2, w_3), w_ref)
    attend_units(
        flags_ref, lengths_ref, x_ref, w_ref, qkv_ref, context_ref, turned_ref, log_ref, bias_ref, seg_k_ref, seg_q_ref
    )
    width = context_ref.shape[1]
    size = width + BIAS_ROWS
    for r in range(0, x_ref.shape[0], BLOCK):
        here = slice(r, r + BLOCK)
        mix_ref[here, :] = product(before_ref[here, :], w_before[3 * size : 3 * size + width, :]) + product(
            context_ref[here, :], w_ref[3 * size : 3 * size + width, :]
        )
    share(flags_ref, mix_ref, keep_ref, send_ref)


def strips(rows, step):
    def one(i, carry):
        step(pl.ds(pl.multiple_of(i * STRIP, STRIP), STRIP))
        return carry

    lax.fori_loop(0, rows // STRIP, one, 0, unroll=2)


def norm_one_kernel(
    tokens_ref, keep_ref, got_ref, out_b_ref, gain_ref, shift_ref, normal_ref, inverse_ref, hidden_ref,
):
    def step(here):
        values = tokens_ref[here, :].astype(F32) + keep_ref[here, :] + got_ref[here, :].astype(F32) + out_b_ref[...]
        centered = values - jnp.mean(values, axis=1, keepdims=True)
        inverse = lax.rsqrt(jnp.mean(centered * centered, axis=1, keepdims=True) + EPSILON)
        normal = centered * inverse
        normal_ref[here, :] = normal
        inverse_ref[here, :] = inverse
        hidden_ref[here, :] = (normal * gain_ref[...] + shift_ref[...]).astype(BF16)

    strips(tokens_ref.shape[0], step)


def feed_units(hidden_ref, up_ref, down_ref, bias_ref, active_ref, slope_ref, sum_ref, before_ref):
    units = up_ref.shape[1]
    for u in range(0, units, BLOCK):
        for r in range(0, hidden_ref.shape[0], 2 * BLOCK):
            here = slice(r, r + 2 * BLOCK)
            pre_up = bias_ref[0:1, u : u + BLOCK] + product(hidden_ref[here, :], up_ref[:, u : u + BLOCK])
            cumulative, density = normal_parts(pre_up)
            active = (pre_up * cumulative).astype(BF16)
            active_ref[u : u + BLOCK, here] = active.T
            slope_ref[here, u : u + BLOCK] = (cumulative + pre_up * density).astype(BF16)
            now = product(active, down_ref[u : u + BLOCK, :])
            if u:
                sum_ref[here, :] += now
            elif before_ref is not None:
                sum_ref[here, :] = before_ref[here, :] + now
            else:
                sum_ref[here, :] = now


def feed_kernel(
    flags_ref, own_ref, other_ref, up_ref, down_ref, bias_ref, hidden_ref, turned_ref, active_ref, slope_ref, sum_ref
):
    join(flags_ref, own_ref, other_ref, hidden_ref)
    turned_ref[...] = hidden_ref[...].T
    feed_units(hidden_ref, up_ref, down_ref, bias_ref, active_ref, slope_ref, sum_ref, None)


def feed_last_kernel(
    flags_ref, hidden_ref, up_a, up_b, down_a, down_b, bias_ref, before_ref,
    up_ref, down_ref, active_ref, slope_ref, keep_ref, send_ref, sum_ref,
):
    assemble(flags_ref[5], (up_a, up_b), up_ref)
    assemble(flags_ref[6], (down_a, down_b), down_ref)
    feed_units(hidden_ref, up_ref, down_ref, bias_ref, active_ref, slope_ref, sum_ref, before_ref)
    share(flags_ref, sum_ref, keep_ref, send_ref)


def norm_two_kernel(
    keep_ref, got_ref, normal_ref, gain_one_ref, shift_one_ref, down_b_ref, gain_ref, shift_ref, cotangent_ref,
    out_ref, grad_ref, low_ref, vector_ref,
):
    vector_ref[...] = jnp.zeros_like(vector_ref)

    def step(here):
        values = keep_ref[here, :] + got_ref[here, :].astype(F32) + down_b_ref[...]
        values = values + (normal_ref[here, :] * gain_one_ref[...] + shift_one_ref[...])
        centered = values - jnp.mean(values, axis=1, keepdims=True)
        inverse = lax.rsqrt(jnp.mean(centered * centered, axis=1, keepdims=True) + EPSILON)
        normal = centered * inverse
        out_ref[here, :] = (normal * gain_ref[...] + shift_ref[...]).astype(BF16)
        upstream = cotangent_ref[here, :].astype(F32)
        scaled = upstream * gain_ref[...]
        first = jnp.mean(scaled, axis=1, keepdims=True)
        second = jnp.mean(scaled * normal, axis=1, keepdims=True)
        grad = inverse * (scaled - first - normal * second)
        grad_ref[here, :] = grad
        low_ref[here, :] = grad.astype(BF16)
        vector_ref[0:1, :] += jnp.sum(upstream * normal, axis=0, keepdims=True)
        vector_ref[1:2, :] += jnp.sum(upstream, axis=0, keepdims=True)
        vector_ref[2:3, :] += jnp.sum(grad, axis=0, keepdims=True)

    strips(keep_ref.shape[0], step)


def quarters(flags_ref, size):
    return [pl.ds(pl.multiple_of(jnp.bitwise_xor(flags_ref[4], i) * size, 16), size) for i in range(4)]


def feed_back_units(
    flags_ref, grad_ref, active_ref, slope_ref, hidden_ref, up_ref, down_ref, before_ref,
    down_grad_ref, bias_grad_ref, sum_ref, turned_ref, grad_pre_ref,
):
    rows, model = grad_ref.shape
    units = slope_ref.shape[1]
    for i, where in enumerate(quarters(flags_ref, units // 4)):
        value = product(active_ref[i * (units // 4) : (i + 1) * (units // 4), :], grad_ref[...])
        down_grad_ref[where, :] = value.astype(BF16)
    for u in range(0, units, BLOCK):
        here = slice(u, u + BLOCK)
        total = 0.0
        for r in range(0, rows, 2 * BLOCK):
            grad_active = cols_product(grad_ref[r : r + 2 * BLOCK, :], down_ref[here, :])
            grad_pre = (slope_ref[r : r + 2 * BLOCK, here].astype(F32) * grad_active).astype(BF16)
            grad_pre_ref[r : r + 2 * BLOCK, here] = grad_pre
            total = total + jnp.sum(grad_pre.astype(F32), axis=0, keepdims=True)
        bias_grad_ref[0:1, here] = total
    for i, where in enumerate(quarters(flags_ref, model // 4)):
        value = product(hidden_ref[i * (model // 4) : (i + 1) * (model // 4), :], grad_pre_ref[...])
        turned_ref[where, :] = value.astype(BF16)
    for r in range(0, rows, BLOCK):
        value = cols_product(grad_pre_ref[r : r + BLOCK, :], up_ref[...])
        if before_ref is not None:
            value = value + before_ref[r : r + BLOCK, :]
        sum_ref[r : r + BLOCK, :] = value


def feed_back_theirs_kernel(
    flags_ref, own_ref, other_ref, active_ref, slope_ref, hidden_ref, up_ref, down_ref,
    grad_ref, down_grad_ref, near_0, near_1, near_2, near_3, bias_grad_ref, sum_ref, turned_ref, grad_pre_ref,
):
    join(flags_ref, own_ref, other_ref, grad_ref)
    feed_back_units(
        flags_ref, grad_ref, active_ref, slope_ref, hidden_ref, up_ref, down_ref, None,
        down_grad_ref, bias_grad_ref, sum_ref, turned_ref, grad_pre_ref,
    )
    quarter = near_0.shape[0]
    for i, near in enumerate((near_0, near_1, near_2, near_3)):
        near[...] = turned_ref[i * quarter : (i + 1) * quarter, :]


def feed_back_mine_kernel(
    flags_ref, grad_ref, active_ref, slope_ref, hidden_ref, up_ref, down_ref, before_ref,
    theirs_0, theirs_1, theirs_2, theirs_3, grad_two_ref,
    down_grad_ref, near_0, near_1, near_2, near_3, bias_grad_ref, keep_ref, send_a, send_b, sum_ref, turned_ref, grad_pre_ref,
):
    feed_back_units(
        flags_ref, grad_ref, active_ref, slope_ref, hidden_ref, up_ref, down_ref, before_ref,
        down_grad_ref, bias_grad_ref, sum_ref, turned_ref, grad_pre_ref,
    )
    quarter = theirs_0.shape[0]
    theirs = (theirs_0, theirs_1, theirs_2, theirs_3)
    for i, near in enumerate((near_0, near_1, near_2, near_3)):
        near[:quarter, :] = turned_ref[i * quarter : (i + 1) * quarter, :]
        near[quarter:, :] = theirs[i][...]
    share(flags_ref, sum_ref, keep_ref, send_a, send_b)
    keep_ref[...] += grad_two_ref[...]


def norm_one_back_kernel(keep_ref, got_a, got_b, normal_ref, inverse_ref, gain_ref, grad_ref, low_ref, vector_ref, got_ref):
    vector_ref[...] = jnp.zeros_like(vector_ref)
    half = got_a.shape[0]
    got_ref[:half, :] = got_a[...]
    got_ref[half:, :] = got_b[...]

    def step(here):
        upstream, normal = keep_ref[here, :] + got_ref[here, :].astype(F32), normal_ref[here, :]
        scaled = upstream * gain_ref[...]
        first = jnp.mean(scaled, axis=1, keepdims=True)
        second = jnp.mean(scaled * normal, axis=1, keepdims=True)
        grad = inverse_ref[here, :] * (scaled - first - normal * second)
        grad_ref[here, :] = grad
        low_ref[here, :] = grad.astype(BF16)
        vector_ref[0:1, :] += jnp.sum(grad, axis=0, keepdims=True)
        vector_ref[1:2, :] += jnp.sum(upstream * normal, axis=0, keepdims=True)
        vector_ref[2:3, :] += jnp.sum(upstream, axis=0, keepdims=True)

    strips(keep_ref.shape[0], step)


def attend_back_kernel(
    flags_ref, lengths_ref, own_ref, other_ref, x_ref, qkv_ref, context_ref, log_ref, w_ref, out_ref, plain_ref,
    grad_ref, grad_context_ref, turned_ref, keys_ref, values_ref, seg_k_ref, seg_q_ref,
):
    rows, model = x_ref.shape
    width = qkv_ref.shape[1] // 3
    size = width + BIAS_ROWS
    join(flags_ref, own_ref, other_ref, grad_ref)
    grad_context_ref[...] = cols_product(grad_ref[...], w_ref[3 * size : 3 * size + width, :]).astype(BF16)
    keys_ref[...] = jnp.zeros_like(keys_ref)
    values_ref[...] = jnp.zeros_like(values_ref)
    seg_k_ref[...], seg_q_ref[...] = masks(flags_ref, lengths_ref, rows)

    def one_block(i, carry):
        here = pl.ds(pl.multiple_of(i * BLOCK, BLOCK), BLOCK)
        seen = window(i, rows)
        bias = jnp.where(seg_k_ref[seen, :] == seg_q_ref[:, here], 0.0, MASKED).astype(F32)
        for h in range(width // HEAD_DIM):
            low, high = h * HEAD_DIM, (h + 1) * HEAD_DIM
            queries = qkv_ref[here, low:high] * BF16(HEAD_DIM**-0.5)
            key_rows = qkv_ref[seen, width + low : width + high]
            value_rows = qkv_ref[seen, 2 * width + low : 2 * width + high]
            grads = grad_context_ref[here, low:high]
            scores = cols_product(key_rows, queries) + bias
            probs = jnp.exp(scores - log_ref[h : h + 1, here])
            values_ref[seen, low:high] += product(probs.astype(BF16), grads)
            grad_probs = cols_product(value_rows, grads)
            inner = jnp.sum(probs * grad_probs, axis=0, keepdims=True)
            grad_scores = (probs * (grad_probs - inner)).astype(BF16)
            keys_ref[seen, low:high] += product(grad_scores, queries)
            grad_queries = rows_product(key_rows, grad_scores) * (HEAD_DIM**-0.5)
            turned_ref[low:high, here] = grad_queries.astype(BF16)
        return carry

    lax.fori_loop(0, rows // BLOCK, one_block, 0)
    plain_ref[:, :width] = turned_ref[:width, :].T
    plain_ref[:, width : 2 * width] = keys_ref[...].astype(BF16)
    plain_ref[:, 2 * width :] = values_ref[...].astype(BF16)
    turned_ref[width:, :] = plain_ref[:, width:].T
    bias = jnp.sum(plain_ref[...].astype(F32), axis=0, keepdims=True)
    for i, here in enumerate(quarters(flags_ref, size)):
        if i < 3:
            grad = product(turned_ref[i * width : (i + 1) * width, :], x_ref[...])
        else:
            grad = product(context_ref[...], grad_ref[...])
        rest = jnp.zeros((BIAS_ROWS, model), F32)
        if i in (0, 2):
            row = jnp.concatenate(
                [bias[:, i * width : (i + 1) * width], jnp.zeros((1, model - width), F32)], axis=1
            )
            rest = jnp.concatenate([row, rest[1:]], axis=0)
        out_ref[here, :] = jnp.concatenate([grad, rest], axis=0).astype(BF16)


def tokens_kernel(flags_ref, grad_ref, plain_0, plain_2, w_0, w_2, keep_ref, send_ref, sum_ref):
    rows, columns = plain_0.shape
    width = columns // 3
    size = width + BIAS_ROWS
    for r in range(0, rows, BLOCK):
        total = 0.0
        for plain, w_ref in ((plain_0, w_0), (plain_2, w_2)):
            for i in range(3):
                total = total + product(
                    plain[r : r + BLOCK, i * width : (i + 1) * width], w_ref[i * size : i * size + width, :]
                )
        sum_ref[r : r + BLOCK, :] = total
    share(flags_ref, sum_ref, keep_ref, send_ref)
    keep_ref[...] += grad_ref[...]


def last_kernel(keep_ref, got_ref, out_ref):
    out_ref[...] = keep_ref[...] + got_ref[...].astype(F32)


def vectors_kernel(flags_ref, one_ref, two_ref, up_0, up_2, out_ref):
    model = one_ref.shape[1]
    out_ref[0:3, :] = one_ref[0:3, :]
    out_ref[3:6, :] = two_ref[0:3, :]
    out_ref[6:16, :] = jnp.zeros((10, model), F32)
    for j, ref in ((0, up_0), (2, up_2)):
        out_ref[pl.ds(6 + jnp.bitwise_xor(flags_ref[3], j), 1), :] = ref[0:1, :]


def tie(*arrays):
    return lax.optimization_barrier(arrays)


def add(*members):
    members = [m.astype(F32) for m in members]
    while len(members) > 1:
        members = [a + b for a, b in zip(members[::2], members[1::2])]
    return members[0].astype(BF16)


class Swaps:
    def __init__(self, dp_size, replica):
        self.dp_size, self.near = dp_size, replica & 3

    def core(self, values_in):
        return lax.ppermute(values_in, "tensor", [(i, i ^ 1) for i in range(4)])

    def chip(self, values_in):
        return lax.ppermute(values_in, "tensor", [(i, i ^ 2) for i in range(4)])

    def replica(self, values_in, mask):
        return lax.ppermute(values_in, "dp", [(i, i ^ mask) for i in range(self.dp_size)])

    def scatter(self, parts):
        return [self.replica(parts[m], m) for m in (1, 2, 3)]

    def far(self, value, mask):
        return self.replica(value, mask)

    def gather(self, value):
        return [self.replica(value, m) for m in (1, 2, 3)]

    @property
    def far_masks(self):
        return [1 << b for b in range(2, self.dp_size.bit_length() - 1)]

    def placed(self, members):
        return [lax.select_n(self.near, *[members[i ^ p] for p in range(4)]) for i in range(4)]


def cut(value):
    size = value.shape[0] // 4
    return [value[i * size : (i + 1) * size] for i in range(4)]


def first_call(
    flags, query_bias, value_bias, up_bias, query_weight, key_weight, value_weight, out_weight, up_weight, down_weight,
):
    model, width = query_weight.shape
    size = width + BIAS_ROWS
    half = (up_weight.shape[0] // 2, up_weight.shape[1])
    outs = [(4 * size, model), (size, model), (size, model), half, (down_weight.shape[0] // 2, model)]
    far, vmem = pl.BlockSpec(memory_space=pl.ANY), pl.BlockSpec(memory_space=pltpu.VMEM)
    near = [(4 * width, model), (4 * size, model), half, outs[4]]
    return pl.pallas_call(
        pack_kernel,
        in_specs=[pl.BlockSpec(memory_space=pltpu.SMEM)] + [vmem] * 3 + [far] * 6,
        out_specs=[far] * 5,
        out_shape=[jax.ShapeDtypeStruct(s, BF16) for s in outs],
        scratch_shapes=[pltpu.VMEM(s, BF16) for s in near] + [pltpu.SemaphoreType.DMA((16,))],
        compiler_params=pltpu.CompilerParams(vmem_limit_bytes=PACK_LIMIT),
        cost_estimate=pl.CostEstimate(flops=0, bytes_accessed=0, transcendentals=0),
    )(
        flags, query_bias[None], value_bias[None], up_bias[None],
        query_weight.T, key_weight.T, value_weight.T, out_weight, up_weight, down_weight,
    )


def body(
    dp_size,
    tokens,
    lengths,
    cotangent,
    query_weight,
    query_bias,
    key_weight,
    value_weight,
    value_bias,
    out_weight,
    out_bias,
    gain_one,
    shift_one,
    up_weight,
    up_bias,
    down_weight,
    down_bias,
    gain_two,
    shift_two,
):
    own, model = tokens.shape
    width = query_weight.shape[1]
    units = up_weight.shape[1]
    rows = 2 * own
    place = lax.axis_index("tensor")
    replica = lax.axis_index("dp")
    flags = [(replica ^ (replica >> 1)) & 1, place % 2, place // 2, place, replica & 3, (replica >> 1) & 1, replica & 1]
    flags = jnp.stack(flags).astype(jnp.int32)
    swaps = Swaps(dp_size, replica)
    swap_core, swap_chip, swap_replica = swaps.core, swaps.chip, swaps.replica
    far_masks = swaps.far_masks

    other_tokens = swap_core(tokens)
    pack, pack_a, pack_b, up_half, down_half = first_call(
        flags, query_bias, value_bias, up_bias, query_weight, key_weight, value_weight, out_weight, up_weight, down_weight
    )
    whole, half_row = (4 * (width + BIAS_ROWS), model), (own, model)
    seg_scratch = [pltpu.VMEM((rows, 1), jnp.int32), pltpu.VMEM((1, rows), jnp.int32)]
    kept_shapes = [((width, rows), BF16), ((8, rows), F32), ((8, model), F32)]
    direct = [swap_chip(pack_a), swap_chip(pack_b)]
    up_direct, down_direct = swap_chip(up_half), swap_chip(down_half)

    inputs, qkv_0, context_0, turned_0, log_0, bias_0 = call(
        attend_kernel,
        [((rows, model), BF16), ((rows, 3 * width), BF16), ((rows, width), BF16)] + kept_shapes,
        (flags, lengths, pack, tokens, other_tokens),
        scalars=2,
        scratch=seg_scratch,
    )
    *direct, inputs = tie(*direct, inputs)
    around = [swap_replica(direct[0], 1), swap_replica(direct[1], 2)]
    *around, up_direct, inputs = tie(*around, up_direct, inputs)
    up_around = swap_replica(up_direct, 2)
    pack_2, qkv_2, turned_2, log_2, bias_2, keep, send = call(
        attend_last_kernel,
        [(whole, BF16), ((rows, 3 * width), BF16)] + kept_shapes + [(half_row, F32), (half_row, BF16)],
        (flags, lengths, *direct, *around, inputs, context_0, pack),
        scalars=2,
        scratch=seg_scratch + [pltpu.VMEM((rows, width), BF16), pltpu.VMEM((rows, model), F32)],
    )
    send, down_direct = tie(send, down_direct)
    got = swap_core(send)
    down_around = swap_replica(down_direct, 1)
    normal_one, inverse_one, hidden = call(
        norm_one_kernel,
        [(half_row, F32), ((own, 1), F32), (half_row, BF16)],
        (tokens, keep, got, out_bias[None], gain_one[None], shift_one[None]),
    )

    act_shapes = [((units, rows), BF16), ((rows, units), BF16)]
    hidden_full, hidden_turned, active_0, slope_0, before = call(
        feed_kernel,
        [((rows, model), BF16), ((model, rows), BF16)] + act_shapes + [((rows, model), F32)],
        (flags, hidden, swap_core(hidden), up_weight, down_weight, bias_0),
        scalars=1,
    )
    before, up_around, down_around = tie(before, up_around, down_around)
    up_2, down_2, active_2, slope_2, keep, send = call(
        feed_last_kernel,
        [((model, units), BF16), ((units, model), BF16)] + act_shapes + [(half_row, F32), (half_row, BF16)],
        (flags, hidden_full, up_direct, up_around, down_direct, down_around, bias_2, before),
        scalars=1,
        scratch=[pltpu.VMEM((rows, model), F32)],
    )
    layer_output, grad_two, low_grad_two, vector_two = call(
        norm_two_kernel,
        [(half_row, BF16), (half_row, F32), (half_row, BF16), ((8, model), F32)],
        (
            keep, swap_core(send), normal_one, gain_one[None], shift_one[None], down_bias[None],
            gain_two[None], shift_two[None], cotangent,
        ),
    )

    back_scratch = [pltpu.VMEM((model, units), BF16), pltpu.VMEM((rows, units), BF16)]
    grad_full, down_theirs, *up_theirs, up_sum_2, running = call(
        feed_back_theirs_kernel,
        [((rows, model), BF16), ((units, model), BF16)] + [((model // 4, units), BF16)] * 4
        + [((8, units), F32), ((rows, model), F32)],
        (flags, low_grad_two, swap_core(low_grad_two), active_2, slope_2, hidden_turned, up_2, down_2),
        scalars=1,
        scratch=back_scratch,
    )
    down_theirs, running = tie(down_theirs, running)
    down_chip = swap_chip(down_theirs)
    down_mine, *up_near, up_sum_0, keep, send_a, send_b = call(
        feed_back_mine_kernel,
        [((units, model), BF16)] + [((model // 2, units), BF16)] * 4
        + [((8, units), F32), (half_row, F32)] + [((own // 2, model), BF16)] * 2,
        (
            flags, grad_full, active_0, slope_0, hidden_turned, up_weight, down_weight, running, *up_theirs, grad_two,
        ),
        scalars=1,
        scratch=[pltpu.VMEM((rows, model), F32)] + back_scratch,
    )
    send_a, send_b, *up_near = tie(send_a, send_b, *up_near)
    got = [swap_core(send_a), swap_core(send_b)]
    up_got = swaps.scatter(up_near)
    grad_one, low_grad_one, vector_one = call(
        norm_one_back_kernel,
        [(half_row, F32), (half_row, BF16), ((8, model), F32)],
        (keep, *got, normal_one, inverse_one, gain_one[None]),
        scratch=[pltpu.VMEM(half_row, BF16)],
    )
    (vectors,) = call(
        vectors_kernel, [((16, model), F32)], (flags, vector_one, vector_two, up_sum_0, up_sum_2), scalars=1
    )
    other_vectors = swap_core(vectors)

    low_other = swap_core(low_grad_one)

    def attend_back(low_grad_one, qkv, turned, log_total, shard):
        return call(
            attend_back_kernel,
            [(whole, BF16), ((rows, 3 * width), BF16)],
            (flags, lengths, low_grad_one, low_other, inputs, qkv, turned, log_total, shard),
            scalars=2,
            scratch=[
                pltpu.VMEM((rows, model), BF16), pltpu.VMEM((rows, width), BF16),
                pltpu.VMEM((3 * width, rows), BF16), pltpu.VMEM((rows, width), F32), pltpu.VMEM((rows, width), F32),
            ] + seg_scratch,
        )

    pack_theirs, plain_2 = attend_back(low_grad_one, qkv_2, turned_2, log_2, pack_2)
    pack_theirs, down_chip, low_grad_one, other_vectors = tie(pack_theirs, down_chip, low_grad_one, other_vectors)
    pack_chip = swap_chip(pack_theirs)
    vectors = vectors + other_vectors
    low_grad_one, down_chip = tie(low_grad_one, down_chip)
    pack_mine, plain_0 = attend_back(low_grad_one, qkv_0, turned_0, log_0, pack)
    pack_mine, vectors, down_chip, *up_got = tie(pack_mine, vectors, down_chip, *up_got)

    down_parts = [add(m, t) for m, t in zip(cut(down_mine), cut(down_chip))]
    up_now = add(up_near[0], *up_got)
    up_now, *down_parts = tie(up_now, *down_parts)
    up_now, up_theirs = up_now[: model // 4], up_now[model // 4 :]
    down_got = swaps.scatter(down_parts)
    up_chip = swap_chip(up_theirs)
    keep, send = call(
        tokens_kernel,
        [(half_row, F32), (half_row, BF16)],
        (flags, grad_one, plain_0, plain_2, pack, pack_2),
        scalars=1,
        scratch=[pltpu.VMEM((rows, model), F32)],
    )
    keep, send, pack_chip, pack_mine, *down_got = tie(keep, send, pack_chip, pack_mine, *down_got)
    pack_parts = [add(m, t) for m, t in zip(cut(pack_mine), cut(pack_chip))]
    down_now = add(down_parts[0], *down_got)
    *pack_parts, down_now, send, vectors = tie(*pack_parts, down_now, send, vectors)
    pack_got = swaps.scatter(pack_parts)
    down_far = swaps.far(down_now, far_masks[0])
    up_chip, send, vectors, keep = tie(up_chip, send, vectors, keep)
    up_now = add(up_now, up_chip)
    up_now, vectors = tie(up_now, vectors)
    up_far = swaps.far(up_now, far_masks[0])
    got = swap_core(send)
    other_vectors = swap_chip(vectors)
    (tokens_grad,) = call(last_kernel, [(half_row, F32)], (keep, got))
    *pack_got, tokens_grad, other_vectors, down_far = tie(*pack_got, tokens_grad, other_vectors, down_far)
    pack_now, down_now = add(pack_parts[0], *pack_got), add(down_now, down_far)
    for mask in far_masks[1:]:
        down_now = add(down_now, swaps.far(down_now, mask))
    vectors = vectors + other_vectors
    pack_now, down_now, vectors, up_far = tie(pack_now, down_now, vectors, up_far)
    pack_far = swaps.far(pack_now, far_masks[0])
    down_all = [down_now] + swaps.gather(down_now)
    up_now = add(up_now, up_far)
    for mask in far_masks[1:]:
        up_now = add(up_now, swaps.far(up_now, mask))
    other_vectors = swap_replica(vectors, 1)
    pack_far, up_now, other_vectors, *down_all = tie(pack_far, up_now, other_vectors, *down_all)
    pack_now = add(pack_now, pack_far)
    for mask in far_masks[1:]:
        pack_now = add(pack_now, swaps.far(pack_now, mask))
    vectors = vectors + other_vectors
    pack_now, vectors, up_now = tie(pack_now, vectors, up_now)
    pack_all = [pack_now] + swaps.gather(pack_now)
    up_all = [up_now] + swaps.gather(up_now)
    for mask in [2] + far_masks:
        vectors = vectors + swap_replica(vectors, mask)
    down_weight_grad = jnp.concatenate(swaps.placed(down_all), axis=0).astype(F32)
    up_weight_grad = jnp.concatenate(swaps.placed(up_all), axis=0).astype(F32)
    pack_all = swaps.placed(pack_all)
    query_grad, key_grad, value_grad, out_grad = [v[:width].astype(F32) for v in pack_all]
    query_bias_grad, value_bias_grad = [pack_all[i][width, :width].astype(F32) for i in (0, 2)]
    up_bias_row = lax.dynamic_index_in_dim(vectors, 6 + place, 0, keepdims=False)
    return (
        layer_output,
        tokens_grad,
        query_grad.T,
        query_bias_grad,
        key_grad.T,
        value_grad.T,
        value_bias_grad,
        out_grad,
        vectors[0],
        vectors[1],
        vectors[2],
        up_weight_grad,
        up_bias_row,
        down_weight_grad,
        vectors[5],
        vectors[3],
        vectors[4],
    )


def solution(mesh):
    placed = (
        P(("dp", "tensor"), None),
        P("dp", None),
        P(("dp", "tensor"), None),
        P(None, "tensor"),
        P("tensor"),
        P(None, "tensor"),
        P(None, "tensor"),
        P("tensor"),
        P("tensor", None),
        P(),
        P(),
        P(),
        P(None, "tensor"),
        P("tensor"),
        P("tensor", None),
        P(),
        P(),
        P(),
    )
    return jax.shard_map(
        functools.partial(body, mesh.shape["dp"]),
        mesh=mesh,
        in_specs=placed,
        out_specs=(
            P(("dp", "tensor"), None),
            P(("dp", "tensor"), None),
            P(None, "tensor"),
            P("tensor"),
            P(None, "tensor"),
            P(None, "tensor"),
            P("tensor"),
            P("tensor", None),
            P(),
            P(),
            P(),
            P(None, "tensor"),
            P("tensor"),
            P("tensor", None),
            P(),
            P(),
            P(),
        ),
        check_vma=False,
    )
```

```python
import functools

import jax
import jax.numpy as jnp
from jax import lax
from jax.experimental import pallas as pl
from jax.experimental.pallas import tpu as pltpu
from jax.sharding import PartitionSpec as P

HEAD_DIM = 64
MOST = 256
EPSILON = 1e-05
MASKED = -1e30
BLOCK = 256
STRIP = 64
LANES = 128
BIAS_ROWS = 16
VMEM_LIMIT = 16 * 1024 * 1024
PACK_LIMIT = 60 * 1024 * 1024
TAIL_SCALE = 0.425
TAIL = (
    0.23966740682492862,
    0.24201181237516,
    0.19964184258583956,
    0.2585875675603689,
    -0.10985333090134082,
    0.4147788772153898,
    -0.3173079260911745,
    0.07247363954140279,
)

BF16 = jnp.bfloat16
F32 = jnp.float32


def product(left_side, right_side):
    return jnp.dot(left_side, right_side, preferred_element_type=F32)


def rows_product(left_side, right_side):
    return lax.dot_general(
        left_side, right_side, (((0,), (0,)), ((), ())), preferred_element_type=F32
    )


def cols_product(left_side, right_side):
    return lax.dot_general(
        left_side, right_side, (((1,), (1,)), ((), ())), preferred_element_type=F32
    )


def normal_parts(z):
    size = jnp.abs(z)
    t = 1.0 / (1.0 + (TAIL_SCALE * 0.7071067811865476) * size)
    series = TAIL[-1]
    for factor in TAIL[-2::-1]:
        series = series * t + factor
    bell = jnp.exp(-0.5 * z * z)
    tail = (0.5 * bell) * (series * t)
    return jnp.where(z >= 0.0, 1.0 - tail, tail), bell * 0.3989422804014327


def call(kernel, outs, args, scalars=0, scratch=(), cost=1.0, far=()):
    specs = [pl.BlockSpec(memory_space=pltpu.SMEM)] * scalars
    specs += [pl.BlockSpec(memory_space=pltpu.VMEM)] * (len(args) + len(outs) - scalars)
    for i in far:
        specs[i] = pl.BlockSpec(memory_space=pl.ANY)
    outputs = pl.pallas_call(
        kernel,
        in_specs=specs[: len(args)],
        out_specs=specs[len(args) :],
        out_shape=[jax.ShapeDtypeStruct(shape, dtype) for shape, dtype in outs],
        scratch_shapes=list(scratch),
        compiler_params=pltpu.CompilerParams(vmem_limit_bytes=VMEM_LIMIT),
        cost_estimate=pl.CostEstimate(
            flops=0, bytes_accessed=0, transcendentals=0
        ),
    )(*args)
    return list(outputs)


def piece(index, size):
    return pl.ds(pl.multiple_of(index * size, 16), size)


def assemble(side, refs, out_ref):
    size, count = refs[0].shape[0], len(refs) // 2
    for i, ref in enumerate(refs):
        first = side if i < count else 1 - side
        out_ref[piece(first * count + i % count, size), :] = ref[...]


def row(ref):
    return ref[...].reshape(1, -1)


def join_parts(flags_ref, own_refs, other_refs, out_ref):
    for side, parts in ((flags_ref[1], own_refs), (1 - flags_ref[1], other_refs)):
        for i, part in enumerate(parts):
            out_ref[piece(side * len(parts) + i, part.shape[0]), :] = part[...]


def join(flags_ref, own_ref, other_ref, out_ref):
    size = own_ref.shape[0]
    out_ref[piece(flags_ref[1], size), :] = own_ref[...]
    out_ref[piece(1 - flags_ref[1], size), :] = other_ref[...]


def pieces_kernel(
    flags_ref, query_b_ref, value_b_ref, up_b_ref, query_ref, key_ref, value_ref, out_w_ref, piece_a, piece_b,
    near_a, near_b, sems,
):
    weights = (query_ref, key_ref, value_ref, out_w_ref)
    width, model = query_ref.shape
    for side in range(2):

        @pl.when(flags_ref[0] == side)
        def load():
            for k, near in enumerate((near_a, near_b)):
                pltpu.make_async_copy(weights[2 * side + k], near.at[:width], sems.at[k]).start()

    blank = jnp.zeros((1, model - 2 * width), F32)
    rows = []
    for part in (row(up_b_ref), jnp.concatenate([row(query_b_ref), row(value_b_ref), blank], axis=1)):
        for _ in range(3):
            rows.append(part.astype(BF16).astype(F32))
            part = part - rows[-1]
    rows.append(jnp.zeros((BIAS_ROWS - 6, model), F32))
    near_a[width:, :] = jnp.concatenate(rows, axis=0).astype(BF16)
    for k, near in enumerate((near_a, near_b)):
        pltpu.make_async_copy(weights[k], near.at[:width], sems.at[k]).wait()
    outs = [
        pltpu.make_async_copy(near, out, sems.at[2 + k])
        for k, (near, out) in enumerate(((near_a, piece_a), (near_b, piece_b)))
    ]
    for copy in outs:
        copy.start()
    for copy in outs:
        copy.wait()


def pack_kernel(
    flags_ref, query_ref, key_ref, value_ref, out_w_ref, up_ref, down_ref, pack_ref, both_out, pack_near, both_near, sems,
):
    width = query_ref.shape[0]
    half = both_out.shape[0] // 2
    sources = (up_ref.at[piece(flags_ref[5], half)], down_ref.at[piece(flags_ref[6], half)])
    loads = [(s, both_near.at[i * half : (i + 1) * half]) for i, s in enumerate(sources)]
    weights = (query_ref, key_ref, value_ref, out_w_ref)
    loads += [(s, pack_near.at[i * width : (i + 1) * width]) for i, s in enumerate(weights)]
    copies = [pltpu.make_async_copy(a, b, sems.at[i]) for i, (a, b) in enumerate(loads)]
    for copy in copies:
        copy.start()
    for copy in copies:
        copy.wait()
    copies = [pltpu.make_async_copy(both_near, both_out, sems.at[6]), pltpu.make_async_copy(pack_near, pack_ref, sems.at[7])]
    for copy in copies:
        copy.start()
    for copy in copies:
        copy.wait()


def document_lanes(flags_ref, lengths_ref, rows):
    shape = (rows, LANES - HEAD_DIM)
    spot = lax.broadcasted_iota(jnp.int32, shape, 0)
    lane = lax.broadcasted_iota(jnp.int32, (1, shape[1]), 1)
    ends = 0
    begin_row, end_row = jnp.zeros_like(lane), jnp.zeros_like(lane)
    documents = lengths_ref.shape[1]
    for d in range(documents):
        begin_row = jnp.where(lane == d, ends, begin_row)
        ends = ends + lengths_ref[flags_ref[2], d]
        end_row = jnp.where(lane == d, ends, end_row)
    inside = (spot >= begin_row) & (spot < end_row)
    outside = jnp.where(lane < documents, MASKED, 0.0)
    return jnp.where(inside, 1.0, 0.0).astype(BF16), jnp.where(inside, 0.0, outside).astype(BF16)


def window(i, rows):
    return slice(max(i - 1, 0) * BLOCK, min(i + 2, rows // BLOCK) * BLOCK)


def attend_units(
    flags_ref, lengths_ref, x_ref, w_ref, biases, heads_ref, context_ref, turned_ref, log_ref, values_ref,
):
    rows, model = x_ref.shape
    width = context_ref.shape[1]
    heads = width // HEAD_DIM
    same, other = document_lanes(flags_ref, lengths_ref, rows)
    tails = (other, same, jnp.zeros_like(same))
    for i, bias in enumerate((biases[0], None, biases[1])):
        weights = w_ref[i * width : (i + 1) * width, :]
        for r in range(0, rows, 2 * BLOCK):
            here = slice(r, r + 2 * BLOCK)
            total = cols_product(x_ref[here, :], weights)
            if bias is not None:
                total = total + bias
            low = total.astype(BF16)
            if i == 0:
                low = low * BF16(HEAD_DIM**-0.5)
            for h in range(heads):
                part = low[:, h * HEAD_DIM : (h + 1) * HEAD_DIM]
                heads_ref[i * heads + h, here, :] = jnp.concatenate([part, tails[i][here, :]], axis=1)
            if i == 2:
                values_ref[:, here] = low.T
    for i in range(rows // BLOCK):
        here, seen = slice(i * BLOCK, (i + 1) * BLOCK), window(i, rows)
        for h in range(heads):
            part = slice(h * HEAD_DIM, (h + 1) * HEAD_DIM)
            queries = heads_ref[h, here, :]
            steps = range(seen.start, seen.stop, BLOCK)
            scores = [cols_product(heads_ref[heads + h, r : r + BLOCK, :], queries) for r in steps]
            top = functools.reduce(jnp.maximum, [jnp.max(s, axis=0, keepdims=True) for s in scores])
            total, context = 0.0, 0.0
            for r, score in zip(steps, scores):
                weights = jnp.exp(score - top)
                total = total + jnp.sum(weights, axis=0, keepdims=True)
                context = context + product(values_ref[part, r : r + BLOCK], weights.astype(BF16))
            turned_ref[part, here] = context * (1.0 / total)
            log_ref[h : h + 1, here] = top + jnp.log(total)
        context_ref[here, :] = turned_ref[:, here].T.astype(BF16)


def attend_kernel(
    flags_ref, lengths_ref, w_ref, query_b_ref, value_b_ref, tokens_ref, other_ref,
    x_ref, heads_ref, context_ref, turned_ref, log_ref, values_ref,
):
    join(flags_ref, tokens_ref, other_ref, x_ref)
    biases = (row(query_b_ref), row(value_b_ref))
    attend_units(
        flags_ref, lengths_ref, x_ref, w_ref, biases, heads_ref, context_ref, turned_ref, log_ref, values_ref
    )


def share(flags_ref, total_ref, keep_ref, *send_refs):
    size = keep_ref.shape[0]
    keep_ref[...] = total_ref[piece(flags_ref[1], size), :]
    part = size // len(send_refs)
    for i, send_ref in enumerate(send_refs):
        send_ref[...] = total_ref[piece((1 - flags_ref[1]) * len(send_refs) + i, part), :].astype(BF16)


def attend_last_kernel(
    flags_ref, lengths_ref, w_0, w_1, w_2, w_3, x_ref, before_ref, w_before,
    w_ref, heads_ref, turned_ref, log_ref, bias_ref, keep_ref, send_a, send_b, values_ref, context_ref, mix_ref,
):
    width = context_ref.shape[1]
    side = flags_ref[0] * 2
    for ref, spot in ((w_0, side), (w_1, side + 1), (w_2, 2 - side), (w_3, 3 - side)):
        w_ref[piece(spot, width), :] = ref[:width, :]
    parts = w_0[width : width + 6, :].astype(F32)
    bias_ref[0:1, :] = parts[0:1] + parts[1:2] + parts[2:3]
    mixed = parts[3:4] + parts[4:5] + parts[5:6]
    biases = (mixed[:, :width], mixed[:, width : 2 * width])
    attend_units(
        flags_ref, lengths_ref, x_ref, w_ref, biases, heads_ref, context_ref, turned_ref, log_ref, values_ref
    )
    for r in range(0, x_ref.shape[0], BLOCK):
        here = slice(r, r + BLOCK)
        mix_ref[here, :] = product(before_ref[here, :], w_before[3 * width :, :]) + product(
            context_ref[here, :], w_ref[3 * width :, :]
        )
    share(flags_ref, mix_ref, keep_ref, send_a, send_b)


def strips(rows, step):
    def one(i, carry):
        step(pl.ds(pl.multiple_of(i * STRIP, STRIP), STRIP))
        return carry

    lax.fori_loop(0, rows // STRIP, one, 0, unroll=2)


def norm_one_kernel(
    tokens_ref, keep_ref, got_a, got_b, out_b_ref, gain_ref, shift_ref, normal_ref, inverse_ref, hidden_a, hidden_b, got_ref, hidden_ref,
):
    half = got_a.shape[0]
    got_ref[:half, :] = got_a[...]
    got_ref[half:, :] = got_b[...]

    def step(here):
        values = tokens_ref[here, :].astype(F32) + keep_ref[here, :] + got_ref[here, :].astype(F32) + row(out_b_ref)
        centered = values - jnp.mean(values, axis=1, keepdims=True)
        inverse = lax.rsqrt(jnp.mean(centered * centered, axis=1, keepdims=True) + EPSILON)
        normal = centered * inverse
        normal_ref[here, :] = normal
        inverse_ref[here, :] = inverse
        hidden_ref[here, :] = (normal * row(gain_ref) + row(shift_ref)).astype(BF16)

    strips(tokens_ref.shape[0], step)
    hidden_a[...] = hidden_ref[:half, :]
    hidden_b[...] = hidden_ref[half:, :]


def feed_units(hidden_ref, up_ref, down_ref, bias, active_ref, slope_ref, sum_ref, before_ref):
    units = up_ref.shape[1]
    for u in range(0, units, BLOCK):
        for r in range(0, hidden_ref.shape[0], 2 * BLOCK):
            here = slice(r, r + 2 * BLOCK)
            pre_up = bias[:, u : u + BLOCK] + product(hidden_ref[here, :], up_ref[:, u : u + BLOCK])
            cumulative, density = normal_parts(pre_up)
            active = (pre_up * cumulative).astype(BF16)
            active_ref[u : u + BLOCK, here] = active.T
            slope_ref[here, u : u + BLOCK] = (cumulative + pre_up * density).astype(BF16)
            now = product(active, down_ref[u : u + BLOCK, :])
            if u:
                sum_ref[here, :] += now
            elif before_ref is not None:
                sum_ref[here, :] = before_ref[here, :] + now
            else:
                sum_ref[here, :] = now


def feed_kernel(
    flags_ref, own_a, own_b, other_a, other_b, up_ref, down_ref, bias_ref,
    hidden_ref, turned_ref, active_ref, slope_ref, sum_ref,
):
    join_parts(flags_ref, (own_a, own_b), (other_a, other_b), hidden_ref)
    turned_ref[...] = hidden_ref[...].T
    feed_units(hidden_ref, up_ref, down_ref, row(bias_ref), active_ref, slope_ref, sum_ref, None)


def feed_last_kernel(
    flags_ref, hidden_ref, both_ref, up_b, down_b, bias_ref, before_ref,
    up_ref, down_ref, active_ref, slope_ref, keep_ref, send_ref, sum_ref,
):
    half = up_b.shape[0]
    for side, first, other, out in ((flags_ref[5], 0, up_b, up_ref), (flags_ref[6], half, down_b, down_ref)):
        out[piece(side, half), :] = both_ref[first : first + half, :]
        out[piece(1 - side, half), :] = other[...]
    feed_units(hidden_ref, up_ref, down_ref, bias_ref[0:1, :], active_ref, slope_ref, sum_ref, before_ref)
    share(flags_ref, sum_ref, keep_ref, send_ref)


def norm_two_kernel(
    keep_ref, got_ref, normal_ref, gain_one_ref, shift_one_ref, down_b_ref, gain_ref, shift_ref, cotangent_ref,
    out_ref, grad_ref, low_ref, vector_ref,
):
    vector_ref[...] = jnp.zeros_like(vector_ref)

    def step(here):
        values = keep_ref[here, :] + got_ref[here, :].astype(F32) + row(down_b_ref)
        values = values + (normal_ref[here, :] * row(gain_one_ref) + row(shift_one_ref))
        centered = values - jnp.mean(values, axis=1, keepdims=True)
        inverse = lax.rsqrt(jnp.mean(centered * centered, axis=1, keepdims=True) + EPSILON)
        normal = centered * inverse
        out_ref[here, :] = (normal * row(gain_ref) + row(shift_ref)).astype(BF16)
        upstream = cotangent_ref[here, :].astype(F32)
        scaled = upstream * row(gain_ref)
        first = jnp.mean(scaled, axis=1, keepdims=True)
        second = jnp.mean(scaled * normal, axis=1, keepdims=True)
        grad = inverse * (scaled - first - normal * second)
        grad_ref[here, :] = grad
        low_ref[here, :] = grad.astype(BF16)
        vector_ref[0:1, :] += jnp.sum(upstream * normal, axis=0, keepdims=True)
        vector_ref[1:2, :] += jnp.sum(upstream, axis=0, keepdims=True)
        vector_ref[2:3, :] += jnp.sum(grad, axis=0, keepdims=True)

    strips(keep_ref.shape[0], step)


def quarters(flags_ref, size):
    return [pl.ds(pl.multiple_of(jnp.bitwise_xor(flags_ref[4], i) * size, 16), size) for i in range(4)]


def feed_back_units(
    flags_ref, grad_ref, active_ref, slope_ref, hidden_ref, up_ref, down_ref, before_ref,
    down_grad_ref, bias_grad_ref, sum_ref, turned_ref, grad_pre_ref,
):
    rows, model = grad_ref.shape
    units = slope_ref.shape[1]
    for i, where in enumerate(quarters(flags_ref, units // 4)):
        value = product(active_ref[i * (units // 4) : (i + 1) * (units // 4), :], grad_ref[...])
        down_grad_ref[where, :] = value.astype(BF16)
    for u in range(0, units, BLOCK):
        here = slice(u, u + BLOCK)
        total = 0.0
        for r in range(0, rows, 2 * BLOCK):
            grad_active = cols_product(grad_ref[r : r + 2 * BLOCK, :], down_ref[here, :])
            grad_pre = (slope_ref[r : r + 2 * BLOCK, here].astype(F32) * grad_active).astype(BF16)
            grad_pre_ref[r : r + 2 * BLOCK, here] = grad_pre
            total = total + jnp.sum(grad_pre.astype(F32), axis=0, keepdims=True)
            bias_grad_ref[:, here] = jnp.concatenate([total, jnp.zeros((7, total.shape[1]), F32)], axis=0)
    for i, where in enumerate(quarters(flags_ref, model // 4)):
        value = product(hidden_ref[i * (model // 4) : (i + 1) * (model // 4), :], grad_pre_ref[...])
        turned_ref[where, :] = value.astype(BF16)
    for r in range(0, rows, BLOCK):
        value = cols_product(grad_pre_ref[r : r + BLOCK, :], up_ref[...])
        if before_ref is not None:
            value = value + before_ref[r : r + BLOCK, :]
        sum_ref[r : r + BLOCK, :] = value


def feed_back_theirs_kernel(
    flags_ref, own_ref, other_ref, active_ref, slope_ref, hidden_ref, up_ref, down_ref,
    grad_ref, down_grad_ref, near_0, near_1, near_2, near_3, bias_grad_ref, sum_ref, turned_ref, grad_pre_ref,
):
    join(flags_ref, own_ref, other_ref, grad_ref)
    feed_back_units(
        flags_ref, grad_ref, active_ref, slope_ref, hidden_ref, up_ref, down_ref, None,
        down_grad_ref, bias_grad_ref, sum_ref, turned_ref, grad_pre_ref,
    )
    quarter = near_0.shape[0]
    for i, near in enumerate((near_0, near_1, near_2, near_3)):
        near[...] = turned_ref[i * quarter : (i + 1) * quarter, :]


def feed_back_mine_kernel(
    flags_ref, grad_ref, active_ref, slope_ref, hidden_ref, up_ref, down_ref, before_ref,
    theirs_0, theirs_1, theirs_2, theirs_3, grad_two_ref,
    down_grad_ref, near_0, near_1, near_2, near_3, bias_grad_ref, keep_ref, send_a, send_b, sum_ref, turned_ref, grad_pre_ref,
):
    feed_back_units(
        flags_ref, grad_ref, active_ref, slope_ref, hidden_ref, up_ref, down_ref, before_ref,
        down_grad_ref, bias_grad_ref, sum_ref, turned_ref, grad_pre_ref,
    )
    quarter = theirs_0.shape[0]
    theirs = (theirs_0, theirs_1, theirs_2, theirs_3)
    for i, near in enumerate((near_0, near_1, near_2, near_3)):
        near[:quarter, :] = turned_ref[i * quarter : (i + 1) * quarter, :]
        near[quarter:, :] = theirs[i][...]
    share(flags_ref, sum_ref, keep_ref, send_a, send_b)
    keep_ref[...] += grad_two_ref[...]


def norm_one_back_kernel(
    keep_ref, got_a, got_b, normal_ref, inverse_ref, gain_ref, two_ref,
    grad_ref, low_a, low_b, vector_ref, got_ref, low_ref,
):
    vector_ref[...] = jnp.zeros_like(vector_ref)
    half = got_a.shape[0]
    got_ref[:half, :] = got_a[...]
    got_ref[half:, :] = got_b[...]

    def step(here):
        upstream, normal = keep_ref[here, :] + got_ref[here, :].astype(F32), normal_ref[here, :]
        scaled = upstream * row(gain_ref)
        first = jnp.mean(scaled, axis=1, keepdims=True)
        second = jnp.mean(scaled * normal, axis=1, keepdims=True)
        grad = inverse_ref[here, :] * (scaled - first - normal * second)
        grad_ref[here, :] = grad
        low_ref[here, :] = grad.astype(BF16)
        vector_ref[0:1, :] += jnp.sum(grad, axis=0, keepdims=True)
        vector_ref[1:2, :] += jnp.sum(upstream * normal, axis=0, keepdims=True)
        vector_ref[2:3, :] += jnp.sum(upstream, axis=0, keepdims=True)

    strips(keep_ref.shape[0], step)
    vector_ref[3:6, :] = two_ref[0:3, :]
    low_a[...] = low_ref[:half, :]
    low_b[...] = low_ref[half:, :]


def attend_back_kernel(
    flags_ref, own_a, own_b, other_a, other_b, vectors_ref, other_vectors_ref, up_sum_ref,
    x_ref, heads_ref, context_ref, log_ref, w_ref, out_ref, plain_ref,
    grad_ref, grad_heads_ref, inner_ref, turned_ref, keys_ref, values_ref,
):
    rows, model = x_ref.shape
    width = context_ref.shape[0]
    heads = width // HEAD_DIM
    size = width + BIAS_ROWS
    join_parts(flags_ref, (own_a, own_b), (other_a, other_b), grad_ref)
    blank = jnp.zeros((2 * BLOCK, LANES - HEAD_DIM), BF16)
    for r in range(0, rows, 2 * BLOCK):
        here = slice(r, r + 2 * BLOCK)
        low = cols_product(grad_ref[here, :], w_ref[3 * width :, :]).astype(BF16)
        turned = low.T.astype(F32) * context_ref[:, here]
        for h in range(heads):
            part = slice(h * HEAD_DIM, (h + 1) * HEAD_DIM)
            grad_heads_ref[h, here, :] = jnp.concatenate([low[:, part], blank], axis=1)
            inner_ref[h : h + 1, here] = jnp.sum(turned[part, :], axis=0, keepdims=True)
    keys_ref[...] = jnp.zeros_like(keys_ref)
    values_ref[...] = jnp.zeros_like(values_ref)
    for i in range(rows // BLOCK):
        here, seen = slice(i * BLOCK, (i + 1) * BLOCK), window(i, rows)
        for h in range(heads):
            queries, grads, key_rows = heads_ref[h, here, :], grad_heads_ref[h, here, :], heads_ref[heads + h, seen, :]
            probs = jnp.exp(cols_product(key_rows, queries) - log_ref[h : h + 1, here])
            grad_probs = cols_product(heads_ref[2 * heads + h, seen, :], grads)
            grad_scores = (probs * (grad_probs - inner_ref[h : h + 1, here])).astype(BF16)
            values_ref[h, seen, :] += product(probs.astype(BF16), grads)
            keys_ref[h, seen, :] += product(grad_scores, queries)
            grad_queries = rows_product(key_rows, grad_scores)[:HEAD_DIM, :] * (HEAD_DIM**-0.5)
            turned_ref[h * HEAD_DIM : (h + 1) * HEAD_DIM, here] = grad_queries.astype(BF16)
    for i, ref in ((1, keys_ref), (2, values_ref)):
        for h in range(heads):
            first = i * width + h * HEAD_DIM
            turned_ref[first : first + HEAD_DIM, :] = ref[h].T[:HEAD_DIM, :].astype(BF16)
    for i in range(3):
        plain_ref[:, i * 2 * LANES : i * 2 * LANES + width] = turned_ref[i * width : (i + 1) * width, :].T
    tops = [jnp.zeros((8, model), F32)] * 4
    for i in (0, 2):
        top = jnp.sum(plain_ref[:, i * 2 * LANES : i * 2 * LANES + width].astype(F32), axis=0, keepdims=True)
        top = jnp.concatenate([top, jnp.zeros((1, model - width), F32)], axis=1)
        tops[i] = jnp.concatenate([top, jnp.zeros((7, model), F32)], axis=0)
    tops[1] = up_sum_ref[...]
    tops[3] = vectors_ref[...] + other_vectors_ref[...]
    for i, here in enumerate(quarters(flags_ref, size)):
        if i < 3:
            grad = product(turned_ref[i * width : (i + 1) * width, :], x_ref[...])
        else:
            grad = product(context_ref[...].astype(BF16), grad_ref[...])
        blank = jnp.zeros((BIAS_ROWS - 8, model), F32)
        out_ref[here, :] = jnp.concatenate([grad, tops[i], blank], axis=0).astype(BF16)


def tokens_kernel(flags_ref, grad_ref, plain_0, plain_2, w_0, w_2, keep_ref, send_ref, sum_ref):
    rows, model = plain_0.shape[0], grad_ref.shape[1]
    width = w_0.shape[0] // 4
    for r in range(0, rows, BLOCK):
        total = 0.0
        for plain, w_ref in ((plain_0, w_0), (plain_2, w_2)):
            for i in range(3):
                total = total + product(
                    plain[r : r + BLOCK, i * 2 * LANES : i * 2 * LANES + width], w_ref[i * width : (i + 1) * width, :]
                )
        sum_ref[r : r + BLOCK, :] = total
    share(flags_ref, sum_ref, keep_ref, send_ref)
    keep_ref[...] += grad_ref[...]


def last_kernel(keep_ref, got_ref, out_ref):
    out_ref[...] = keep_ref[...] + got_ref[...].astype(F32)


def unpack_kernel(
    flags_ref, part_0, part_1, part_2, part_3,
    query_ref, key_ref, value_ref, out_w_ref, query_b_ref, value_b_ref, up_b_ref, *refs,
):
    vector_refs, parts = refs[:-1], refs[-1]
    for i, ref in enumerate((part_0, part_1, part_2, part_3)):
        parts[jnp.bitwise_xor(flags_ref[4], i)] = ref[...]
    width = query_ref.shape[0]
    for i, ref in enumerate((query_ref, key_ref, value_ref, out_w_ref)):
        ref[...] = parts[i, :width, :].astype(F32)
    tops = [parts[i, width : width + BIAS_ROWS, :].astype(F32) for i in range(4)]
    query_b_ref[...] = tops[0][0, :width]
    value_b_ref[...] = tops[2][0, :width]
    up_b_ref[...] = tops[1][0, :]
    for i, ref in enumerate(vector_refs):
        ref[...] = tops[3][i, :]


def tie(*arrays):
    return lax.optimization_barrier(arrays)


def add(*members):
    members = [m.astype(F32) for m in members]
    while len(members) > 1:
        members = [a + b for a, b in zip(members[::2], members[1::2])]
    return members[0].astype(BF16)


class Swaps:
    def __init__(self, dp_size, replica):
        self.dp_size, self.near = dp_size, replica & 3

    def core(self, values_in):
        return lax.ppermute(values_in, "tensor", [(i, i ^ 1) for i in range(4)])

    def chip(self, values_in):
        return lax.ppermute(values_in, "tensor", [(i, i ^ 2) for i in range(4)])

    def replica(self, values_in, mask):
        return lax.ppermute(values_in, "dp", [(i, i ^ mask) for i in range(self.dp_size)])

    def scatter(self, parts):
        return [self.replica(parts[m], m) for m in (1, 2, 3)]

    def far(self, value, mask):
        return self.replica(value, mask)

    def gather(self, value):
        return [self.replica(value, m) for m in (1, 2, 3)]

    @property
    def far_masks(self):
        return [1 << b for b in range(2, self.dp_size.bit_length() - 1)]

    def placed(self, members):
        return [lax.select_n(self.near, *[members[i ^ p] for p in range(4)]) for i in range(4)]


def cut_pair(value):
    half = value.shape[0] // 2
    return [value[:half], value[half:]]


def cut(value):
    size = value.shape[0] // 4
    return [value[i * size : (i + 1) * size] for i in range(4)]


def first_calls(
    flags, query_bias, value_bias, up_bias, query_weight, key_weight, value_weight, out_weight, up_weight, down_weight,
):
    model, width = query_weight.shape
    far, vmem = pl.BlockSpec(memory_space=pl.ANY), pl.BlockSpec(memory_space=pltpu.VMEM)
    smem = pl.BlockSpec(memory_space=pltpu.SMEM)
    params = dict(
        compiler_params=pltpu.CompilerParams(vmem_limit_bytes=PACK_LIMIT),
        cost_estimate=pl.CostEstimate(flops=0, bytes_accessed=0, transcendentals=0),
    )
    weights = (query_weight.T, key_weight.T, value_weight.T, out_weight)
    shapes = [(width + BIAS_ROWS, model), (width, model)]
    pieces = pl.pallas_call(
        pieces_kernel,
        in_specs=[smem] + [vmem] * 3 + [far] * 4,
        out_specs=[far] * 2,
        out_shape=[jax.ShapeDtypeStruct(s, BF16) for s in shapes],
        scratch_shapes=[pltpu.VMEM(s, BF16) for s in shapes] + [pltpu.SemaphoreType.DMA((4,))],
        **params,
    )(flags, query_bias, value_bias, up_bias, *weights)
    pieces, weights = tie(pieces, weights)
    outs = [(4 * width, model), up_weight.shape]
    rest = pl.pallas_call(
        pack_kernel,
        in_specs=[smem] + [far] * 6,
        out_specs=[far] * 2,
        out_shape=[jax.ShapeDtypeStruct(s, BF16) for s in outs],
        scratch_shapes=[pltpu.VMEM(s, BF16) for s in outs] + [pltpu.SemaphoreType.DMA((8,))],
        **params,
    )(flags, *weights, up_weight, down_weight)
    return [*pieces, *rest]


def body(
    dp_size,
    tokens,
    lengths,
    cotangent,
    query_weight,
    query_bias,
    key_weight,
    value_weight,
    value_bias,
    out_weight,
    out_bias,
    gain_one,
    shift_one,
    up_weight,
    up_bias,
    down_weight,
    down_bias,
    gain_two,
    shift_two,
):
    own, model = tokens.shape
    width = query_weight.shape[1]
    units = up_weight.shape[1]
    rows = 2 * own
    place = lax.axis_index("tensor")
    replica = lax.axis_index("dp")
    flags = [(replica ^ (replica >> 1)) & 1, place % 2, place // 2, place, replica & 3, (replica >> 1) & 1, replica & 1]
    flags = jnp.stack(flags).astype(jnp.int32)
    swaps = Swaps(dp_size, replica)
    swap_core, swap_chip, swap_replica = swaps.core, swaps.chip, swaps.replica
    far_masks = swaps.far_masks

    other_tokens = swap_core(tokens)
    pack_a, pack_b, pack, both_half = first_calls(
        flags, query_bias, value_bias, up_bias, query_weight, key_weight, value_weight, out_weight, up_weight, down_weight
    )
    whole, half_row = (4 * (width + BIAS_ROWS), model), (own, model)
    halves = [((own // 2, model), BF16)] * 2
    heads_shape = ((3 * width // HEAD_DIM, rows, LANES), BF16)
    values_scratch = pltpu.VMEM((width, rows), BF16)
    kept_shapes = [((width, rows), F32), ((8, rows), F32)]
    direct = [swap_chip(pack_a), swap_chip(pack_b)]
    both_direct = swap_chip(both_half)

    inputs, qkv_0, context_0, turned_0, log_0 = call(
        attend_kernel,
        [((rows, model), BF16), heads_shape, ((rows, width), BF16)] + kept_shapes,
        (flags, lengths, pack, query_bias, value_bias, tokens, other_tokens),
        scalars=2,
        scratch=[values_scratch],
    )
    *direct, inputs = tie(*direct, inputs)
    around = [swap_replica(direct[0], 1), swap_replica(direct[1], 2)]
    *around, inputs = tie(*around, inputs)
    pack_2, qkv_2, turned_2, log_2, bias_2, keep, send_a, send_b = call(
        attend_last_kernel,
        [((4 * width, model), BF16), heads_shape] + kept_shapes + [((8, model), F32), (half_row, F32)] + halves,
        (flags, lengths, *direct, *around, inputs, context_0, pack),
        scalars=2,
        scratch=[values_scratch, pltpu.VMEM((rows, width), BF16), pltpu.VMEM((rows, model), F32)],
    )
    got = [swap_core(send_a), swap_core(send_b)]
    normal_one, inverse_one, *hidden = call(
        norm_one_kernel,
        [(half_row, F32), ((own, 1), F32)] + halves,
        (tokens, keep, *got, out_bias, gain_one, shift_one),
        scratch=[pltpu.VMEM(half_row, BF16)] * 2,
    )
    other_hidden = [swap_core(v) for v in hidden]
    hidden[0], other_hidden[0], other_hidden[1], both_direct = tie(hidden[0], *other_hidden, both_direct)
    up_around = swap_replica(both_direct[: model // 2], 2)
    down_around = swap_replica(both_direct[model // 2 :], 1)

    act_shapes = [((units, rows), BF16), ((rows, units), BF16)]
    hidden_full, hidden_turned, active_0, slope_0, before = call(
        feed_kernel,
        [((rows, model), BF16), ((model, rows), BF16)] + act_shapes + [((rows, model), F32)],
        (flags, *hidden, *other_hidden, up_weight, down_weight, up_bias),
        scalars=1,
    )
    before, up_around, down_around = tie(before, up_around, down_around)
    up_2, down_2, active_2, slope_2, keep, send = call(
        feed_last_kernel,
        [((model, units), BF16), ((units, model), BF16)] + act_shapes + [(half_row, F32), (half_row, BF16)],
        (flags, hidden_full, both_direct, up_around, down_around, bias_2, before),
        scalars=1,
        scratch=[pltpu.VMEM((rows, model), F32)],
    )
    layer_output, grad_two, low_grad_two, vector_two = call(
        norm_two_kernel,
        [(half_row, BF16), (half_row, F32), (half_row, BF16), ((8, model), F32)],
        (
            keep, swap_core(send), normal_one, gain_one, shift_one, down_bias,
            gain_two, shift_two, cotangent,
        ),
    )

    back_scratch = [pltpu.VMEM((model, units), BF16), pltpu.VMEM((rows, units), BF16)]
    grad_full, down_theirs, *up_theirs, up_sum_2, running = call(
        feed_back_theirs_kernel,
        [((rows, model), BF16), ((units, model), BF16)] + [((model // 4, units), BF16)] * 4
        + [((8, units), F32), ((rows, model), F32)],
        (flags, low_grad_two, swap_core(low_grad_two), active_2, slope_2, hidden_turned, up_2, down_2),
        scalars=1,
        scratch=back_scratch,
    )
    down_theirs, running = tie(down_theirs, running)
    down_chip = swap_chip(down_theirs)
    down_mine, *up_near, up_sum_0, keep, send_a, send_b = call(
        feed_back_mine_kernel,
        [((units, model), BF16)] + [((model // 2, units), BF16)] * 4
        + [((8, units), F32), (half_row, F32)] + [((own // 2, model), BF16)] * 2,
        (
            flags, grad_full, active_0, slope_0, hidden_turned, up_weight, down_weight, running, *up_theirs, grad_two,
        ),
        scalars=1,
        scratch=[pltpu.VMEM((rows, model), F32)] + back_scratch,
    )
    got = [swap_core(send_a), swap_core(send_b)]
    grad_one, low_a, low_b, vector_one = call(
        norm_one_back_kernel,
        [(half_row, F32)] + halves + [((8, model), F32)],
        (keep, *got, normal_one, inverse_one, gain_one, vector_two),
        scratch=[pltpu.VMEM(half_row, BF16)] * 2,
    )
    low_other = [swap_core(low_a), swap_core(low_b)]
    other_vector = swap_core(vector_one)
    up_got = swaps.scatter(up_near)


    def attend_back(low_a, qkv, turned, log_total, shard, up_sum):
        return call(
            attend_back_kernel,
            [(whole, BF16), ((rows, 6 * LANES), BF16)],
            (
                flags, low_a, low_b, *low_other, vector_one, other_vector, up_sum,
                inputs, qkv, turned, log_total, shard,
            ),
            scalars=1,
            scratch=[
                pltpu.VMEM((rows, model), BF16), pltpu.VMEM((width // HEAD_DIM, rows, LANES), BF16),
                pltpu.VMEM((8, rows), F32), pltpu.VMEM((3 * width, rows), BF16),
                pltpu.VMEM((width // HEAD_DIM, rows, LANES), F32), pltpu.VMEM((width // HEAD_DIM, rows, LANES), F32),
            ],
        )

    pack_theirs, plain_2 = attend_back(low_a, qkv_2, turned_2, log_2, pack_2, up_sum_2)
    pack_theirs, low_a = tie(pack_theirs, low_a)
    pack_chip = swap_chip(pack_theirs)
    pack_mine, plain_0 = attend_back(low_a, qkv_0, turned_0, log_0, pack, up_sum_0)
    keep, send = call(
        tokens_kernel,
        [(half_row, F32), (half_row, BF16)],
        (flags, grad_one, plain_0, plain_2, pack, pack_2),
        scalars=1,
        scratch=[pltpu.VMEM((rows, model), F32)],
    )
    pack_mine, keep, send, down_chip, *up_got = tie(pack_mine, keep, send, down_chip, *up_got)

    down_parts = [add(m, t) for m, t in zip(cut(down_mine), cut(down_chip))]
    up_now = add(up_near[0], *up_got)
    up_now, *down_parts = tie(up_now, *down_parts)
    up_now, up_theirs = up_now[: model // 4], up_now[model // 4 :]
    down_got = swaps.scatter(down_parts)
    up_chip = swap_chip(up_theirs)
    send, *down_got = tie(send, *down_got)
    down_now = add(down_parts[0], *down_got)
    (down_now,) = tie(down_now)
    down_far = swaps.far(down_now, far_masks[0])
    pack_chip, pack_mine = tie(pack_chip, pack_mine)
    pack_parts = [add(m, t) for m, t in zip(cut(pack_mine), cut(pack_chip))]
    pack_parts = tie(*pack_parts)
    pack_got = swaps.scatter(pack_parts)
    up_chip, down_far, send = tie(up_chip, down_far, send)
    up_now, down_now = add(up_now, up_chip), add(down_now, down_far)
    for mask in far_masks[1:]:
        down_now = add(down_now, swaps.far(down_now, mask))
    up_now, down_now = tie(up_now, down_now)
    up_far = swaps.far(up_now, far_masks[0])
    got = swap_core(send)
    (tokens_grad,) = call(last_kernel, [(half_row, F32)], (keep, got))
    *pack_got, tokens_grad, down_now = tie(*pack_got, tokens_grad, down_now)
    pack_now = add(pack_parts[0], *pack_got)
    pack_now, down_now = tie(pack_now, down_now)
    pack_far = swaps.far(pack_now, far_masks[0])
    down_all = [down_now] + swaps.gather(down_now)
    up_now = add(up_now, up_far)
    for mask in far_masks[1:]:
        up_now = add(up_now, swaps.far(up_now, mask))
    pack_far, up_now, *down_all = tie(pack_far, up_now, *down_all)
    pack_now = add(pack_now, pack_far)
    for mask in far_masks[1:]:
        pack_now = add(pack_now, swaps.far(pack_now, mask))
    both = jnp.concatenate([pack_now, up_now], axis=0)
    (both,) = tie(both)
    both_all = [both] + swaps.gather(both)
    pack_all, up_all = [v[: width + BIAS_ROWS] for v in both_all], [v[width + BIAS_ROWS :] for v in both_all]
    down_weight_grad = jnp.concatenate(swaps.placed(down_all), axis=0).astype(F32)
    up_weight_grad = jnp.concatenate(swaps.placed(up_all), axis=0).astype(F32)
    shard = [((width, model), F32)] * 4 + [((width,), F32)] * 2 + [((units,), F32)] + [((model,), F32)] * 6
    (
        query_grad, key_grad, value_grad, out_grad, query_bias_grad, value_bias_grad, up_bias_row, *vectors,
    ) = call(
        unpack_kernel, shard, (flags, *pack_all), scalars=1, scratch=[pltpu.VMEM((4, width + BIAS_ROWS, model), BF16)]
    )
    return (
        layer_output,
        tokens_grad,
        query_grad.T,
        query_bias_grad,
        key_grad.T,
        value_grad.T,
        value_bias_grad,
        out_grad,
        vectors[0],
        vectors[1],
        vectors[2],
        up_weight_grad,
        up_bias_row,
        down_weight_grad,
        vectors[5],
        vectors[3],
        vectors[4],
    )


def solution(mesh):
    placed = (
        P(("dp", "tensor"), None),
        P("dp", None),
        P(("dp", "tensor"), None),
        P(None, "tensor"),
        P("tensor"),
        P(None, "tensor"),
        P(None, "tensor"),
        P("tensor"),
        P("tensor", None),
        P(),
        P(),
        P(),
        P(None, "tensor"),
        P("tensor"),
        P("tensor", None),
        P(),
        P(),
        P(),
    )
    return jax.shard_map(
        functools.partial(body, mesh.shape["dp"]),
        mesh=mesh,
        in_specs=placed,
        out_specs=(
            P(("dp", "tensor"), None),
            P(("dp", "tensor"), None),
            P(None, "tensor"),
            P("tensor"),
            P(None, "tensor"),
            P(None, "tensor"),
            P("tensor"),
            P("tensor", None),
            P(),
            P(),
            P(),
            P(None, "tensor"),
            P("tensor"),
            P("tensor", None),
            P(),
            P(),
            P(),
        ),
        check_vma=False,
    )
```

```python
import functools

import jax
import jax.numpy as jnp
from jax import lax
from jax.experimental import pallas as pl
from jax.experimental.pallas import tpu as pltpu
from jax.sharding import PartitionSpec as P

HEAD_DIM = 64
MOST = 256
EPSILON = 1e-05
MASKED = -1e30
BLOCK = 256
STRIP = 64
LANES = 128
BIAS_ROWS = 16
VMEM_LIMIT = 16 * 1024 * 1024
PACK_LIMIT = 60 * 1024 * 1024
TAIL_SCALE = 0.425
TAIL = (
    0.23966740682492862,
    0.24201181237516,
    0.19964184258583956,
    0.2585875675603689,
    -0.10985333090134082,
    0.4147788772153898,
    -0.3173079260911745,
    0.07247363954140279,
)

BF16 = jnp.bfloat16
F32 = jnp.float32


def product(left_side, right_side):
    return jnp.dot(left_side, right_side, preferred_element_type=F32)


def rows_product(left_side, right_side):
    return lax.dot_general(
        left_side, right_side, (((0,), (0,)), ((), ())), preferred_element_type=F32
    )


def cols_product(left_side, right_side):
    return lax.dot_general(
        left_side, right_side, (((1,), (1,)), ((), ())), preferred_element_type=F32
    )


def normal_parts(z):
    size = jnp.abs(z)
    t = 1.0 / (1.0 + (TAIL_SCALE * 0.7071067811865476) * size)
    series = TAIL[-1]
    for factor in TAIL[-2::-1]:
        series = series * t + factor
    bell = jnp.exp(-0.5 * z * z)
    tail = (0.5 * bell) * (series * t)
    return jnp.where(z >= 0.0, 1.0 - tail, tail), bell * 0.3989422804014327


def call(kernel, outs, args, scalars=0, scratch=(), cost=1.0, far=()):
    specs = [pl.BlockSpec(memory_space=pltpu.SMEM)] * scalars
    specs += [pl.BlockSpec(memory_space=pltpu.VMEM)] * (len(args) + len(outs) - scalars)
    for i in far:
        specs[i] = pl.BlockSpec(memory_space=pl.ANY)
    outputs = pl.pallas_call(
        kernel,
        in_specs=specs[: len(args)],
        out_specs=specs[len(args) :],
        out_shape=[jax.ShapeDtypeStruct(shape, dtype) for shape, dtype in outs],
        scratch_shapes=list(scratch),
        compiler_params=pltpu.CompilerParams(vmem_limit_bytes=VMEM_LIMIT),
        cost_estimate=pl.CostEstimate(
            flops=0, bytes_accessed=0, transcendentals=0
        ),
    )(*args)
    return list(outputs)


def piece(index, size):
    return pl.ds(pl.multiple_of(index * size, 16), size)


def assemble(side, refs, out_ref):
    size, count = refs[0].shape[0], len(refs) // 2
    for i, ref in enumerate(refs):
        first = side if i < count else 1 - side
        out_ref[piece(first * count + i % count, size), :] = ref[...]


def row(ref):
    return ref[...].reshape(1, -1)


def join_parts(flags_ref, own_refs, other_refs, out_ref):
    for side, parts in ((flags_ref[1], own_refs), (1 - flags_ref[1], other_refs)):
        for i, part in enumerate(parts):
            size = out_ref.shape[0] // (2 * len(parts))
            out_ref[piece(side * len(parts) + i, size), :] = part[:size, :]


def join(flags_ref, own_ref, other_ref, out_ref):
    size = own_ref.shape[0]
    out_ref[piece(flags_ref[1], size), :] = own_ref[...]
    out_ref[piece(1 - flags_ref[1], size), :] = other_ref[...]


def pieces_kernel(
    flags_ref, query_b_ref, value_b_ref, up_b_ref, query_ref, key_ref, value_ref, out_w_ref, piece_a, piece_b,
    near_a, near_b, sems,
):
    weights = (query_ref, key_ref, value_ref, out_w_ref)
    width, model = query_ref.shape
    for side in range(2):

        @pl.when(flags_ref[0] == side)
        def load():
            for k, near in enumerate((near_a, near_b)):
                pltpu.make_async_copy(weights[2 * side + k], near.at[:width], sems.at[k]).start()

    blank = jnp.zeros((1, model - 2 * width), F32)
    rows = []
    for part in (row(up_b_ref), jnp.concatenate([row(query_b_ref), row(value_b_ref), blank], axis=1)):
        for _ in range(3):
            rows.append(part.astype(BF16).astype(F32))
            part = part - rows[-1]
    rows.append(jnp.zeros((BIAS_ROWS - 6, model), F32))
    near_a[width:, :] = jnp.concatenate(rows, axis=0).astype(BF16)
    for k, near in enumerate((near_a, near_b)):
        pltpu.make_async_copy(weights[k], near.at[:width], sems.at[k]).wait()
    outs = [
        pltpu.make_async_copy(near, out, sems.at[2 + k])
        for k, (near, out) in enumerate(((near_a, piece_a), (near_b, piece_b)))
    ]
    for copy in outs:
        copy.start()
    for copy in outs:
        copy.wait()


def pack_kernel(
    flags_ref, query_ref, key_ref, value_ref, out_w_ref, up_ref, down_ref,
    pack_ref, up_out, down_out, pack_near, up_near, down_near, sems,
):
    width = query_ref.shape[0]
    half = up_out.shape[0]
    loads = [(ref.at[piece(flags_ref[0], half)], near) for ref, near in ((up_ref, up_near), (down_ref, down_near))]
    weights = (query_ref, key_ref, value_ref, out_w_ref)
    loads += [(s, pack_near.at[i * width : (i + 1) * width]) for i, s in enumerate(weights)]
    copies = [pltpu.make_async_copy(a, b, sems.at[i]) for i, (a, b) in enumerate(loads)]
    for copy in copies:
        copy.start()
    for copy in copies:
        copy.wait()
    stores = ((up_near, up_out), (down_near, down_out), (pack_near, pack_ref))
    copies = [pltpu.make_async_copy(a, b, sems.at[6 + i]) for i, (a, b) in enumerate(stores)]
    for copy in copies:
        copy.start()
    for copy in copies:
        copy.wait()


def document_lanes(flags_ref, lengths_ref, rows):
    shape = (rows, LANES - HEAD_DIM)
    spot = lax.broadcasted_iota(jnp.int32, shape, 0)
    lane = lax.broadcasted_iota(jnp.int32, (1, shape[1]), 1)
    ends = 0
    begin_row, end_row = jnp.zeros_like(lane), jnp.zeros_like(lane)
    documents = lengths_ref.shape[1]
    for d in range(documents):
        begin_row = jnp.where(lane == d, ends, begin_row)
        ends = ends + lengths_ref[flags_ref[2], d]
        end_row = jnp.where(lane == d, ends, end_row)
    inside = (spot >= begin_row) & (spot < end_row)
    outside = jnp.where(lane < documents, MASKED, 0.0)
    return jnp.where(inside, 1.0, 0.0).astype(BF16), jnp.where(inside, 0.0, outside).astype(BF16)


def window(i, rows):
    return slice(max(i - 1, 0) * BLOCK, min(i + 2, rows // BLOCK) * BLOCK)


def attend_units(
    flags_ref, lengths_ref, x_ref, w_ref, biases, heads_ref, context_ref, turned_ref, log_ref, values_ref,
):
    rows, model = x_ref.shape
    width = context_ref.shape[1]
    heads = width // HEAD_DIM
    same, other = document_lanes(flags_ref, lengths_ref, rows)
    tails = (other, same, jnp.zeros_like(same))
    for i, bias in enumerate((biases[0], None, biases[1])):
        weights = w_ref[i * width : (i + 1) * width, :]
        for r in range(0, rows, 2 * BLOCK):
            here = slice(r, r + 2 * BLOCK)
            total = cols_product(x_ref[here, :], weights)
            if bias is not None:
                total = total + bias
            low = total.astype(BF16)
            if i == 0:
                low = low * BF16(HEAD_DIM**-0.5)
            for h in range(heads):
                part = low[:, h * HEAD_DIM : (h + 1) * HEAD_DIM]
                heads_ref[i * heads + h, here, :] = jnp.concatenate([part, tails[i][here, :]], axis=1)
            if i == 2:
                values_ref[:, here] = low.T
    for i in range(rows // BLOCK):
        here, seen = slice(i * BLOCK, (i + 1) * BLOCK), window(i, rows)
        for h in range(heads):
            part = slice(h * HEAD_DIM, (h + 1) * HEAD_DIM)
            queries = heads_ref[h, here, :]
            steps = range(seen.start, seen.stop, BLOCK)
            scores = [cols_product(heads_ref[heads + h, r : r + BLOCK, :], queries) for r in steps]
            top = functools.reduce(jnp.maximum, [jnp.max(s, axis=0, keepdims=True) for s in scores])
            total, context = 0.0, 0.0
            for r, score in zip(steps, scores):
                weights = jnp.exp(score - top)
                total = total + jnp.sum(weights, axis=0, keepdims=True)
                context = context + product(values_ref[part, r : r + BLOCK], weights.astype(BF16))
            turned_ref[part, here] = context * (1.0 / total)
            log_ref[h : h + 1, here] = top + jnp.log(total)
        context_ref[here, :] = turned_ref[:, here].T.astype(BF16)


def attend_kernel(
    flags_ref, lengths_ref, w_ref, query_b_ref, value_b_ref, tokens_ref, other_ref,
    x_ref, heads_ref, context_ref, turned_ref, log_ref, values_ref,
):
    join(flags_ref, tokens_ref, other_ref, x_ref)
    biases = (row(query_b_ref), row(value_b_ref))
    attend_units(
        flags_ref, lengths_ref, x_ref, w_ref, biases, heads_ref, context_ref, turned_ref, log_ref, values_ref
    )


def share(flags_ref, total_ref, keep_ref, *send_refs):
    size = keep_ref.shape[0]
    keep_ref[...] = total_ref[piece(flags_ref[1], size), :]
    part = size // len(send_refs)
    for i, send_ref in enumerate(send_refs):
        send_ref[...] = total_ref[piece((1 - flags_ref[1]) * len(send_refs) + i, part), :].astype(BF16)


def attend_last_kernel(
    flags_ref, lengths_ref, w_0, w_1, w_2, w_3, x_ref, before_ref, w_before,
    w_ref, heads_ref, turned_ref, log_ref, bias_ref, keep_ref, send_0, send_1, send_2, send_3,
    values_ref, context_ref, mix_ref,
):
    width = context_ref.shape[1]
    side = flags_ref[0] * 2
    for ref, spot in ((w_0, side), (w_1, side + 1), (w_2, 2 - side), (w_3, 3 - side)):
        w_ref[piece(spot, width), :] = ref[:width, :]
    parts = w_0[width : width + 6, :].astype(F32)
    bias_ref[0:1, :] = parts[0:1] + parts[1:2] + parts[2:3]
    mixed = parts[3:4] + parts[4:5] + parts[5:6]
    biases = (mixed[:, :width], mixed[:, width : 2 * width])
    attend_units(
        flags_ref, lengths_ref, x_ref, w_ref, biases, heads_ref, context_ref, turned_ref, log_ref, values_ref
    )
    for r in range(0, x_ref.shape[0], BLOCK):
        here = slice(r, r + BLOCK)
        mix_ref[here, :] = product(before_ref[here, :], w_before[3 * width :, :]) + product(
            context_ref[here, :], w_ref[3 * width :, :]
        )
    share(flags_ref, mix_ref, keep_ref, send_0, send_1, send_2, send_3)


def strips(rows, step):
    def one(i, carry):
        step(pl.ds(pl.multiple_of(i * STRIP, STRIP), STRIP))
        return carry

    lax.fori_loop(0, rows // STRIP, one, 0, unroll=4)


def norm_one_kernel(
    tokens_ref, keep_ref, got_0, got_1, got_2, got_3, out_b_ref, gain_ref, shift_ref,
    normal_ref, inverse_ref, hidden_0, hidden_1, hidden_2, hidden_3, got_ref, hidden_ref,
):
    part = got_0.shape[0]
    for i, got in enumerate((got_0, got_1, got_2, got_3)):
        got_ref[i * part : (i + 1) * part, :] = got[...]

    def step(here):
        values = tokens_ref[here, :].astype(F32) + keep_ref[here, :] + got_ref[here, :].astype(F32) + row(out_b_ref)
        centered = values - jnp.mean(values, axis=1, keepdims=True)
        inverse = lax.rsqrt(jnp.mean(centered * centered, axis=1, keepdims=True) + EPSILON)
        normal = centered * inverse
        normal_ref[here, :] = normal
        inverse_ref[here, :] = inverse
        hidden_ref[here, :] = (normal * row(gain_ref) + row(shift_ref)).astype(BF16)

    strips(tokens_ref.shape[0], step)
    for i, hidden in enumerate((hidden_0, hidden_1, hidden_2, hidden_3)):
        hidden[...] = hidden_ref[i * part : (i + 1) * part, :]


def feed_units(hidden_ref, up_ref, down_ref, bias, active_ref, slope_ref, sum_ref, before_ref):
    units = up_ref.shape[1]
    for u in range(0, units, BLOCK):
        for r in range(0, hidden_ref.shape[0], 2 * BLOCK):
            here = slice(r, r + 2 * BLOCK)
            pre_up = bias[:, u : u + BLOCK] + product(hidden_ref[here, :], up_ref[:, u : u + BLOCK])
            cumulative, density = normal_parts(pre_up)
            active = (pre_up * cumulative).astype(BF16)
            active_ref[u : u + BLOCK, here] = active.T
            slope_ref[here, u : u + BLOCK] = (cumulative + pre_up * density).astype(BF16)
            now = product(active, down_ref[u : u + BLOCK, :])
            if u:
                sum_ref[here, :] += now
            elif before_ref is not None:
                sum_ref[here, :] = before_ref[here, :] + now
            else:
                sum_ref[here, :] = now


def feed_kernel(flags_ref, *refs):
    own_refs, other_refs, refs = refs[:4], refs[4:8], refs[8:]
    up_ref, down_ref, bias_ref, hidden_ref, turned_ref, active_ref, slope_ref, sum_ref = refs
    join_parts(flags_ref, own_refs, other_refs, hidden_ref)
    turned_ref[...] = hidden_ref[...].T
    feed_units(hidden_ref, up_ref, down_ref, row(bias_ref), active_ref, slope_ref, sum_ref, None)


def feed_last_kernel(
    flags_ref, hidden_ref, up_a, up_b, up_c, down_a, down_b, down_c, bias_ref, before_ref,
    up_ref, down_ref, active_ref, slope_ref, keep_ref, send_ref, sum_ref,
):
    for (direct, *around), out in (((up_a, up_b, up_c), up_ref), ((down_a, down_b, down_c), down_ref)):
        half = direct.shape[0]
        out[piece(flags_ref[0], half), :] = direct[...]
        for i, ref in enumerate(around):
            out[piece((1 - flags_ref[0]) * 2 + i, half // 2), :] = ref[...]
    feed_units(hidden_ref, up_ref, down_ref, bias_ref[0:1, :], active_ref, slope_ref, sum_ref, before_ref)
    share(flags_ref, sum_ref, keep_ref, send_ref)


def norm_two_kernel(
    keep_ref, got_ref, normal_ref, gain_one_ref, shift_one_ref, down_b_ref, gain_ref, shift_ref, cotangent_ref,
    out_ref, grad_ref, low_ref, vector_ref,
):
    vector_ref[...] = jnp.zeros_like(vector_ref)

    def step(here):
        values = keep_ref[here, :] + got_ref[here, :].astype(F32) + row(down_b_ref)
        values = values + (normal_ref[here, :] * row(gain_one_ref) + row(shift_one_ref))
        centered = values - jnp.mean(values, axis=1, keepdims=True)
        inverse = lax.rsqrt(jnp.mean(centered * centered, axis=1, keepdims=True) + EPSILON)
        normal = centered * inverse
        out_ref[here, :] = (normal * row(gain_ref) + row(shift_ref)).astype(BF16)
        upstream = cotangent_ref[here, :].astype(F32)
        scaled = upstream * row(gain_ref)
        first = jnp.mean(scaled, axis=1, keepdims=True)
        second = jnp.mean(scaled * normal, axis=1, keepdims=True)
        grad = inverse * (scaled - first - normal * second)
        grad_ref[here, :] = grad
        low_ref[here, :] = grad.astype(BF16)
        vector_ref[0:1, :] += jnp.sum(upstream * normal, axis=0, keepdims=True)
        vector_ref[1:2, :] += jnp.sum(upstream, axis=0, keepdims=True)
        vector_ref[2:3, :] += jnp.sum(grad, axis=0, keepdims=True)

    strips(keep_ref.shape[0], step)


def quarters(flags_ref, size):
    return [pl.ds(pl.multiple_of(jnp.bitwise_xor(flags_ref[4], i) * size, 16), size) for i in range(4)]


def feed_back_units(
    flags_ref, grad_ref, active_ref, slope_ref, hidden_ref, up_ref, down_ref, before_ref,
    down_grad_ref, bias_grad_ref, sum_ref, turned_ref, grad_pre_ref,
):
    rows, model = grad_ref.shape
    units = slope_ref.shape[1]
    for i, where in enumerate(quarters(flags_ref, units // 4)):
        value = product(active_ref[i * (units // 4) : (i + 1) * (units // 4), :], grad_ref[...])
        down_grad_ref[where, :] = value.astype(BF16)
    for u in range(0, units, BLOCK):
        here = slice(u, u + BLOCK)
        total = 0.0
        for r in range(0, rows, 2 * BLOCK):
            grad_active = cols_product(grad_ref[r : r + 2 * BLOCK, :], down_ref[here, :])
            grad_pre = (slope_ref[r : r + 2 * BLOCK, here].astype(F32) * grad_active).astype(BF16)
            grad_pre_ref[r : r + 2 * BLOCK, here] = grad_pre
            total = total + jnp.sum(grad_pre.astype(F32), axis=0, keepdims=True)
            bias_grad_ref[:, here] = jnp.concatenate([total, jnp.zeros((7, total.shape[1]), F32)], axis=0)
    for i, where in enumerate(quarters(flags_ref, model // 4)):
        value = product(hidden_ref[i * (model // 4) : (i + 1) * (model // 4), :], grad_pre_ref[...])
        turned_ref[where, :] = value.astype(BF16)
    for r in range(0, rows, BLOCK):
        value = cols_product(grad_pre_ref[r : r + BLOCK, :], up_ref[...])
        if before_ref is not None:
            value = value + before_ref[r : r + BLOCK, :]
        sum_ref[r : r + BLOCK, :] = value


def split(turned_ref, keep_ref, send_ref):
    quarter = turned_ref.shape[0] // 4
    for i in range(2):
        there = slice(i * quarter, (i + 1) * quarter)
        keep_ref[there, :] = turned_ref[2 * i * quarter : (2 * i + 1) * quarter, :]
        send_ref[there, :] = turned_ref[(2 * i + 1) * quarter : (2 * i + 2) * quarter, :]


def feed_back_theirs_kernel(
    flags_ref, own_ref, other_ref, active_ref, slope_ref, hidden_ref, up_ref, down_ref,
    grad_ref, down_grad_ref, keep_up, send_up, bias_grad_ref, sum_ref, turned_ref, grad_pre_ref,
):
    join(flags_ref, own_ref, other_ref, grad_ref)
    feed_back_units(
        flags_ref, grad_ref, active_ref, slope_ref, hidden_ref, up_ref, down_ref, None,
        down_grad_ref, bias_grad_ref, sum_ref, turned_ref, grad_pre_ref,
    )
    split(turned_ref, keep_up, send_up)


def feed_back_mine_kernel(
    flags_ref, grad_ref, active_ref, slope_ref, hidden_ref, up_ref, down_ref, before_ref,
    grad_two_ref, down_grad_ref, keep_up, send_up, bias_grad_ref, keep_ref, send_0, send_1, send_2, send_3, sum_ref, turned_ref, grad_pre_ref,
):
    feed_back_units(
        flags_ref, grad_ref, active_ref, slope_ref, hidden_ref, up_ref, down_ref, before_ref,
        down_grad_ref, bias_grad_ref, sum_ref, turned_ref, grad_pre_ref,
    )
    split(turned_ref, keep_up, send_up)
    share(flags_ref, sum_ref, keep_ref, send_0, send_1, send_2, send_3)
    keep_ref[...] += grad_two_ref[...]


def norm_one_back_kernel(
    keep_ref, got_0, got_1, got_2, got_3, normal_ref, inverse_ref, gain_ref, two_ref,
    grad_ref, low_a, low_b, got_ref, low_ref, vector_ref,
):
    vector_ref[...] = jnp.zeros_like(vector_ref)
    part, half = got_0.shape[0], low_a.shape[0]
    for i, got in enumerate((got_0, got_1, got_2, got_3)):
        got_ref[i * part : (i + 1) * part, :] = got[...]

    def step(here):
        upstream, normal = keep_ref[here, :] + got_ref[here, :].astype(F32), normal_ref[here, :]
        scaled = upstream * row(gain_ref)
        first = jnp.mean(scaled, axis=1, keepdims=True)
        second = jnp.mean(scaled * normal, axis=1, keepdims=True)
        grad = inverse_ref[here, :] * (scaled - first - normal * second)
        grad_ref[here, :] = grad
        low_ref[here, :] = grad.astype(BF16)
        vector_ref[0:1, :] += jnp.sum(grad, axis=0, keepdims=True)
        vector_ref[1:2, :] += jnp.sum(upstream * normal, axis=0, keepdims=True)
        vector_ref[2:3, :] += jnp.sum(upstream, axis=0, keepdims=True)

    strips(keep_ref.shape[0], step)
    vector_ref[3:6, :] = two_ref[0:3, :]
    low_a[...] = low_ref[:half, :]
    low_b[:half, :] = low_ref[half:, :]
    low_b[half : half + 8, :] = vector_ref[...].astype(BF16)
    low_b[half + 8 :, :] = jnp.zeros((low_b.shape[0] - half - 8, low_b.shape[1]), BF16)


def attend_back_kernel(
    flags_ref, own_a, own_b, other_a, other_b, up_sum_ref,
    x_ref, heads_ref, context_ref, log_ref, w_ref, out_ref, plain_ref,
    grad_ref, grad_heads_ref, inner_ref, turned_ref, keys_ref, values_ref,
):
    rows, model = x_ref.shape
    width = context_ref.shape[0]
    heads = width // HEAD_DIM
    size = width + BIAS_ROWS
    half = own_a.shape[0]
    join_parts(flags_ref, (own_a, own_b), (other_a, other_b), grad_ref)
    blank = jnp.zeros((2 * BLOCK, LANES - HEAD_DIM), BF16)
    for r in range(0, rows, 2 * BLOCK):
        here = slice(r, r + 2 * BLOCK)
        low = cols_product(grad_ref[here, :], w_ref[3 * width :, :]).astype(BF16)
        turned = low.T.astype(F32) * context_ref[:, here]
        for h in range(heads):
            part = slice(h * HEAD_DIM, (h + 1) * HEAD_DIM)
            grad_heads_ref[h, here, :] = jnp.concatenate([low[:, part], blank], axis=1)
            inner_ref[h : h + 1, here] = jnp.sum(turned[part, :], axis=0, keepdims=True)
    keys_ref[...] = jnp.zeros_like(keys_ref)
    values_ref[...] = jnp.zeros_like(values_ref)
    for i in range(rows // BLOCK):
        here, seen = slice(i * BLOCK, (i + 1) * BLOCK), window(i, rows)
        for h in range(heads):
            queries, grads, key_rows = heads_ref[h, here, :], grad_heads_ref[h, here, :], heads_ref[heads + h, seen, :]
            probs = jnp.exp(cols_product(key_rows, queries) - log_ref[h : h + 1, here])
            grad_probs = cols_product(heads_ref[2 * heads + h, seen, :], grads)
            grad_scores = (probs * (grad_probs - inner_ref[h : h + 1, here])).astype(BF16)
            values_ref[h, seen, :] += product(probs.astype(BF16), grads)
            keys_ref[h, seen, :] += product(grad_scores, queries)
            grad_queries = rows_product(key_rows, grad_scores)[:HEAD_DIM, :] * (HEAD_DIM**-0.5)
            turned_ref[h * HEAD_DIM : (h + 1) * HEAD_DIM, here] = grad_queries.astype(BF16)
    for i, ref in ((1, keys_ref), (2, values_ref)):
        for h in range(heads):
            first = i * width + h * HEAD_DIM
            turned_ref[first : first + HEAD_DIM, :] = ref[h].T[:HEAD_DIM, :].astype(BF16)
    for i in range(3):
        plain_ref[:, i * 2 * LANES : i * 2 * LANES + width] = turned_ref[i * width : (i + 1) * width, :].T
    tops = [jnp.zeros((8, model), F32)] * 4
    for i in (0, 2):
        top = jnp.sum(plain_ref[:, i * 2 * LANES : i * 2 * LANES + width].astype(F32), axis=0, keepdims=True)
        top = jnp.concatenate([top, jnp.zeros((1, model - width), F32)], axis=1)
        tops[i] = jnp.concatenate([top, jnp.zeros((7, model), F32)], axis=0)
    tops[1] = up_sum_ref[...]
    tops[3] = own_b[half : half + 8, :].astype(F32) + other_b[half : half + 8, :].astype(F32)
    for i, here in enumerate(quarters(flags_ref, size)):
        if i < 3:
            grad = product(turned_ref[i * width : (i + 1) * width, :], x_ref[...])
        else:
            grad = product(context_ref[...].astype(BF16), grad_ref[...])
        blank = jnp.zeros((BIAS_ROWS - 8, model), F32)
        out_ref[here, :] = jnp.concatenate([grad, tops[i], blank], axis=0).astype(BF16)


def tokens_kernel(flags_ref, grad_ref, plain_0, plain_2, w_0, w_2, keep_ref, send_ref, sum_ref):
    rows, model = plain_0.shape[0], grad_ref.shape[1]
    width = w_0.shape[0] // 4
    for r in range(0, rows, BLOCK):
        total = 0.0
        for plain, w_ref in ((plain_0, w_0), (plain_2, w_2)):
            for i in range(3):
                total = total + product(
                    plain[r : r + BLOCK, i * 2 * LANES : i * 2 * LANES + width], w_ref[i * width : (i + 1) * width, :]
                )
        sum_ref[r : r + BLOCK, :] = total
    share(flags_ref, sum_ref, keep_ref, send_ref)
    keep_ref[...] += grad_ref[...]


def last_kernel(keep_ref, got_ref, out_ref):
    out_ref[...] = keep_ref[...] + got_ref[...].astype(F32)


def unpack_kernel(
    flags_ref, part_0, part_1, part_2, part_3,
    query_ref, key_ref, value_ref, out_w_ref, query_b_ref, value_b_ref, up_b_ref, *refs,
):
    vector_refs, parts = refs[:-1], refs[-1]
    for i, ref in enumerate((part_0, part_1, part_2, part_3)):
        parts[jnp.bitwise_xor(flags_ref[4], i)] = ref[...]
    width = query_ref.shape[0]
    for i, ref in enumerate((query_ref, key_ref, value_ref, out_w_ref)):
        ref[...] = parts[i, :width, :].astype(F32)
    tops = [parts[i, width : width + BIAS_ROWS, :].astype(F32) for i in range(4)]
    query_b_ref[...] = tops[0][0, :width]
    value_b_ref[...] = tops[2][0, :width]
    up_b_ref[...] = tops[1][0, :]
    for i, ref in enumerate(vector_refs):
        ref[...] = tops[3][i, :]


def tie(*arrays):
    return lax.optimization_barrier(arrays)


def add(*members):
    members = [m.astype(F32) for m in members]
    while len(members) > 1:
        members = [a + b for a, b in zip(members[::2], members[1::2])]
    return members[0].astype(BF16)


class Swaps:
    def __init__(self, dp_size, replica):
        self.dp_size, self.near = dp_size, replica & 3

    def core(self, values_in):
        return lax.ppermute(values_in, "tensor", [(i, i ^ 1) for i in range(4)])

    def chip(self, values_in):
        return lax.ppermute(values_in, "tensor", [(i, i ^ 2) for i in range(4)])

    def replica(self, values_in, mask):
        return lax.ppermute(values_in, "dp", [(i, i ^ mask) for i in range(self.dp_size)])

    def scatter(self, parts):
        return [self.replica(parts[m], m) for m in (1, 2, 3)]

    def far(self, value, mask):
        return self.replica(value, mask)

    def gather(self, value):
        return [self.replica(value, m) for m in (1, 2, 3)]

    @property
    def far_masks(self):
        return [1 << b for b in range(2, self.dp_size.bit_length() - 1)]

    def placed(self, members):
        return [lax.select_n(self.near, *[members[i ^ p] for p in range(4)]) for i in range(4)]


def cut_pair(value):
    half = value.shape[0] // 2
    return [value[:half], value[half:]]


def cut(value):
    size = value.shape[0] // 4
    return [value[i * size : (i + 1) * size] for i in range(4)]


def first_calls(
    flags, query_bias, value_bias, up_bias, query_weight, key_weight, value_weight, out_weight, up_weight, down_weight,
):
    model, width = query_weight.shape
    far, vmem = pl.BlockSpec(memory_space=pl.ANY), pl.BlockSpec(memory_space=pltpu.VMEM)
    smem = pl.BlockSpec(memory_space=pltpu.SMEM)
    params = dict(
        compiler_params=pltpu.CompilerParams(vmem_limit_bytes=PACK_LIMIT),
        cost_estimate=pl.CostEstimate(flops=0, bytes_accessed=0, transcendentals=0),
    )
    weights = (query_weight.T, key_weight.T, value_weight.T, out_weight)
    shapes = [(width + BIAS_ROWS, model), (width, model)]
    pieces = pl.pallas_call(
        pieces_kernel,
        in_specs=[smem] + [vmem] * 3 + [far] * 4,
        out_specs=[far] * 2,
        out_shape=[jax.ShapeDtypeStruct(s, BF16) for s in shapes],
        scratch_shapes=[pltpu.VMEM(s, BF16) for s in shapes] + [pltpu.SemaphoreType.DMA((4,))],
        **params,
    )(flags, query_bias, value_bias, up_bias, *weights)
    pieces, weights = tie(pieces, weights)
    halves = [(w.shape[0] // 2, w.shape[1]) for w in (up_weight, down_weight)]
    outs = [(4 * width, model)] + halves
    rest = pl.pallas_call(
        pack_kernel,
        in_specs=[smem] + [far] * 6,
        out_specs=[far] * 3,
        out_shape=[jax.ShapeDtypeStruct(s, BF16) for s in outs],
        scratch_shapes=[pltpu.VMEM(s, BF16) for s in outs] + [pltpu.SemaphoreType.DMA((9,))],
        **params,
    )(flags, *weights, up_weight, down_weight)
    return [*pieces, *rest]


def body(
    dp_size,
    tokens,
    lengths,
    cotangent,
    query_weight,
    query_bias,
    key_weight,
    value_weight,
    value_bias,
    out_weight,
    out_bias,
    gain_one,
    shift_one,
    up_weight,
    up_bias,
    down_weight,
    down_bias,
    gain_two,
    shift_two,
):
    own, model = tokens.shape
    width = query_weight.shape[1]
    units = up_weight.shape[1]
    rows = 2 * own
    place = lax.axis_index("tensor")
    replica = lax.axis_index("dp")
    flags = [(replica ^ (replica >> 1)) & 1, place % 2, place // 2, place, replica & 3, (replica >> 1) & 1, replica & 1]
    flags = jnp.stack(flags).astype(jnp.int32)
    swaps = Swaps(dp_size, replica)
    swap_core, swap_chip, swap_replica = swaps.core, swaps.chip, swaps.replica
    far_masks = swaps.far_masks

    other_tokens = swap_core(tokens)
    pack_a, pack_b, pack, up_half, down_half = first_calls(
        flags, query_bias, value_bias, up_bias, query_weight, key_weight, value_weight, out_weight, up_weight, down_weight
    )
    whole, half_row = (4 * (width + BIAS_ROWS), model), (own, model)
    halves, fourths = [((own // 2, model), BF16)] * 2, [((own // 4, model), BF16)] * 4
    heads_shape = ((3 * width // HEAD_DIM, rows, LANES), BF16)
    values_scratch = pltpu.VMEM((width, rows), BF16)
    kept_shapes = [((width, rows), F32), ((8, rows), F32)]
    direct = [swap_chip(pack_a), swap_chip(pack_b)]
    up_direct, down_direct = swap_chip(up_half), swap_chip(down_half)

    inputs, qkv_0, context_0, turned_0, log_0 = call(
        attend_kernel,
        [((rows, model), BF16), heads_shape, ((rows, width), BF16)] + kept_shapes,
        (flags, lengths, pack, query_bias, value_bias, tokens, other_tokens),
        scalars=2,
        scratch=[values_scratch],
    )
    *direct, inputs = tie(*direct, inputs)
    around = [swap_replica(direct[0], 1), swap_replica(direct[1], 2)]
    *around, inputs = tie(*around, inputs)
    pack_2, qkv_2, turned_2, log_2, bias_2, keep, *sends = call(
        attend_last_kernel,
        [((4 * width, model), BF16), heads_shape] + kept_shapes + [((8, model), F32), (half_row, F32)] + fourths,
        (flags, lengths, *direct, *around, inputs, context_0, pack),
        scalars=2,
        scratch=[values_scratch, pltpu.VMEM((rows, width), BF16), pltpu.VMEM((rows, model), F32)],
    )
    *sends, up_direct = tie(*sends, up_direct)
    got = [swap_core(v) for v in sends]
    fourth = model // 4
    up_around = [swap_replica(up_direct[:fourth], 1), swap_replica(up_direct[fourth:], 2)]
    normal_one, inverse_one, *hidden = call(
        norm_one_kernel,
        [(half_row, F32), ((own, 1), F32)] + fourths,
        (tokens, keep, *got, out_bias, gain_one, shift_one),
        scratch=[pltpu.VMEM(half_row, BF16)] * 2,
    )
    other_hidden = [swap_core(v) for v in hidden]
    hidden[0], down_direct, *held = tie(hidden[0], down_direct, *other_hidden, *up_around)
    other_hidden, up_around = held[:4], held[4:]
    fourth = units // 4
    down_around = [swap_replica(down_direct[:fourth], 1), swap_replica(down_direct[fourth:], 2)]

    act_shapes = [((units, rows), BF16), ((rows, units), BF16)]
    hidden_full, hidden_turned, active_0, slope_0, before = call(
        feed_kernel,
        [((rows, model), BF16), ((model, rows), BF16)] + act_shapes + [((rows, model), F32)],
        (flags, *hidden, *other_hidden, up_weight, down_weight, up_bias),
        scalars=1,
    )
    before, *down_around = tie(before, *down_around)
    up_2, down_2, active_2, slope_2, keep, send = call(
        feed_last_kernel,
        [((model, units), BF16), ((units, model), BF16)] + act_shapes + [(half_row, F32), (half_row, BF16)],
        (flags, hidden_full, up_direct, *up_around, down_direct, *down_around, bias_2, before),
        scalars=1,
        scratch=[pltpu.VMEM((rows, model), F32)],
    )
    layer_output, grad_two, low_grad_two, vector_two = call(
        norm_two_kernel,
        [(half_row, BF16), (half_row, F32), (half_row, BF16), ((8, model), F32)],
        (
            keep, swap_core(send), normal_one, gain_one, shift_one, down_bias,
            gain_two, shift_two, cotangent,
        ),
    )

    back_scratch = [pltpu.VMEM((model, units), BF16), pltpu.VMEM((rows, units), BF16)]
    grad_full, down_theirs, up_keep_2, up_send_2, up_sum_2, running = call(
        feed_back_theirs_kernel,
        [((rows, model), BF16), ((units, model), BF16)] + [((model // 2, units), BF16)] * 2
        + [((8, units), F32), ((rows, model), F32)],
        (flags, low_grad_two, swap_core(low_grad_two), active_2, slope_2, hidden_turned, up_2, down_2),
        scalars=1,
        scratch=back_scratch,
    )
    down_theirs, running = tie(down_theirs, running)
    down_chip = swap_chip(down_theirs)
    down_mine, up_keep_0, up_send, up_sum_0, keep, send_0, send_1, send_2, send_3 = call(
        feed_back_mine_kernel,
        [((units, model), BF16)] + [((model // 2, units), BF16)] * 2 + [((8, units), F32), (half_row, F32)]
        + [((own // 4, model), BF16)] * 4,
        (
            flags, grad_full, active_0, slope_0, hidden_turned, up_weight, down_weight, running, grad_two,
        ),
        scalars=1,
        scratch=[pltpu.VMEM((rows, model), F32)] + back_scratch,
    )
    up_got = [swap_replica(up_send, 1), swap_replica(up_send_2, 1)]
    got = [swap_core(v) for v in (send_0, send_1, send_2, send_3)]
    grad_one, low_a, low_b = call(
        norm_one_back_kernel,
        [(half_row, F32), halves[0], ((own // 2 + BIAS_ROWS, model), BF16)],
        (keep, *got, normal_one, inverse_one, gain_one, vector_two),
        scratch=[pltpu.VMEM(half_row, BF16)] * 2 + [pltpu.VMEM((8, model), F32)],
    )
    low_other = [swap_core(low_a), swap_core(low_b)]


    def attend_back(low_a, qkv, turned, log_total, shard, up_sum):
        return call(
            attend_back_kernel,
            [(whole, BF16), ((rows, 6 * LANES), BF16)],
            (
                flags, low_a, low_b, *low_other, up_sum,
                inputs, qkv, turned, log_total, shard,
            ),
            scalars=1,
            scratch=[
                pltpu.VMEM((rows, model), BF16), pltpu.VMEM((width // HEAD_DIM, rows, LANES), BF16),
                pltpu.VMEM((8, rows), F32), pltpu.VMEM((3 * width, rows), BF16),
                pltpu.VMEM((width // HEAD_DIM, rows, LANES), F32), pltpu.VMEM((width // HEAD_DIM, rows, LANES), F32),
            ],
        )

    pack_theirs, plain_2 = attend_back(low_a, qkv_2, turned_2, log_2, pack_2, up_sum_2)
    pack_theirs, low_a = tie(pack_theirs, low_a)
    pack_chip = swap_chip(pack_theirs)
    pack_mine, plain_0 = attend_back(low_a, qkv_0, turned_0, log_0, pack, up_sum_0)
    keep, send = call(
        tokens_kernel,
        [(half_row, F32), (half_row, BF16)],
        (flags, grad_one, plain_0, plain_2, pack, pack_2),
        scalars=1,
        scratch=[pltpu.VMEM((rows, model), F32)],
    )
    pack_mine, keep, send, down_chip = tie(pack_mine, keep, send, down_chip)

    down_parts = [add(m, t) for m, t in zip(cut(down_mine), cut(down_chip))]
    down_parts = tie(*down_parts)
    down_got = swaps.scatter(down_parts)
    *down_got, up_got[0], up_got[1] = tie(*down_got, *up_got)
    down_now = add(down_parts[0], *down_got)
    up_mine, up_theirs = add(up_keep_0, up_got[0]), add(up_keep_2, up_got[1])
    down_now, up_mine, up_theirs = tie(down_now, up_mine, up_theirs)
    down_far, up_chip = swaps.far(down_now, far_masks[0]), swap_chip(up_theirs)
    pack_chip, pack_mine = tie(pack_chip, pack_mine)
    pack_parts = [add(m, t) for m, t in zip(cut(pack_mine), cut(pack_chip))]
    pack_parts = tie(*pack_parts)
    pack_got = swaps.scatter(pack_parts)
    *pack_got, up_chip, down_far = tie(*pack_got, up_chip, down_far)
    pack_now = add(pack_parts[0], *pack_got)
    up_now, up_next = [add(m, t) for m, t in zip(cut_pair(up_mine), cut_pair(up_chip))]
    down_now = add(down_now, down_far)
    for mask in far_masks[1:]:
        down_now = add(down_now, swaps.far(down_now, mask))
    pack_now, up_now, up_next, down_now, send = tie(pack_now, up_now, up_next, down_now, send)
    pack_far = swaps.far(pack_now, far_masks[0])
    up_got = swap_replica(up_next, 2)
    down_pair = jnp.concatenate([down_now, swap_replica(down_now, 2)], axis=0)
    got = swap_core(send)
    (down_pair,) = tie(down_pair)
    down_other = swap_replica(down_pair, 1)
    pack_far, up_got, got = tie(pack_far, up_got, got)
    pack_now, up_now = add(pack_now, pack_far), add(up_now, up_got)
    for mask in far_masks[1:]:
        pack_now = add(pack_now, swaps.far(pack_now, mask))
    pack_now, up_now = tie(pack_now, up_now)
    pack_all = [pack_now] + swaps.gather(pack_now)
    up_far = swaps.far(up_now, far_masks[0])
    (tokens_grad,) = call(last_kernel, [(half_row, F32)], (keep, got))
    up_far, tokens_grad, down_other = tie(up_far, tokens_grad, down_other)
    up_now = add(up_now, up_far)
    for mask in far_masks[1:]:
        up_now = add(up_now, swaps.far(up_now, mask))
    (up_now,) = tie(up_now)
    up_all = [up_now] + swaps.gather(up_now)
    first, second = cut_pair(down_pair), cut_pair(down_other)
    down_all = [first[0], second[0], first[1], second[1]]
    down_weight_grad = jnp.concatenate(swaps.placed(down_all), axis=0).astype(F32)
    up_weight_grad = jnp.concatenate(swaps.placed(up_all), axis=0).astype(F32)
    shard = [((width, model), F32)] * 4 + [((width,), F32)] * 2 + [((units,), F32)] + [((model,), F32)] * 6
    (
        query_grad, key_grad, value_grad, out_grad, query_bias_grad, value_bias_grad, up_bias_row, *vectors,
    ) = call(
        unpack_kernel, shard, (flags, *pack_all), scalars=1, scratch=[pltpu.VMEM((4, width + BIAS_ROWS, model), BF16)]
    )
    return (
        layer_output,
        tokens_grad,
        query_grad.T,
        query_bias_grad,
        key_grad.T,
        value_grad.T,
        value_bias_grad,
        out_grad,
        vectors[0],
        vectors[1],
        vectors[2],
        up_weight_grad,
        up_bias_row,
        down_weight_grad,
        vectors[5],
        vectors[3],
        vectors[4],
    )


def solution(mesh):
    placed = (
        P(("dp", "tensor"), None),
        P("dp", None),
        P(("dp", "tensor"), None),
        P(None, "tensor"),
        P("tensor"),
        P(None, "tensor"),
        P(None, "tensor"),
        P("tensor"),
        P("tensor", None),
        P(),
        P(),
        P(),
        P(None, "tensor"),
        P("tensor"),
        P("tensor", None),
        P(),
        P(),
        P(),
    )
    return jax.shard_map(
        functools.partial(body, mesh.shape["dp"]),
        mesh=mesh,
        in_specs=placed,
        out_specs=(
            P(("dp", "tensor"), None),
            P(("dp", "tensor"), None),
            P(None, "tensor"),
            P("tensor"),
            P(None, "tensor"),
            P(None, "tensor"),
            P("tensor"),
            P("tensor", None),
            P(),
            P(),
            P(),
            P(None, "tensor"),
            P("tensor"),
            P("tensor", None),
            P(),
            P(),
            P(),
        ),
        check_vma=False,
    )
```

```python
import functools

import jax
import jax.numpy as jnp
from jax import lax
from jax.experimental import pallas as pl
from jax.experimental.pallas import tpu as pltpu
from jax.sharding import PartitionSpec as P

HEAD_DIM = 64
MOST = 256
EPSILON = 1e-05
MASKED = -1e30
BLOCK = 256
STRIP = 64
LANES = 128
BIAS_ROWS = 16
VMEM_LIMIT = 16 * 1024 * 1024
PACK_LIMIT = 60 * 1024 * 1024
TAIL_SCALE = 0.425
TAIL = (
    0.23966740682492862,
    0.24201181237516,
    0.19964184258583956,
    0.2585875675603689,
    -0.10985333090134082,
    0.4147788772153898,
    -0.3173079260911745,
    0.07247363954140279,
)

BF16 = jnp.bfloat16
F32 = jnp.float32


def product(left_side, right_side):
    return jnp.dot(left_side, right_side, preferred_element_type=F32)


def rows_product(left_side, right_side):
    return lax.dot_general(
        left_side, right_side, (((0,), (0,)), ((), ())), preferred_element_type=F32
    )


def cols_product(left_side, right_side):
    return lax.dot_general(
        left_side, right_side, (((1,), (1,)), ((), ())), preferred_element_type=F32
    )


def normal_parts(z):
    size = jnp.abs(z)
    t = 1.0 / (1.0 + (TAIL_SCALE * 0.7071067811865476) * size)
    series = TAIL[-1]
    for factor in TAIL[-2::-1]:
        series = series * t + factor
    bell = jnp.exp(-0.5 * z * z)
    tail = (0.5 * bell) * (series * t)
    return jnp.where(z >= 0.0, 1.0 - tail, tail), bell * 0.3989422804014327


def call(kernel, outs, args, scalars=0, scratch=(), cost=1.0, far=()):
    specs = [pl.BlockSpec(memory_space=pltpu.SMEM)] * scalars
    specs += [pl.BlockSpec(memory_space=pltpu.VMEM)] * (len(args) + len(outs) - scalars)
    for i in far:
        specs[i] = pl.BlockSpec(memory_space=pl.ANY)
    outputs = pl.pallas_call(
        kernel,
        in_specs=specs[: len(args)],
        out_specs=specs[len(args) :],
        out_shape=[jax.ShapeDtypeStruct(shape, dtype) for shape, dtype in outs],
        scratch_shapes=list(scratch),
        compiler_params=pltpu.CompilerParams(vmem_limit_bytes=VMEM_LIMIT),
        cost_estimate=pl.CostEstimate(
            flops=0, bytes_accessed=0, transcendentals=0
        ),
    )(*args)
    return list(outputs)


def piece(index, size):
    return pl.ds(pl.multiple_of(index * size, 16), size)


def assemble(side, refs, out_ref):
    size, count = refs[0].shape[0], len(refs) // 2
    for i, ref in enumerate(refs):
        first = side if i < count else 1 - side
        out_ref[piece(first * count + i % count, size), :] = ref[...]


def row(ref):
    return ref[...].reshape(1, -1)


def join_parts(flags_ref, own_refs, other_refs, out_ref):
    for side, parts in ((flags_ref[1], own_refs), (1 - flags_ref[1], other_refs)):
        for i, part in enumerate(parts):
            size = out_ref.shape[0] // (2 * len(parts))
            out_ref[piece(side * len(parts) + i, size), :] = part[:size, :]


def join(flags_ref, own_ref, other_ref, out_ref):
    size = own_ref.shape[0]
    out_ref[piece(flags_ref[1], size), :] = own_ref[...]
    out_ref[piece(1 - flags_ref[1], size), :] = other_ref[...]


def pieces_kernel(
    flags_ref, query_b_ref, value_b_ref, up_b_ref, query_ref, key_ref, value_ref, out_w_ref, near_a, near_b, sems,
):
    weights = (query_ref, key_ref, value_ref, out_w_ref)
    width, model = query_ref.shape
    for side in range(2):

        @pl.when(flags_ref[0] == side)
        def load():
            for k, near in enumerate((near_a, near_b)):
                pltpu.make_async_copy(weights[2 * side + k], near.at[:width], sems.at[k]).start()

    blank = jnp.zeros((1, model - 2 * width), F32)
    rows = []
    for part in (row(up_b_ref), jnp.concatenate([row(query_b_ref), row(value_b_ref), blank], axis=1)):
        for _ in range(3):
            rows.append(part.astype(BF16).astype(F32))
            part = part - rows[-1]
    rows.append(jnp.zeros((BIAS_ROWS - 6, model), F32))
    near_a[width:, :] = jnp.concatenate(rows, axis=0).astype(BF16)
    for k, near in enumerate((near_a, near_b)):
        pltpu.make_async_copy(weights[k], near.at[:width], sems.at[k]).wait()


def pack_kernel(
    flags_ref, query_ref, key_ref, value_ref, out_w_ref, up_ref, down_ref,
    pack_ref, up_out, down_out, pack_near, up_near, down_near, sems,
):
    width = query_ref.shape[0]
    half = up_out.shape[0]
    loads = [(ref.at[piece(flags_ref[0], half)], near) for ref, near in ((up_ref, up_near), (down_ref, down_near))]
    weights = (query_ref, key_ref, value_ref, out_w_ref)
    loads += [(s, pack_near.at[i * width : (i + 1) * width]) for i, s in enumerate(weights)]
    copies = [pltpu.make_async_copy(a, b, sems.at[i]) for i, (a, b) in enumerate(loads)]
    for copy in copies:
        copy.start()
    for copy in copies:
        copy.wait()
    stores = ((up_near, up_out), (down_near, down_out), (pack_near, pack_ref))
    copies = [pltpu.make_async_copy(a, b, sems.at[6 + i]) for i, (a, b) in enumerate(stores)]
    for copy in copies:
        copy.start()
    for copy in copies:
        copy.wait()


def document_lanes(flags_ref, lengths_ref, rows):
    shape = (rows, LANES - HEAD_DIM)
    spot = lax.broadcasted_iota(jnp.int32, shape, 0)
    lane = lax.broadcasted_iota(jnp.int32, (1, shape[1]), 1)
    ends = 0
    begin_row, end_row = jnp.zeros_like(lane), jnp.zeros_like(lane)
    documents = lengths_ref.shape[1]
    for d in range(documents):
        begin_row = jnp.where(lane == d, ends, begin_row)
        ends = ends + lengths_ref[flags_ref[2], d]
        end_row = jnp.where(lane == d, ends, end_row)
    inside = (spot >= begin_row) & (spot < end_row)
    outside = jnp.where(lane < documents, MASKED, 0.0)
    return jnp.where(inside, 1.0, 0.0).astype(BF16), jnp.where(inside, 0.0, outside).astype(BF16)


def window(i, rows):
    return slice(max(i - 1, 0) * BLOCK, min(i + 2, rows // BLOCK) * BLOCK)


def attend_units(
    flags_ref, lengths_ref, x_ref, w_ref, biases, heads_ref, context_ref, turned_ref, log_ref, values_ref,
):
    rows, model = x_ref.shape
    width = context_ref.shape[1]
    heads = width // HEAD_DIM
    same, other = document_lanes(flags_ref, lengths_ref, rows)
    tails = (other, same, jnp.zeros_like(same))
    for i, bias in enumerate((biases[0], None, biases[1])):
        weights = w_ref[i * width : (i + 1) * width, :]
        for r in range(0, rows, 2 * BLOCK):
            here = slice(r, r + 2 * BLOCK)
            total = cols_product(x_ref[here, :], weights)
            if bias is not None:
                total = total + bias
            low = total.astype(BF16)
            if i == 0:
                low = low * BF16(HEAD_DIM**-0.5)
            for h in range(heads):
                part = low[:, h * HEAD_DIM : (h + 1) * HEAD_DIM]
                heads_ref[i * heads + h, here, :] = jnp.concatenate([part, tails[i][here, :]], axis=1)
            if i == 2:
                values_ref[:, here] = low.T
    for i in range(rows // BLOCK):
        here, seen = slice(i * BLOCK, (i + 1) * BLOCK), window(i, rows)
        for h in range(heads):
            part = slice(h * HEAD_DIM, (h + 1) * HEAD_DIM)
            queries = heads_ref[h, here, :]
            steps = range(seen.start, seen.stop, BLOCK)
            scores = [cols_product(heads_ref[heads + h, r : r + BLOCK, :], queries) for r in steps]
            top = functools.reduce(jnp.maximum, [jnp.max(s, axis=0, keepdims=True) for s in scores])
            total, context = 0.0, 0.0
            for r, score in zip(steps, scores):
                weights = jnp.exp(score - top)
                total = total + jnp.sum(weights, axis=0, keepdims=True)
                context = context + product(values_ref[part, r : r + BLOCK], weights.astype(BF16))
            turned_ref[part, here] = context * (1.0 / total)
            log_ref[h : h + 1, here] = top + jnp.log(total)
        context_ref[here, :] = turned_ref[:, here].T.astype(BF16)


def attend_kernel(
    flags_ref, lengths_ref, w_ref, query_b_ref, value_b_ref, tokens_ref, other_ref,
    x_ref, heads_ref, context_ref, turned_ref, log_ref, values_ref,
):
    join(flags_ref, tokens_ref, other_ref, x_ref)
    biases = (row(query_b_ref), row(value_b_ref))
    attend_units(
        flags_ref, lengths_ref, x_ref, w_ref, biases, heads_ref, context_ref, turned_ref, log_ref, values_ref
    )


def share(flags_ref, total_ref, keep_ref, *send_refs):
    size = keep_ref.shape[0]
    keep_ref[...] = total_ref[piece(flags_ref[1], size), :]
    part = size // len(send_refs)
    for i, send_ref in enumerate(send_refs):
        send_ref[...] = total_ref[piece((1 - flags_ref[1]) * len(send_refs) + i, part), :].astype(BF16)


def attend_last_kernel(
    flags_ref, lengths_ref, w_0, w_1, w_2, w_3, x_ref, before_ref, w_before,
    w_ref, heads_ref, turned_ref, log_ref, bias_ref, keep_ref, send_0, send_1, send_2, send_3,
    values_ref, context_ref, mix_ref,
):
    width = context_ref.shape[1]
    side = flags_ref[0] * 2
    for ref, spot in ((w_0, side), (w_1, side + 1), (w_2, 2 - side), (w_3, 3 - side)):
        w_ref[piece(spot, width), :] = ref[:width, :]
    parts = w_0[width : width + 6, :].astype(F32)
    bias_ref[0:1, :] = parts[0:1] + parts[1:2] + parts[2:3]
    mixed = parts[3:4] + parts[4:5] + parts[5:6]
    biases = (mixed[:, :width], mixed[:, width : 2 * width])
    attend_units(
        flags_ref, lengths_ref, x_ref, w_ref, biases, heads_ref, context_ref, turned_ref, log_ref, values_ref
    )
    for r in range(0, x_ref.shape[0], BLOCK):
        here = slice(r, r + BLOCK)
        mix_ref[here, :] = product(before_ref[here, :], w_before[3 * width :, :]) + product(
            context_ref[here, :], w_ref[3 * width :, :]
        )
    share(flags_ref, mix_ref, keep_ref, send_0, send_1, send_2, send_3)


def strips(rows, step, sums=0, model=0):
    def one(i, carry):
        found = step(pl.ds(pl.multiple_of(i * STRIP, STRIP), STRIP))
        if not sums:
            return carry
        return tuple(c + jnp.sum(f.reshape(STRIP // 8, 8, model), axis=0) for c, f in zip(carry, found))

    first = tuple(jnp.zeros((8, model), F32) for _ in range(sums))
    total = lax.fori_loop(0, rows // STRIP, one, first if sums else 0, unroll=4)
    return [jnp.sum(t, axis=0, keepdims=True) for t in total] if sums else None


def norm_one_kernel(
    tokens_ref, keep_ref, got_0, got_1, got_2, got_3, out_b_ref, gain_ref, shift_ref,
    normal_ref, inverse_ref, hidden_0, hidden_1, hidden_2, hidden_3, got_ref, hidden_ref,
):
    part = got_0.shape[0]
    for i, got in enumerate((got_0, got_1, got_2, got_3)):
        got_ref[i * part : (i + 1) * part, :] = got[...]

    def step(here):
        values = tokens_ref[here, :].astype(F32) + keep_ref[here, :] + got_ref[here, :].astype(F32) + row(out_b_ref)
        centered = values - jnp.mean(values, axis=1, keepdims=True)
        inverse = lax.rsqrt(jnp.mean(centered * centered, axis=1, keepdims=True) + EPSILON)
        normal = centered * inverse
        normal_ref[here, :] = normal
        inverse_ref[here, :] = inverse
        hidden_ref[here, :] = (normal * row(gain_ref) + row(shift_ref)).astype(BF16)

    strips(tokens_ref.shape[0], step)
    for i, hidden in enumerate((hidden_0, hidden_1, hidden_2, hidden_3)):
        hidden[...] = hidden_ref[i * part : (i + 1) * part, :]


def feed_units(hidden_ref, up_ref, down_ref, bias, active_ref, slope_ref, sum_ref, before_ref):
    units = up_ref.shape[1]
    for u in range(0, units, BLOCK):
        for r in range(0, hidden_ref.shape[0], 2 * BLOCK):
            here = slice(r, r + 2 * BLOCK)
            pre_up = bias[:, u : u + BLOCK] + product(hidden_ref[here, :], up_ref[:, u : u + BLOCK])
            cumulative, density = normal_parts(pre_up)
            active = (pre_up * cumulative).astype(BF16)
            active_ref[u : u + BLOCK, here] = active.T
            slope_ref[here, u : u + BLOCK] = (cumulative + pre_up * density).astype(BF16)
            now = product(active, down_ref[u : u + BLOCK, :])
            if u:
                sum_ref[here, :] += now
            elif before_ref is not None:
                sum_ref[here, :] = before_ref[here, :] + now
            else:
                sum_ref[here, :] = now


def feed_kernel(flags_ref, *refs):
    own_refs, other_refs, refs = refs[:4], refs[4:8], refs[8:]
    up_ref, down_ref, bias_ref, hidden_ref, turned_ref, active_ref, slope_ref, sum_ref = refs
    join_parts(flags_ref, own_refs, other_refs, hidden_ref)
    turned_ref[...] = hidden_ref[...].T
    feed_units(hidden_ref, up_ref, down_ref, row(bias_ref), active_ref, slope_ref, sum_ref, None)


def feed_last_kernel(
    flags_ref, hidden_ref, up_a, up_b, up_c, down_a, down_b, down_c, bias_ref, before_ref,
    up_ref, down_ref, active_ref, slope_ref, keep_ref, send_ref, sum_ref,
):
    for (direct, *around), out in (((up_a, up_b, up_c), up_ref), ((down_a, down_b, down_c), down_ref)):
        half = direct.shape[0]
        out[piece(flags_ref[0], half), :] = direct[...]
        for i, ref in enumerate(around):
            out[piece((1 - flags_ref[0]) * 2 + i, half // 2), :] = ref[...]
    feed_units(hidden_ref, up_ref, down_ref, bias_ref[0:1, :], active_ref, slope_ref, sum_ref, before_ref)
    share(flags_ref, sum_ref, keep_ref, send_ref)


def norm_two_kernel(
    keep_ref, got_ref, normal_ref, gain_one_ref, shift_one_ref, down_b_ref, gain_ref, shift_ref, cotangent_ref,
    out_ref, grad_ref, low_ref, vector_ref,
):
    def step(here):
        values = keep_ref[here, :] + got_ref[here, :].astype(F32) + row(down_b_ref)
        values = values + (normal_ref[here, :] * row(gain_one_ref) + row(shift_one_ref))
        centered = values - jnp.mean(values, axis=1, keepdims=True)
        inverse = lax.rsqrt(jnp.mean(centered * centered, axis=1, keepdims=True) + EPSILON)
        normal = centered * inverse
        out_ref[here, :] = (normal * row(gain_ref) + row(shift_ref)).astype(BF16)
        upstream = cotangent_ref[here, :].astype(F32)
        scaled = upstream * row(gain_ref)
        first = jnp.mean(scaled, axis=1, keepdims=True)
        second = jnp.mean(scaled * normal, axis=1, keepdims=True)
        grad = inverse * (scaled - first - normal * second)
        grad_ref[here, :] = grad
        low_ref[here, :] = grad.astype(BF16)
        return upstream * normal, upstream, grad

    rows, model = keep_ref.shape
    vector_ref[...] = jnp.concatenate(strips(rows, step, 3, model) + [jnp.zeros((5, model), F32)], axis=0)


def quarters(flags_ref, size):
    return [pl.ds(pl.multiple_of(jnp.bitwise_xor(flags_ref[4], i) * size, 16), size) for i in range(4)]


def down_back_units(flags_ref, grad_ref, active_ref, down_grad_ref):
    quarter = active_ref.shape[0] // 4
    for i, where in enumerate(quarters(flags_ref, quarter)):
        value = product(active_ref[i * quarter : (i + 1) * quarter, :], grad_ref[...])
        down_grad_ref[where, :] = value.astype(BF16)


def down_back_kernel(flags_ref, own_ref, other_ref, active_ref, grad_ref, down_grad_ref):
    join(flags_ref, own_ref, other_ref, grad_ref)
    down_back_units(flags_ref, grad_ref, active_ref, down_grad_ref)


def feed_back_units(
    flags_ref, grad_ref, slope_ref, hidden_ref, up_ref, down_ref, before_ref, bias_grad_ref, sum_ref, turned_ref, grad_pre_ref,
):
    rows, model = grad_ref.shape
    units = slope_ref.shape[1]
    for u in range(0, units, BLOCK):
        here = slice(u, u + BLOCK)
        total = 0.0
        for r in range(0, rows, 2 * BLOCK):
            grad_active = cols_product(grad_ref[r : r + 2 * BLOCK, :], down_ref[here, :])
            grad_pre = (slope_ref[r : r + 2 * BLOCK, here].astype(F32) * grad_active).astype(BF16)
            grad_pre_ref[r : r + 2 * BLOCK, here] = grad_pre
            total = total + jnp.sum(grad_pre.astype(F32), axis=0, keepdims=True)
            bias_grad_ref[:, here] = jnp.concatenate([total, jnp.zeros((7, total.shape[1]), F32)], axis=0)
    for i, where in enumerate(quarters(flags_ref, model // 4)):
        value = product(hidden_ref[i * (model // 4) : (i + 1) * (model // 4), :], grad_pre_ref[...])
        turned_ref[where, :] = value.astype(BF16)
    for r in range(0, rows, BLOCK):
        value = cols_product(grad_pre_ref[r : r + BLOCK, :], up_ref[...])
        if before_ref is not None:
            value = value + before_ref[r : r + BLOCK, :]
        sum_ref[r : r + BLOCK, :] = value


def split(turned_ref, keep_ref, sends, first):
    quarter, half = turned_ref.shape[0] // 4, turned_ref.shape[1] // 2
    for columns, (stay, go), send in ((slice(0, half), ((0, 2), (1, 3)), 0), (slice(half, 2 * half), ((0, 1), (2, 3)), 1)):
        for i in range(2):
            there = slice(i * quarter, (i + 1) * quarter)
            keep_ref[there, columns] = turned_ref[stay[i] * quarter : (stay[i] + 1) * quarter, columns]
            there = slice(first + i * quarter, first + (i + 1) * quarter)
            sends[send][there, :] = turned_ref[go[i] * quarter : (go[i] + 1) * quarter, columns]


def feed_back_theirs_kernel(
    flags_ref, grad_ref, slope_ref, hidden_ref, up_ref, down_ref,
    keep_up, send_y, send_z, bias_grad_ref, sum_ref, turned_ref, grad_pre_ref,
):
    feed_back_units(
        flags_ref, grad_ref, slope_ref, hidden_ref, up_ref, down_ref, None, bias_grad_ref, sum_ref, turned_ref, grad_pre_ref
    )
    split(turned_ref, keep_up, (send_y, send_z), 0)


def feed_back_mine_kernel(
    flags_ref, grad_ref, active_ref, slope_ref, hidden_ref, up_ref, down_ref, before_ref,
    theirs_y, theirs_z, grad_two_ref, down_grad_ref, keep_up, send_y, send_z, bias_grad_ref, keep_ref, send_0, send_1, send_2, send_3, sum_ref, turned_ref, grad_pre_ref,
):
    down_back_units(flags_ref, grad_ref, active_ref, down_grad_ref)
    feed_back_units(
        flags_ref, grad_ref, slope_ref, hidden_ref, up_ref, down_ref, before_ref,
        bias_grad_ref, sum_ref, turned_ref, grad_pre_ref,
    )
    half = theirs_y.shape[0]
    send_y[:half, :] = theirs_y[...]
    send_z[:half, :] = theirs_z[...]
    split(turned_ref, keep_up, (send_y, send_z), half)
    share(flags_ref, sum_ref, keep_ref, send_0, send_1, send_2, send_3)
    keep_ref[...] += grad_two_ref[...]


def norm_one_back_kernel(
    keep_ref, got_0, got_1, got_2, got_3, normal_ref, inverse_ref, gain_ref, two_ref,
    grad_ref, low_a, low_b, got_ref, low_ref, vector_ref,
):
    part, half = got_0.shape[0], low_a.shape[0]
    for i, got in enumerate((got_0, got_1, got_2, got_3)):
        got_ref[i * part : (i + 1) * part, :] = got[...]

    def step(here):
        upstream, normal = keep_ref[here, :] + got_ref[here, :].astype(F32), normal_ref[here, :]
        scaled = upstream * row(gain_ref)
        first = jnp.mean(scaled, axis=1, keepdims=True)
        second = jnp.mean(scaled * normal, axis=1, keepdims=True)
        grad = inverse_ref[here, :] * (scaled - first - normal * second)
        grad_ref[here, :] = grad
        low_ref[here, :] = grad.astype(BF16)
        return grad, upstream * normal, upstream

    rows, model = keep_ref.shape
    vector_ref[...] = jnp.concatenate(
        strips(rows, step, 3, model) + [two_ref[0:3, :], jnp.zeros((2, model), F32)], axis=0
    )
    low_a[...] = low_ref[:half, :]
    low_b[:half, :] = low_ref[half:, :]
    low_b[half : half + 8, :] = vector_ref[...].astype(BF16)
    low_b[half + 8 :, :] = jnp.zeros((low_b.shape[0] - half - 8, low_b.shape[1]), BF16)


def attend_back_kernel(
    flags_ref, own_a, own_b, other_a, other_b, up_sum_ref,
    x_ref, heads_ref, context_ref, log_ref, w_ref, out_ref, plain_ref,
    grad_ref, grad_heads_ref, inner_ref, turned_ref, keys_ref, values_ref,
):
    rows, model = x_ref.shape
    width = context_ref.shape[0]
    heads = width // HEAD_DIM
    size = width + BIAS_ROWS
    half = own_a.shape[0]
    join_parts(flags_ref, (own_a, own_b), (other_a, other_b), grad_ref)
    blank = jnp.zeros((2 * BLOCK, LANES - HEAD_DIM), BF16)
    for r in range(0, rows, 2 * BLOCK):
        here = slice(r, r + 2 * BLOCK)
        low = cols_product(grad_ref[here, :], w_ref[3 * width :, :]).astype(BF16)
        turned = low.T.astype(F32) * context_ref[:, here]
        for h in range(heads):
            part = slice(h * HEAD_DIM, (h + 1) * HEAD_DIM)
            grad_heads_ref[h, here, :] = jnp.concatenate([low[:, part], blank], axis=1)
            inner_ref[h : h + 1, here] = jnp.sum(turned[part, :], axis=0, keepdims=True)
    keys_ref[...] = jnp.zeros_like(keys_ref)
    values_ref[...] = jnp.zeros_like(values_ref)
    for i in range(rows // BLOCK):
        here, seen = slice(i * BLOCK, (i + 1) * BLOCK), window(i, rows)
        for h in range(heads):
            queries, grads, key_rows = heads_ref[h, here, :], grad_heads_ref[h, here, :], heads_ref[heads + h, seen, :]
            probs = jnp.exp(cols_product(key_rows, queries) - log_ref[h : h + 1, here])
            grad_probs = cols_product(heads_ref[2 * heads + h, seen, :], grads)
            grad_scores = (probs * (grad_probs - inner_ref[h : h + 1, here])).astype(BF16)
            values_ref[h, seen, :] += product(probs.astype(BF16), grads)
            keys_ref[h, seen, :] += product(grad_scores, queries)
            grad_queries = rows_product(key_rows, grad_scores)[:HEAD_DIM, :] * (HEAD_DIM**-0.5)
            turned_ref[h * HEAD_DIM : (h + 1) * HEAD_DIM, here] = grad_queries.astype(BF16)
    for i, ref in ((1, keys_ref), (2, values_ref)):
        for h in range(heads):
            first = i * width + h * HEAD_DIM
            turned_ref[first : first + HEAD_DIM, :] = ref[h].T[:HEAD_DIM, :].astype(BF16)
    for i in range(3):
        plain_ref[:, i * 2 * LANES : i * 2 * LANES + width] = turned_ref[i * width : (i + 1) * width, :].T
    tops = [jnp.zeros((8, model), F32)] * 4
    for i in (0, 2):
        top = jnp.sum(plain_ref[:, i * 2 * LANES : i * 2 * LANES + width].astype(F32), axis=0, keepdims=True)
        top = jnp.concatenate([top, jnp.zeros((1, model - width), F32)], axis=1)
        tops[i] = jnp.concatenate([top, jnp.zeros((7, model), F32)], axis=0)
    tops[1] = up_sum_ref[...]
    tops[3] = own_b[half : half + 8, :].astype(F32) + other_b[half : half + 8, :].astype(F32)
    for i, here in enumerate(quarters(flags_ref, size)):
        if i < 3:
            grad = product(turned_ref[i * width : (i + 1) * width, :], x_ref[...])
        else:
            grad = product(context_ref[...].astype(BF16), grad_ref[...])
        blank = jnp.zeros((BIAS_ROWS - 8, model), F32)
        out_ref[here, :] = jnp.concatenate([grad, tops[i], blank], axis=0).astype(BF16)


def tokens_kernel(flags_ref, grad_ref, plain_0, plain_2, w_0, w_2, keep_ref, send_ref, sum_ref):
    rows, model = plain_0.shape[0], grad_ref.shape[1]
    width = w_0.shape[0] // 4
    for r in range(0, rows, BLOCK):
        total = 0.0
        for plain, w_ref in ((plain_0, w_0), (plain_2, w_2)):
            for i in range(3):
                total = total + product(
                    plain[r : r + BLOCK, i * 2 * LANES : i * 2 * LANES + width], w_ref[i * width : (i + 1) * width, :]
                )
        sum_ref[r : r + BLOCK, :] = total
    share(flags_ref, sum_ref, keep_ref, send_ref)
    keep_ref[...] += grad_ref[...]


def last_kernel(keep_ref, got_ref, out_ref):
    out_ref[...] = keep_ref[...] + got_ref[...].astype(F32)


def unpack_kernel(
    flags_ref, part_0, part_1, part_2, part_3,
    query_ref, key_ref, value_ref, out_w_ref, query_b_ref, value_b_ref, up_b_ref, *refs,
):
    vector_refs, parts = refs[:-1], refs[-1]
    for i, ref in enumerate((part_0, part_1, part_2, part_3)):
        parts[jnp.bitwise_xor(flags_ref[4], i)] = ref[...]
    width = query_ref.shape[0]
    for i, ref in enumerate((query_ref, key_ref, value_ref, out_w_ref)):
        ref[...] = parts[i, :width, :].astype(F32)
    tops = [parts[i, width : width + BIAS_ROWS, :].astype(F32) for i in range(4)]
    query_b_ref[...] = tops[0][0, :width]
    value_b_ref[...] = tops[2][0, :width]
    up_b_ref[...] = tops[1][0, :]
    for i, ref in enumerate(vector_refs):
        ref[...] = tops[3][i, :]


def tie(*arrays):
    return lax.optimization_barrier(arrays)


def add(*members):
    members = [m.astype(F32) for m in members]
    while len(members) > 1:
        members = [a + b for a, b in zip(members[::2], members[1::2])]
    return members[0].astype(BF16)


class Swaps:
    def __init__(self, dp_size, replica):
        self.dp_size, self.near = dp_size, replica & 3

    def core(self, values_in):
        return lax.ppermute(values_in, "tensor", [(i, i ^ 1) for i in range(4)])

    def chip(self, values_in):
        return lax.ppermute(values_in, "tensor", [(i, i ^ 2) for i in range(4)])

    def replica(self, values_in, mask):
        return lax.ppermute(values_in, "dp", [(i, i ^ mask) for i in range(self.dp_size)])

    def scatter(self, parts):
        return [self.replica(parts[m], m) for m in (1, 2, 3)]

    def far(self, value, mask):
        return self.replica(value, mask)

    def gather(self, value):
        return [self.replica(value, m) for m in (1, 2, 3)]

    @property
    def far_masks(self):
        return [1 << b for b in range(2, self.dp_size.bit_length() - 1)]

    def placed(self, members):
        return [lax.select_n(self.near, *[members[i ^ p] for p in range(4)]) for i in range(4)]


def cut_pair(value):
    half = value.shape[0] // 2
    return [value[:half], value[half:]]


def cut(value):
    size = value.shape[0] // 4
    return [value[i * size : (i + 1) * size] for i in range(4)]


def first_calls(
    flags, query_bias, value_bias, up_bias, query_weight, key_weight, value_weight, out_weight, up_weight, down_weight,
):
    model, width = query_weight.shape
    far, vmem = pl.BlockSpec(memory_space=pl.ANY), pl.BlockSpec(memory_space=pltpu.VMEM)
    smem = pl.BlockSpec(memory_space=pltpu.SMEM)
    params = dict(
        compiler_params=pltpu.CompilerParams(vmem_limit_bytes=PACK_LIMIT),
        cost_estimate=pl.CostEstimate(flops=0, bytes_accessed=0, transcendentals=0),
    )
    weights = (query_weight.T, key_weight.T, value_weight.T, out_weight)
    shapes = [(width + BIAS_ROWS, model), (width, model)]
    pieces = pl.pallas_call(
        pieces_kernel,
        in_specs=[smem] + [vmem] * 3 + [far] * 4,
        out_specs=[vmem] * 2,
        out_shape=[jax.ShapeDtypeStruct(s, BF16) for s in shapes],
        scratch_shapes=[pltpu.SemaphoreType.DMA((2,))],
        **params,
    )(flags, query_bias, value_bias, up_bias, *weights)
    pieces, weights = tie(pieces, weights)
    halves = [(w.shape[0] // 2, w.shape[1]) for w in (up_weight, down_weight)]
    outs = [(4 * width, model)] + halves
    rest = pl.pallas_call(
        pack_kernel,
        in_specs=[smem] + [far] * 6,
        out_specs=[far] * 3,
        out_shape=[jax.ShapeDtypeStruct(s, BF16) for s in outs],
        scratch_shapes=[pltpu.VMEM(s, BF16) for s in outs] + [pltpu.SemaphoreType.DMA((9,))],
        **params,
    )(flags, *weights, up_weight, down_weight)
    return [*pieces, *rest]


def body(
    dp_size,
    tokens,
    lengths,
    cotangent,
    query_weight,
    query_bias,
    key_weight,
    value_weight,
    value_bias,
    out_weight,
    out_bias,
    gain_one,
    shift_one,
    up_weight,
    up_bias,
    down_weight,
    down_bias,
    gain_two,
    shift_two,
):
    own, model = tokens.shape
    width = query_weight.shape[1]
    units = up_weight.shape[1]
    rows = 2 * own
    place = lax.axis_index("tensor")
    replica = lax.axis_index("dp")
    flags = [(replica ^ (replica >> 1)) & 1, place % 2, place // 2, place, replica & 3, (replica >> 1) & 1, replica & 1]
    flags = jnp.stack(flags).astype(jnp.int32)
    swaps = Swaps(dp_size, replica)
    swap_core, swap_chip, swap_replica = swaps.core, swaps.chip, swaps.replica
    far_masks = swaps.far_masks

    other_tokens = swap_core(tokens)
    pack_a, pack_b, pack, up_half, down_half = first_calls(
        flags, query_bias, value_bias, up_bias, query_weight, key_weight, value_weight, out_weight, up_weight, down_weight
    )
    whole, half_row = (4 * (width + BIAS_ROWS), model), (own, model)
    halves, fourths = [((own // 2, model), BF16)] * 2, [((own // 4, model), BF16)] * 4
    heads_shape = ((3 * width // HEAD_DIM, rows, LANES), BF16)
    values_scratch = pltpu.VMEM((width, rows), BF16)
    kept_shapes = [((width, rows), F32), ((8, rows), F32)]
    direct = [swap_chip(pack_a), swap_chip(pack_b)]
    up_direct, down_direct = swap_chip(up_half), swap_chip(down_half)

    inputs, qkv_0, context_0, turned_0, log_0 = call(
        attend_kernel,
        [((rows, model), BF16), heads_shape, ((rows, width), BF16)] + kept_shapes,
        (flags, lengths, pack, query_bias, value_bias, tokens, other_tokens),
        scalars=2,
        scratch=[values_scratch],
    )
    *direct, inputs = tie(*direct, inputs)
    around = [swap_replica(direct[0], 1), swap_replica(direct[1], 2)]
    *around, inputs = tie(*around, inputs)
    pack_2, qkv_2, turned_2, log_2, bias_2, keep, *sends = call(
        attend_last_kernel,
        [((4 * width, model), BF16), heads_shape] + kept_shapes + [((8, model), F32), (half_row, F32)] + fourths,
        (flags, lengths, *direct, *around, inputs, context_0, pack),
        scalars=2,
        scratch=[values_scratch, pltpu.VMEM((rows, width), BF16), pltpu.VMEM((rows, model), F32)],
    )
    *sends, up_direct = tie(*sends, up_direct)
    got = [swap_core(v) for v in sends]
    fourth = model // 4
    up_around = [swap_replica(up_direct[:fourth], 1), swap_replica(up_direct[fourth:], 2)]
    normal_one, inverse_one, *hidden = call(
        norm_one_kernel,
        [(half_row, F32), ((own, 1), F32)] + fourths,
        (tokens, keep, *got, out_bias, gain_one, shift_one),
        scratch=[pltpu.VMEM(half_row, BF16)] * 2,
    )
    other_hidden = [swap_core(v) for v in hidden]
    hidden[0], down_direct, *held = tie(hidden[0], down_direct, *other_hidden, *up_around)
    other_hidden, up_around = held[:4], held[4:]
    fourth = units // 4
    down_around = [swap_replica(down_direct[:fourth], 1), swap_replica(down_direct[fourth:], 2)]

    act_shapes = [((units, rows), BF16), ((rows, units), BF16)]
    hidden_full, hidden_turned, active_0, slope_0, before = call(
        feed_kernel,
        [((rows, model), BF16), ((model, rows), BF16)] + act_shapes + [((rows, model), F32)],
        (flags, *hidden, *other_hidden, up_weight, down_weight, up_bias),
        scalars=1,
    )
    before, *down_around = tie(before, *down_around)
    up_2, down_2, active_2, slope_2, keep, send = call(
        feed_last_kernel,
        [((model, units), BF16), ((units, model), BF16)] + act_shapes + [(half_row, F32), (half_row, BF16)],
        (flags, hidden_full, up_direct, *up_around, down_direct, *down_around, bias_2, before),
        scalars=1,
        scratch=[pltpu.VMEM((rows, model), F32)],
    )
    layer_output, grad_two, low_grad_two, vector_two = call(
        norm_two_kernel,
        [(half_row, BF16), (half_row, F32), (half_row, BF16), ((8, model), F32)],
        (
            keep, swap_core(send), normal_one, gain_one, shift_one, down_bias,
            gain_two, shift_two, cotangent,
        ),
    )

    back_scratch = [pltpu.VMEM((model, units), BF16), pltpu.VMEM((rows, units), BF16)]
    grad_full, down_theirs = call(
        down_back_kernel,
        [((rows, model), BF16), ((units, model), BF16)],
        (flags, low_grad_two, swap_core(low_grad_two), active_2),
        scalars=1,
    )
    down_theirs, grad_full = tie(down_theirs, grad_full)
    down_chip = swap_chip(down_theirs)
    up_keep_2, *up_sends, up_sum_2, running = call(
        feed_back_theirs_kernel,
        [((model // 2, units), BF16)] + [((model // 2, units // 2), BF16)] * 2 + [((8, units), F32), ((rows, model), F32)],
        (flags, grad_full, slope_2, hidden_turned, up_2, down_2),
        scalars=1,
        scratch=back_scratch,
    )
    down_mine, up_keep_0, *up_sends, up_sum_0, keep, send_0, send_1, send_2, send_3 = call(
        feed_back_mine_kernel,
        [((units, model), BF16), ((model // 2, units), BF16)] + [((model, units // 2), BF16)] * 2
        + [((8, units), F32), (half_row, F32)]
        + [((own // 4, model), BF16)] * 4,
        (
            flags, grad_full, active_0, slope_0, hidden_turned, up_weight, down_weight, running, *up_sends, grad_two,
        ),
        scalars=1,
        scratch=[pltpu.VMEM((rows, model), F32)] + back_scratch,
    )
    up_got = [swap_replica(up_sends[0], 1), swap_replica(up_sends[1], 2)]
    got = [swap_core(v) for v in (send_0, send_1, send_2, send_3)]
    grad_one, low_a, low_b = call(
        norm_one_back_kernel,
        [(half_row, F32), halves[0], ((own // 2 + BIAS_ROWS, model), BF16)],
        (keep, *got, normal_one, inverse_one, gain_one, vector_two),
        scratch=[pltpu.VMEM(half_row, BF16)] * 2 + [pltpu.VMEM((8, model), F32)],
    )
    low_other = [swap_core(low_a), swap_core(low_b)]


    def attend_back(low_a, qkv, turned, log_total, shard, up_sum):
        return call(
            attend_back_kernel,
            [(whole, BF16), ((rows, 6 * LANES), BF16)],
            (
                flags, low_a, low_b, *low_other, up_sum,
                inputs, qkv, turned, log_total, shard,
            ),
            scalars=1,
            scratch=[
                pltpu.VMEM((rows, model), BF16), pltpu.VMEM((width // HEAD_DIM, rows, LANES), BF16),
                pltpu.VMEM((8, rows), F32), pltpu.VMEM((3 * width, rows), BF16),
                pltpu.VMEM((width // HEAD_DIM, rows, LANES), F32), pltpu.VMEM((width // HEAD_DIM, rows, LANES), F32),
            ],
        )

    pack_theirs, plain_2 = attend_back(low_a, qkv_2, turned_2, log_2, pack_2, up_sum_2)
    pack_theirs, low_a = tie(pack_theirs, low_a)
    pack_chip = swap_chip(pack_theirs)
    pack_mine, plain_0 = attend_back(low_a, qkv_0, turned_0, log_0, pack, up_sum_0)
    keep, send = call(
        tokens_kernel,
        [(half_row, F32), (half_row, BF16)],
        (flags, grad_one, plain_0, plain_2, pack, pack_2),
        scalars=1,
        scratch=[pltpu.VMEM((rows, model), F32)],
    )
    pack_mine, keep, send, down_chip, *up_got = tie(pack_mine, keep, send, down_chip, *up_got)

    down_parts = [add(m, t) for m, t in zip(cut(down_mine), cut(down_chip))]
    up_theirs, up_mine = [
        add(keep_up, jnp.concatenate([got_up[here] for got_up in up_got], axis=1))
        for keep_up, here in ((up_keep_2, slice(0, model // 2)), (up_keep_0, slice(model // 2, model)))
    ]
    up_theirs, up_mine, *down_parts = tie(up_theirs, up_mine, *down_parts)
    down_got = swaps.scatter(down_parts)
    up_chip = swap_chip(up_theirs)
    down_got = tie(*down_got)
    down_now = add(down_parts[0], *down_got)
    (down_now,) = tie(down_now)
    down_far = swaps.far(down_now, far_masks[0])
    pack_chip, pack_mine = tie(pack_chip, pack_mine)
    pack_parts = [add(m, t) for m, t in zip(cut(pack_mine), cut(pack_chip))]
    pack_parts = tie(*pack_parts)
    pack_got = swaps.scatter(pack_parts)
    *pack_got, up_chip, down_far = tie(*pack_got, up_chip, down_far)
    pack_now = add(pack_parts[0], *pack_got)
    up_now, up_next = [add(m, t) for m, t in zip(cut_pair(up_mine), cut_pair(up_chip))]
    up_next = [up_next[:, : units // 2], up_next[:, units // 2 :]]
    down_now = add(down_now, down_far)
    for mask in far_masks[1:]:
        down_now = add(down_now, swaps.far(down_now, mask))
    pack_now, up_now, up_next[0], up_next[1], down_now, send = tie(pack_now, up_now, *up_next, down_now, send)
    pack_far = swaps.far(pack_now, far_masks[0])
    up_got = [swap_replica(up_next[0], 2), swap_replica(up_next[1], 1)]
    down_pair = jnp.concatenate([down_now, swap_replica(down_now, 2)], axis=0)
    got = swap_core(send)
    (down_pair,) = tie(down_pair)
    down_other = swap_replica(down_pair, 1)
    *up_got, got = tie(*up_got, got)
    up_now = add(up_now, jnp.concatenate(up_got, axis=1))
    (up_now,) = tie(up_now)
    up_far = swaps.far(up_now, far_masks[0])
    (pack_far,) = tie(pack_far)
    pack_now = add(pack_now, pack_far)
    for mask in far_masks[1:]:
        pack_now = add(pack_now, swaps.far(pack_now, mask))
    (pack_now,) = tie(pack_now)
    pack_all = [pack_now] + swaps.gather(pack_now)
    (tokens_grad,) = call(last_kernel, [(half_row, F32)], (keep, got))
    up_far, tokens_grad, down_other = tie(up_far, tokens_grad, down_other)
    up_now = add(up_now, up_far)
    for mask in far_masks[1:]:
        up_now = add(up_now, swaps.far(up_now, mask))
    up_now, late_flags = tie(up_now, flags)
    up_all = [up_now] + swaps.gather(up_now)
    first, second = cut_pair(down_pair), cut_pair(down_other)
    down_all = [first[0], second[0], first[1], second[1]]
    down_weight_grad = jnp.concatenate(swaps.placed(down_all), axis=0).astype(F32)
    up_weight_grad = jnp.concatenate(swaps.placed(up_all), axis=0).astype(F32)
    shard = [((width, model), F32)] * 4 + [((width,), F32)] * 2 + [((units,), F32)] + [((model,), F32)] * 6
    (
        query_grad, key_grad, value_grad, out_grad, query_bias_grad, value_bias_grad, up_bias_row, *vectors,
    ) = call(
        unpack_kernel, shard, (late_flags, *pack_all), scalars=1, scratch=[pltpu.VMEM((4, width + BIAS_ROWS, model), BF16)]
    )
    return (
        layer_output,
        tokens_grad,
        query_grad.T,
        query_bias_grad,
        key_grad.T,
        value_grad.T,
        value_bias_grad,
        out_grad,
        vectors[0],
        vectors[1],
        vectors[2],
        up_weight_grad,
        up_bias_row,
        down_weight_grad,
        vectors[5],
        vectors[3],
        vectors[4],
    )


def solution(mesh):
    placed = (
        P(("dp", "tensor"), None),
        P("dp", None),
        P(("dp", "tensor"), None),
        P(None, "tensor"),
        P("tensor"),
        P(None, "tensor"),
        P(None, "tensor"),
        P("tensor"),
        P("tensor", None),
        P(),
        P(),
        P(),
        P(None, "tensor"),
        P("tensor"),
        P("tensor", None),
        P(),
        P(),
        P(),
    )
    return jax.shard_map(
        functools.partial(body, mesh.shape["dp"]),
        mesh=mesh,
        in_specs=placed,
        out_specs=(
            P(("dp", "tensor"), None),
            P(("dp", "tensor"), None),
            P(None, "tensor"),
            P("tensor"),
            P(None, "tensor"),
            P(None, "tensor"),
            P("tensor"),
            P("tensor", None),
            P(),
            P(),
            P(),
            P(None, "tensor"),
            P("tensor"),
            P("tensor", None),
            P(),
            P(),
            P(),
        ),
        check_vma=False,
    )
```

```python
import functools

import jax
import jax.numpy as jnp
from jax import lax
from jax.experimental import pallas as pl
from jax.experimental.pallas import tpu as pltpu
from jax.sharding import PartitionSpec as P

HEAD_DIM = 64
MOST = 256
EPSILON = 1e-05
MASKED = -1e30
BLOCK = 256
STRIP = 64
LANES = 128
BIAS_ROWS = 16
LEFT = 512
VMEM_LIMIT = 16 * 1024 * 1024
PACK_LIMIT = 60 * 1024 * 1024
TAIL_SCALE = 0.425
TAIL = (
    0.23966740682492862,
    0.24201181237516,
    0.19964184258583956,
    0.2585875675603689,
    -0.10985333090134082,
    0.4147788772153898,
    -0.3173079260911745,
    0.07247363954140279,
)

BF16 = jnp.bfloat16
F32 = jnp.float32


def product(left_side, right_side):
    return jnp.dot(left_side, right_side, preferred_element_type=F32)


def rows_product(left_side, right_side):
    return lax.dot_general(
        left_side, right_side, (((0,), (0,)), ((), ())), preferred_element_type=F32
    )


def cols_product(left_side, right_side):
    return lax.dot_general(
        left_side, right_side, (((1,), (1,)), ((), ())), preferred_element_type=F32
    )


def normal_parts(z):
    size = jnp.abs(z)
    t = 1.0 / (1.0 + (TAIL_SCALE * 0.7071067811865476) * size)
    series = TAIL[-1]
    for factor in TAIL[-2::-1]:
        series = series * t + factor
    bell = jnp.exp(-0.5 * z * z)
    tail = (0.5 * bell) * (series * t)
    return jnp.where(z >= 0.0, 1.0 - tail, tail), bell * 0.3989422804014327


def call(kernel, outs, args, scalars=0, scratch=(), cost=1.0, far=()):
    specs = [pl.BlockSpec(memory_space=pltpu.SMEM)] * scalars
    specs += [pl.BlockSpec(memory_space=pltpu.VMEM)] * (len(args) + len(outs) - scalars)
    for i in far:
        specs[i] = pl.BlockSpec(memory_space=pl.ANY)
    outputs = pl.pallas_call(
        kernel,
        in_specs=specs[: len(args)],
        out_specs=specs[len(args) :],
        out_shape=[jax.ShapeDtypeStruct(shape, dtype) for shape, dtype in outs],
        scratch_shapes=list(scratch),
        compiler_params=pltpu.CompilerParams(vmem_limit_bytes=VMEM_LIMIT),
        cost_estimate=pl.CostEstimate(
            flops=0, bytes_accessed=0, transcendentals=0
        ),
    )(*args)
    return list(outputs)


def piece(index, size):
    return pl.ds(pl.multiple_of(index * size, 16), size)


def assemble(side, refs, out_ref):
    size, count = refs[0].shape[0], len(refs) // 2
    for i, ref in enumerate(refs):
        first = side if i < count else 1 - side
        out_ref[piece(first * count + i % count, size), :] = ref[...]


def row(ref):
    return ref[...].reshape(1, -1)


def join_parts(flags_ref, own_refs, other_refs, out_ref):
    for side, parts in ((flags_ref[1], own_refs), (1 - flags_ref[1], other_refs)):
        for i, part in enumerate(parts):
            size = out_ref.shape[0] // (2 * len(parts))
            out_ref[piece(side * len(parts) + i, size), :] = part[:size, :]


def join(flags_ref, own_ref, other_ref, out_ref):
    size = own_ref.shape[0]
    out_ref[piece(flags_ref[1], size), :] = own_ref[...]
    out_ref[piece(1 - flags_ref[1], size), :] = other_ref[...]


def pieces_kernel(
    flags_ref, query_b_ref, value_b_ref, up_b_ref, query_ref, key_ref, value_ref, out_w_ref, near_a, near_b, sems,
):
    weights = (query_ref, key_ref, value_ref, out_w_ref)
    width, model = query_ref.shape
    for side in range(2):

        @pl.when(flags_ref[0] == side)
        def load():
            for k, near in enumerate((near_a, near_b)):
                pltpu.make_async_copy(weights[2 * side + k], near.at[:width], sems.at[k]).start()

    blank = jnp.zeros((1, model - 2 * width), F32)
    rows = []
    for part in (row(up_b_ref), jnp.concatenate([row(query_b_ref), row(value_b_ref), blank], axis=1)):
        for _ in range(3):
            rows.append(part.astype(BF16).astype(F32))
            part = part - rows[-1]
    rows.append(jnp.zeros((BIAS_ROWS - 6, model), F32))
    near_a[width:, :] = jnp.concatenate(rows, axis=0).astype(BF16)
    for k, near in enumerate((near_a, near_b)):
        pltpu.make_async_copy(weights[k], near.at[:width], sems.at[k]).wait()


def pack_kernel(
    flags_ref, query_ref, key_ref, value_ref, out_w_ref, up_ref, down_ref,
    pack_ref, up_out, down_out, pack_near, up_near, down_near, sems,
):
    width = query_ref.shape[0]
    half = up_out.shape[0]
    loads = [(ref.at[piece(flags_ref[0], half)], near) for ref, near in ((up_ref, up_near), (down_ref, down_near))]
    weights = (query_ref, key_ref, value_ref, out_w_ref)
    loads += [(s, pack_near.at[i * width : (i + 1) * width]) for i, s in enumerate(weights)]
    copies = [pltpu.make_async_copy(a, b, sems.at[i]) for i, (a, b) in enumerate(loads)]
    for copy in copies:
        copy.start()
    for copy in copies:
        copy.wait()
    stores = ((up_near, up_out), (down_near, down_out), (pack_near, pack_ref))
    copies = [pltpu.make_async_copy(a, b, sems.at[6 + i]) for i, (a, b) in enumerate(stores)]
    for copy in copies:
        copy.start()
    for copy in copies:
        copy.wait()


def document_lanes(flags_ref, lengths_ref, rows):
    shape = (rows, LANES - HEAD_DIM)
    spot = lax.broadcasted_iota(jnp.int32, shape, 0)
    lane = lax.broadcasted_iota(jnp.int32, (1, shape[1]), 1)
    ends = 0
    begin_row, end_row = jnp.zeros_like(lane), jnp.zeros_like(lane)
    documents = lengths_ref.shape[1]
    for d in range(documents):
        begin_row = jnp.where(lane == d, ends, begin_row)
        ends = ends + lengths_ref[flags_ref[2], d]
        end_row = jnp.where(lane == d, ends, end_row)
    inside = (spot >= begin_row) & (spot < end_row)
    outside = jnp.where(lane < documents, MASKED, 0.0)
    return jnp.where(inside, 1.0, 0.0).astype(BF16), jnp.where(inside, 0.0, outside).astype(BF16)


def window(i, rows):
    return slice(max(i - 1, 0) * BLOCK, min(i + 2, rows // BLOCK) * BLOCK)


def attend_units(
    flags_ref, lengths_ref, x_ref, w_ref, biases, heads_ref, context_ref, turned_ref, log_ref, values_ref,
):
    rows, model = x_ref.shape
    width = context_ref.shape[1]
    heads = width // HEAD_DIM
    same, other = document_lanes(flags_ref, lengths_ref, rows)
    tails = (other, same, jnp.zeros_like(same))
    for i, bias in enumerate((biases[0], None, biases[1])):
        weights = w_ref[i * width : (i + 1) * width, :]
        for r in range(0, rows, 2 * BLOCK):
            here = slice(r, r + 2 * BLOCK)
            total = cols_product(x_ref[here, :], weights)
            if bias is not None:
                total = total + bias
            low = total.astype(BF16)
            if i == 0:
                low = low * BF16(HEAD_DIM**-0.5)
            for h in range(heads):
                part = low[:, h * HEAD_DIM : (h + 1) * HEAD_DIM]
                heads_ref[i * heads + h, here, :] = jnp.concatenate([part, tails[i][here, :]], axis=1)
            if i == 2:
                values_ref[:, here] = low.T
    for i in range(rows // BLOCK):
        here, seen = slice(i * BLOCK, (i + 1) * BLOCK), window(i, rows)
        for h in range(heads):
            part = slice(h * HEAD_DIM, (h + 1) * HEAD_DIM)
            queries = heads_ref[h, here, :]
            steps = range(seen.start, seen.stop, BLOCK)
            scores = [cols_product(heads_ref[heads + h, r : r + BLOCK, :], queries) for r in steps]
            top = functools.reduce(jnp.maximum, [jnp.max(s, axis=0, keepdims=True) for s in scores])
            total, context = 0.0, 0.0
            for r, score in zip(steps, scores):
                weights = jnp.exp(score - top)
                total = total + jnp.sum(weights, axis=0, keepdims=True)
                context = context + product(values_ref[part, r : r + BLOCK], weights.astype(BF16))
            turned_ref[part, here] = context * (1.0 / total)
            log_ref[h : h + 1, here] = top + jnp.log(total)
        context_ref[here, :] = turned_ref[:, here].T.astype(BF16)


def attend_kernel(
    flags_ref, lengths_ref, w_ref, query_b_ref, value_b_ref, tokens_ref, other_ref,
    x_ref, heads_ref, context_ref, turned_ref, log_ref, values_ref,
):
    join(flags_ref, tokens_ref, other_ref, x_ref)
    biases = (row(query_b_ref), row(value_b_ref))
    attend_units(
        flags_ref, lengths_ref, x_ref, w_ref, biases, heads_ref, context_ref, turned_ref, log_ref, values_ref
    )


def share(flags_ref, total_ref, keep_ref, *send_refs):
    size = keep_ref.shape[0]
    keep_ref[...] = total_ref[piece(flags_ref[1], size), :]
    part = size // len(send_refs)
    for i, send_ref in enumerate(send_refs):
        send_ref[...] = total_ref[piece((1 - flags_ref[1]) * len(send_refs) + i, part), :].astype(BF16)


def attend_last_kernel(
    flags_ref, lengths_ref, w_0, w_1, w_2, w_3, x_ref, before_ref, w_before,
    w_ref, heads_ref, turned_ref, log_ref, bias_ref, keep_ref, send_0, send_1, send_2, send_3,
    values_ref, context_ref, mix_ref,
):
    width = context_ref.shape[1]
    side = flags_ref[0] * 2
    for ref, spot in ((w_0, side), (w_1, side + 1), (w_2, 2 - side), (w_3, 3 - side)):
        w_ref[piece(spot, width), :] = ref[:width, :]
    parts = w_0[width : width + 6, :].astype(F32)
    bias_ref[0:1, :] = parts[0:1] + parts[1:2] + parts[2:3]
    mixed = parts[3:4] + parts[4:5] + parts[5:6]
    biases = (mixed[:, :width], mixed[:, width : 2 * width])
    attend_units(
        flags_ref, lengths_ref, x_ref, w_ref, biases, heads_ref, context_ref, turned_ref, log_ref, values_ref
    )
    for r in range(0, x_ref.shape[0], BLOCK):
        here = slice(r, r + BLOCK)
        mix_ref[here, :] = product(before_ref[here, :], w_before[3 * width :, :]) + product(
            context_ref[here, :], w_ref[3 * width :, :]
        )
    share(flags_ref, mix_ref, keep_ref, send_0, send_1, send_2, send_3)


def strips(rows, step, sums=0, model=0):
    def one(i, carry):
        found = step(pl.ds(pl.multiple_of(i * STRIP, STRIP), STRIP))
        if not sums:
            return carry
        return tuple(c + jnp.sum(f.reshape(STRIP // 8, 8, model), axis=0) for c, f in zip(carry, found))

    first = tuple(jnp.zeros((8, model), F32) for _ in range(sums))
    total = lax.fori_loop(0, rows // STRIP, one, first if sums else 0, unroll=4)
    return [jnp.sum(t, axis=0, keepdims=True) for t in total] if sums else None


def norm_one_kernel(
    tokens_ref, keep_ref, got_0, got_1, got_2, got_3, out_b_ref, gain_ref, shift_ref,
    normal_ref, inverse_ref, hidden_0, hidden_1, hidden_2, hidden_3, got_ref, hidden_ref,
):
    part = got_0.shape[0]
    for i, got in enumerate((got_0, got_1, got_2, got_3)):
        got_ref[i * part : (i + 1) * part, :] = got[...]

    def step(here):
        values = tokens_ref[here, :].astype(F32) + keep_ref[here, :] + got_ref[here, :].astype(F32) + row(out_b_ref)
        centered = values - jnp.mean(values, axis=1, keepdims=True)
        inverse = lax.rsqrt(jnp.mean(centered * centered, axis=1, keepdims=True) + EPSILON)
        normal = centered * inverse
        normal_ref[here, :] = normal
        inverse_ref[here, :] = inverse
        hidden_ref[here, :] = (normal * row(gain_ref) + row(shift_ref)).astype(BF16)

    strips(tokens_ref.shape[0], step)
    for i, hidden in enumerate((hidden_0, hidden_1, hidden_2, hidden_3)):
        hidden[...] = hidden_ref[i * part : (i + 1) * part, :]


def feed_units(hidden_ref, up_ref, down_ref, bias, active_ref, slope_ref, sum_ref, before_ref):
    units = up_ref.shape[1]
    for u in range(0, units, BLOCK):
        for r in range(0, hidden_ref.shape[0], 2 * BLOCK):
            here = slice(r, r + 2 * BLOCK)
            pre_up = bias[:, u : u + BLOCK] + product(hidden_ref[here, :], up_ref[:, u : u + BLOCK])
            cumulative, density = normal_parts(pre_up)
            active = (pre_up * cumulative).astype(BF16)
            active_ref[u : u + BLOCK, here] = active.T
            slope_ref[here, u : u + BLOCK] = (cumulative + pre_up * density).astype(BF16)
            now = product(active, down_ref[u : u + BLOCK, :])
            if u:
                sum_ref[here, :] += now
            elif before_ref is not None:
                sum_ref[here, :] = before_ref[here, :] + now
            else:
                sum_ref[here, :] = now


def feed_kernel(flags_ref, *refs):
    own_refs, other_refs, refs = refs[:4], refs[4:8], refs[8:]
    up_ref, down_ref, bias_ref, hidden_ref, turned_ref, active_ref, slope_ref, sum_ref = refs
    join_parts(flags_ref, own_refs, other_refs, hidden_ref)
    turned_ref[...] = hidden_ref[...].T
    feed_units(hidden_ref, up_ref, down_ref, row(bias_ref), active_ref, slope_ref, sum_ref, None)


def feed_last_kernel(
    flags_ref, hidden_ref, up_a, up_b, up_c, down_a, down_b, down_c, bias_ref, before_ref,
    up_ref, down_ref, active_ref, slope_ref, keep_ref, send_ref, sum_ref,
):
    for (direct, *around), out in (((up_a, up_b, up_c), up_ref), ((down_a, down_b, down_c), down_ref)):
        half = direct.shape[0]
        out[piece(flags_ref[0], half), :] = direct[...]
        for i, ref in enumerate(around):
            out[piece((1 - flags_ref[0]) * 2 + i, half // 2), :] = ref[...]
    feed_units(hidden_ref, up_ref, down_ref, bias_ref[0:1, :], active_ref, slope_ref, sum_ref, before_ref)
    share(flags_ref, sum_ref, keep_ref, send_ref)


def norm_two_kernel(
    keep_ref, got_ref, normal_ref, gain_one_ref, shift_one_ref, down_b_ref, gain_ref, shift_ref, cotangent_ref,
    out_ref, grad_ref, low_ref, vector_ref,
):
    def step(here):
        values = keep_ref[here, :] + got_ref[here, :].astype(F32) + row(down_b_ref)
        values = values + (normal_ref[here, :] * row(gain_one_ref) + row(shift_one_ref))
        centered = values - jnp.mean(values, axis=1, keepdims=True)
        inverse = lax.rsqrt(jnp.mean(centered * centered, axis=1, keepdims=True) + EPSILON)
        normal = centered * inverse
        out_ref[here, :] = (normal * row(gain_ref) + row(shift_ref)).astype(BF16)
        upstream = cotangent_ref[here, :].astype(F32)
        scaled = upstream * row(gain_ref)
        first = jnp.mean(scaled, axis=1, keepdims=True)
        second = jnp.mean(scaled * normal, axis=1, keepdims=True)
        grad = inverse * (scaled - first - normal * second)
        grad_ref[here, :] = grad
        low_ref[here, :] = grad.astype(BF16)
        return upstream * normal, upstream, grad

    rows, model = keep_ref.shape
    vector_ref[...] = jnp.concatenate(strips(rows, step, 3, model) + [jnp.zeros((5, model), F32)], axis=0)


def quarters(flags_ref, size):
    return [pl.ds(pl.multiple_of(jnp.bitwise_xor(flags_ref[4], i) * size, 16), size) for i in range(4)]


def down_back_units(flags_ref, grad_ref, active_ref, down_grad_ref):
    quarter = active_ref.shape[0] // 4
    for i, where in enumerate(quarters(flags_ref, quarter)):
        value = product(active_ref[i * quarter : (i + 1) * quarter, :], grad_ref[...])
        down_grad_ref[where, :] = value.astype(BF16)


def down_back_kernel(flags_ref, own_ref, other_ref, active_ref, grad_ref, down_grad_ref):
    join(flags_ref, own_ref, other_ref, grad_ref)
    down_back_units(flags_ref, grad_ref, active_ref, down_grad_ref)


def feed_back_units(
    flags_ref, grad_ref, slope_ref, hidden_ref, up_ref, down_ref, before_ref, bias_grad_ref, sum_ref, turned_ref, grad_pre_ref,
):
    rows, model = grad_ref.shape
    units = slope_ref.shape[1]
    for u in range(0, units, BLOCK):
        here = slice(u, u + BLOCK)
        total = 0.0
        for r in range(0, rows, 2 * BLOCK):
            grad_active = cols_product(grad_ref[r : r + 2 * BLOCK, :], down_ref[here, :])
            grad_pre = (slope_ref[r : r + 2 * BLOCK, here].astype(F32) * grad_active).astype(BF16)
            grad_pre_ref[r : r + 2 * BLOCK, here] = grad_pre
            total = total + jnp.sum(grad_pre.astype(F32), axis=0, keepdims=True)
            bias_grad_ref[:, here] = jnp.concatenate([total, jnp.zeros((7, total.shape[1]), F32)], axis=0)
    for i, where in enumerate(quarters(flags_ref, model // 4)):
        value = product(hidden_ref[i * (model // 4) : (i + 1) * (model // 4), :], grad_pre_ref[...])
        turned_ref[where, :] = value.astype(BF16)
    for r in range(0, rows, BLOCK):
        value = cols_product(grad_pre_ref[r : r + BLOCK, :], up_ref[...])
        if before_ref is not None:
            value = value + before_ref[r : r + BLOCK, :]
        sum_ref[r : r + BLOCK, :] = value


def split(turned_ref, keep_ref, sends, first):
    quarter, half = turned_ref.shape[0] // 4, turned_ref.shape[1] // 2
    for columns, (stay, go), send in ((slice(0, half), ((0, 2), (1, 3)), 0), (slice(half, 2 * half), ((0, 1), (2, 3)), 1)):
        for i in range(2):
            there = slice(i * quarter, (i + 1) * quarter)
            keep_ref[there, columns] = turned_ref[stay[i] * quarter : (stay[i] + 1) * quarter, columns]
            there = slice(first + i * quarter, first + (i + 1) * quarter)
            sends[send][there, :] = turned_ref[go[i] * quarter : (go[i] + 1) * quarter, columns]


def feed_back_theirs_kernel(
    flags_ref, grad_ref, slope_ref, hidden_ref, up_ref, down_ref,
    keep_up, send_y, send_z, bias_grad_ref, sum_ref, turned_ref, grad_pre_ref,
):
    feed_back_units(
        flags_ref, grad_ref, slope_ref, hidden_ref, up_ref, down_ref, None, bias_grad_ref, sum_ref, turned_ref, grad_pre_ref
    )
    split(turned_ref, keep_up, (send_y, send_z), 0)


def feed_back_mine_kernel(
    flags_ref, grad_ref, active_ref, slope_ref, hidden_ref, up_ref, down_ref, before_ref,
    theirs_y, theirs_z, grad_two_ref, down_grad_ref, keep_up, send_y, send_z, bias_grad_ref, keep_ref, send_0, send_1, send_2, send_3, sum_ref, turned_ref, grad_pre_ref,
):
    down_back_units(flags_ref, grad_ref, active_ref, down_grad_ref)
    feed_back_units(
        flags_ref, grad_ref, slope_ref, hidden_ref, up_ref, down_ref, before_ref,
        bias_grad_ref, sum_ref, turned_ref, grad_pre_ref,
    )
    half = theirs_y.shape[0]
    send_y[:half, :] = theirs_y[...]
    send_z[:half, :] = theirs_z[...]
    split(turned_ref, keep_up, (send_y, send_z), half)
    share(flags_ref, sum_ref, keep_ref, send_0, send_1, send_2, send_3)
    keep_ref[...] += grad_two_ref[...]


def norm_one_back_kernel(
    keep_ref, got_0, got_1, got_2, got_3, normal_ref, inverse_ref, gain_ref, two_ref,
    grad_ref, low_a, low_b, got_ref, low_ref, vector_ref,
):
    part, half = got_0.shape[0], low_a.shape[0]
    for i, got in enumerate((got_0, got_1, got_2, got_3)):
        got_ref[i * part : (i + 1) * part, :] = got[...]

    def step(here):
        upstream, normal = keep_ref[here, :] + got_ref[here, :].astype(F32), normal_ref[here, :]
        scaled = upstream * row(gain_ref)
        first = jnp.mean(scaled, axis=1, keepdims=True)
        second = jnp.mean(scaled * normal, axis=1, keepdims=True)
        grad = inverse_ref[here, :] * (scaled - first - normal * second)
        grad_ref[here, :] = grad
        low_ref[here, :] = grad.astype(BF16)
        return grad, upstream * normal, upstream

    rows, model = keep_ref.shape
    vector_ref[...] = jnp.concatenate(
        strips(rows, step, 3, model) + [two_ref[0:3, :], jnp.zeros((2, model), F32)], axis=0
    )
    low_a[...] = low_ref[:half, :]
    low_b[:half, :] = low_ref[half:, :]
    low_b[half : half + 8, :] = vector_ref[...].astype(BF16)
    low_b[half + 8 :, :] = jnp.zeros((low_b.shape[0] - half - 8, low_b.shape[1]), BF16)


def attend_back_kernel(
    flags_ref, own_a, own_b, other_a, other_b, up_sum_ref,
    x_ref, heads_ref, context_ref, log_ref, w_ref, left_ref, right_ref, plain_ref,
    grad_ref, grad_heads_ref, inner_ref, turned_ref, keys_ref, values_ref,
):
    rows, model = x_ref.shape
    width = context_ref.shape[0]
    heads = width // HEAD_DIM
    size = width + BIAS_ROWS
    half = own_a.shape[0]
    join_parts(flags_ref, (own_a, own_b), (other_a, other_b), grad_ref)
    blank = jnp.zeros((2 * BLOCK, LANES - HEAD_DIM), BF16)
    for r in range(0, rows, 2 * BLOCK):
        here = slice(r, r + 2 * BLOCK)
        low = cols_product(grad_ref[here, :], w_ref[3 * width :, :]).astype(BF16)
        turned = low.T.astype(F32) * context_ref[:, here]
        for h in range(heads):
            part = slice(h * HEAD_DIM, (h + 1) * HEAD_DIM)
            grad_heads_ref[h, here, :] = jnp.concatenate([low[:, part], blank], axis=1)
            inner_ref[h : h + 1, here] = jnp.sum(turned[part, :], axis=0, keepdims=True)
    keys_ref[...] = jnp.zeros_like(keys_ref)
    values_ref[...] = jnp.zeros_like(values_ref)
    for i in range(rows // BLOCK):
        here, seen = slice(i * BLOCK, (i + 1) * BLOCK), window(i, rows)
        for h in range(heads):
            queries, grads, key_rows = heads_ref[h, here, :], grad_heads_ref[h, here, :], heads_ref[heads + h, seen, :]
            probs = jnp.exp(cols_product(key_rows, queries) - log_ref[h : h + 1, here])
            grad_probs = cols_product(heads_ref[2 * heads + h, seen, :], grads)
            grad_scores = (probs * (grad_probs - inner_ref[h : h + 1, here])).astype(BF16)
            values_ref[h, seen, :] += product(probs.astype(BF16), grads)
            keys_ref[h, seen, :] += product(grad_scores, queries)
            grad_queries = rows_product(key_rows, grad_scores)[:HEAD_DIM, :] * (HEAD_DIM**-0.5)
            turned_ref[h * HEAD_DIM : (h + 1) * HEAD_DIM, here] = grad_queries.astype(BF16)
    for i, ref in ((1, keys_ref), (2, values_ref)):
        for h in range(heads):
            first = i * width + h * HEAD_DIM
            turned_ref[first : first + HEAD_DIM, :] = ref[h].T[:HEAD_DIM, :].astype(BF16)
    for i in range(3):
        plain_ref[:, i * 2 * LANES : i * 2 * LANES + width] = turned_ref[i * width : (i + 1) * width, :].T
    tops = [jnp.zeros((8, model), F32)] * 4
    for i in (0, 2):
        top = jnp.sum(plain_ref[:, i * 2 * LANES : i * 2 * LANES + width].astype(F32), axis=0, keepdims=True)
        top = jnp.concatenate([top, jnp.zeros((1, model - width), F32)], axis=1)
        tops[i] = jnp.concatenate([top, jnp.zeros((7, model), F32)], axis=0)
    tops[1] = up_sum_ref[...]
    tops[3] = own_b[half : half + 8, :].astype(F32) + other_b[half : half + 8, :].astype(F32)
    for i, here in enumerate(quarters(flags_ref, size)):
        if i < 3:
            grad = product(turned_ref[i * width : (i + 1) * width, :], x_ref[...])
        else:
            grad = product(context_ref[...].astype(BF16), grad_ref[...])
        blank = jnp.zeros((BIAS_ROWS - 8, model), F32)
        value = jnp.concatenate([grad, tops[i], blank], axis=0).astype(BF16)
        left_ref[here, :] = value[:, :LEFT]
        right_ref[here, :] = value[:, LEFT:]


def tokens_kernel(flags_ref, grad_ref, plain_0, plain_2, w_0, w_2, keep_ref, send_ref, sum_ref):
    rows, model = plain_0.shape[0], grad_ref.shape[1]
    width = w_0.shape[0] // 4
    for r in range(0, rows, BLOCK):
        total = 0.0
        for plain, w_ref in ((plain_0, w_0), (plain_2, w_2)):
            for i in range(3):
                total = total + product(
                    plain[r : r + BLOCK, i * 2 * LANES : i * 2 * LANES + width], w_ref[i * width : (i + 1) * width, :]
                )
        sum_ref[r : r + BLOCK, :] = total
    share(flags_ref, sum_ref, keep_ref, send_ref)
    keep_ref[...] += grad_ref[...]


def last_kernel(keep_ref, got_ref, out_ref):
    out_ref[...] = keep_ref[...] + got_ref[...].astype(F32)


def unpack_kernel(
    flags_ref, part_0, part_1, part_2, part_3,
    query_ref, key_ref, value_ref, out_w_ref, query_b_ref, value_b_ref, up_b_ref, *refs,
):
    vector_refs, parts = refs[:-1], refs[-1]
    for i, ref in enumerate((part_0, part_1, part_2, part_3)):
        parts[jnp.bitwise_xor(flags_ref[4], i)] = ref[...]
    width = query_ref.shape[0]
    for i, ref in enumerate((query_ref, key_ref, value_ref, out_w_ref)):
        ref[...] = parts[i, :width, :].astype(F32)
    tops = [parts[i, width : width + BIAS_ROWS, :].astype(F32) for i in range(4)]
    query_b_ref[...] = tops[0][0, :width]
    value_b_ref[...] = tops[2][0, :width]
    up_b_ref[...] = tops[1][0, :]
    for i, ref in enumerate(vector_refs):
        ref[...] = tops[3][i, :]


def tie(*arrays):
    return lax.optimization_barrier(arrays)


def add(*members):
    members = [m.astype(F32) for m in members]
    while len(members) > 1:
        members = [a + b for a, b in zip(members[::2], members[1::2])]
    return members[0].astype(BF16)


class Swaps:
    def __init__(self, dp_size, replica):
        self.dp_size, self.near = dp_size, replica & 3

    def core(self, values_in):
        return lax.ppermute(values_in, "tensor", [(i, i ^ 1) for i in range(4)])

    def chip(self, values_in):
        return lax.ppermute(values_in, "tensor", [(i, i ^ 2) for i in range(4)])

    def replica(self, values_in, mask):
        return lax.ppermute(values_in, "dp", [(i, i ^ mask) for i in range(self.dp_size)])

    def scatter(self, parts):
        return [self.replica(parts[m], m) for m in (1, 2, 3)]

    def far(self, value, mask):
        return self.replica(value, mask)

    def gather(self, value):
        return [self.replica(value, m) for m in (1, 2, 3)]

    @property
    def far_masks(self):
        return [1 << b for b in range(2, self.dp_size.bit_length() - 1)]

    def placed(self, members):
        return [lax.select_n(self.near, *[members[i ^ p] for p in range(4)]) for i in range(4)]


def cut_pair(value):
    half = value.shape[0] // 2
    return [value[:half], value[half:]]


def cut(value):
    size = value.shape[0] // 4
    return [value[i * size : (i + 1) * size] for i in range(4)]


def first_calls(
    flags, query_bias, value_bias, up_bias, query_weight, key_weight, value_weight, out_weight, up_weight, down_weight,
):
    model, width = query_weight.shape
    far, vmem = pl.BlockSpec(memory_space=pl.ANY), pl.BlockSpec(memory_space=pltpu.VMEM)
    smem = pl.BlockSpec(memory_space=pltpu.SMEM)
    params = dict(
        compiler_params=pltpu.CompilerParams(vmem_limit_bytes=PACK_LIMIT),
        cost_estimate=pl.CostEstimate(flops=0, bytes_accessed=0, transcendentals=0),
    )
    weights = (query_weight.T, key_weight.T, value_weight.T, out_weight)
    shapes = [(width + BIAS_ROWS, model), (width, model)]
    pieces = pl.pallas_call(
        pieces_kernel,
        in_specs=[smem] + [vmem] * 3 + [far] * 4,
        out_specs=[vmem] * 2,
        out_shape=[jax.ShapeDtypeStruct(s, BF16) for s in shapes],
        scratch_shapes=[pltpu.SemaphoreType.DMA((2,))],
        **params,
    )(flags, query_bias, value_bias, up_bias, *weights)
    pieces, weights = tie(pieces, weights)
    halves = [(w.shape[0] // 2, w.shape[1]) for w in (up_weight, down_weight)]
    outs = [(4 * width, model)] + halves
    rest = pl.pallas_call(
        pack_kernel,
        in_specs=[smem] + [far] * 6,
        out_specs=[far] * 3,
        out_shape=[jax.ShapeDtypeStruct(s, BF16) for s in outs],
        scratch_shapes=[pltpu.VMEM(s, BF16) for s in outs] + [pltpu.SemaphoreType.DMA((9,))],
        **params,
    )(flags, *weights, up_weight, down_weight)
    return [*pieces, *rest]


def body(
    dp_size,
    tokens,
    lengths,
    cotangent,
    query_weight,
    query_bias,
    key_weight,
    value_weight,
    value_bias,
    out_weight,
    out_bias,
    gain_one,
    shift_one,
    up_weight,
    up_bias,
    down_weight,
    down_bias,
    gain_two,
    shift_two,
):
    own, model = tokens.shape
    width = query_weight.shape[1]
    units = up_weight.shape[1]
    rows = 2 * own
    place = lax.axis_index("tensor")
    replica = lax.axis_index("dp")
    flags = [(replica ^ (replica >> 1)) & 1, place % 2, place // 2, place, replica & 3, (replica >> 1) & 1, replica & 1]
    flags = jnp.stack(flags).astype(jnp.int32)
    swaps = Swaps(dp_size, replica)
    swap_core, swap_chip, swap_replica = swaps.core, swaps.chip, swaps.replica
    far_masks = swaps.far_masks

    other_tokens = swap_core(tokens)
    pack_a, pack_b, pack, up_half, down_half = first_calls(
        flags, query_bias, value_bias, up_bias, query_weight, key_weight, value_weight, out_weight, up_weight, down_weight
    )
    whole, half_row = (4 * (width + BIAS_ROWS), model), (own, model)
    halves, fourths = [((own // 2, model), BF16)] * 2, [((own // 4, model), BF16)] * 4
    heads_shape = ((3 * width // HEAD_DIM, rows, LANES), BF16)
    values_scratch = pltpu.VMEM((width, rows), BF16)
    kept_shapes = [((width, rows), F32), ((8, rows), F32)]
    direct = [swap_chip(pack_a), swap_chip(pack_b)]
    up_direct, down_direct = swap_chip(up_half), swap_chip(down_half)

    inputs, qkv_0, context_0, turned_0, log_0 = call(
        attend_kernel,
        [((rows, model), BF16), heads_shape, ((rows, width), BF16)] + kept_shapes,
        (flags, lengths, pack, query_bias, value_bias, tokens, other_tokens),
        scalars=2,
        scratch=[values_scratch],
    )
    *direct, inputs = tie(*direct, inputs)
    around = [swap_replica(direct[0], 1), swap_replica(direct[1], 2)]
    *around, inputs = tie(*around, inputs)
    pack_2, qkv_2, turned_2, log_2, bias_2, keep, *sends = call(
        attend_last_kernel,
        [((4 * width, model), BF16), heads_shape] + kept_shapes + [((8, model), F32), (half_row, F32)] + fourths,
        (flags, lengths, *direct, *around, inputs, context_0, pack),
        scalars=2,
        scratch=[values_scratch, pltpu.VMEM((rows, width), BF16), pltpu.VMEM((rows, model), F32)],
    )
    *sends, up_direct = tie(*sends, up_direct)
    got = [swap_core(v) for v in sends]
    fourth = model // 4
    up_around = [swap_replica(up_direct[:fourth], 1), swap_replica(up_direct[fourth:], 2)]
    normal_one, inverse_one, *hidden = call(
        norm_one_kernel,
        [(half_row, F32), ((own, 1), F32)] + fourths,
        (tokens, keep, *got, out_bias, gain_one, shift_one),
        scratch=[pltpu.VMEM(half_row, BF16)] * 2,
    )
    other_hidden = [swap_core(v) for v in hidden]
    hidden[0], down_direct, *held = tie(hidden[0], down_direct, *other_hidden, *up_around)
    other_hidden, up_around = held[:4], held[4:]
    fourth = units // 4
    down_around = [swap_replica(down_direct[:fourth], 1), swap_replica(down_direct[fourth:], 2)]

    act_shapes = [((units, rows), BF16), ((rows, units), BF16)]
    hidden_full, hidden_turned, active_0, slope_0, before = call(
        feed_kernel,
        [((rows, model), BF16), ((model, rows), BF16)] + act_shapes + [((rows, model), F32)],
        (flags, *hidden, *other_hidden, up_weight, down_weight, up_bias),
        scalars=1,
    )
    before, *down_around = tie(before, *down_around)
    up_2, down_2, active_2, slope_2, keep, send = call(
        feed_last_kernel,
        [((model, units), BF16), ((units, model), BF16)] + act_shapes + [(half_row, F32), (half_row, BF16)],
        (flags, hidden_full, up_direct, *up_around, down_direct, *down_around, bias_2, before),
        scalars=1,
        scratch=[pltpu.VMEM((rows, model), F32)],
    )
    layer_output, grad_two, low_grad_two, vector_two = call(
        norm_two_kernel,
        [(half_row, BF16), (half_row, F32), (half_row, BF16), ((8, model), F32)],
        (
            keep, swap_core(send), normal_one, gain_one, shift_one, down_bias,
            gain_two, shift_two, cotangent,
        ),
    )

    back_scratch = [pltpu.VMEM((model, units), BF16), pltpu.VMEM((rows, units), BF16)]
    grad_full, down_theirs = call(
        down_back_kernel,
        [((rows, model), BF16), ((units, model), BF16)],
        (flags, low_grad_two, swap_core(low_grad_two), active_2),
        scalars=1,
    )
    down_theirs, grad_full = tie(down_theirs, grad_full)
    down_chip = swap_chip(down_theirs)
    up_keep_2, *up_sends, up_sum_2, running = call(
        feed_back_theirs_kernel,
        [((model // 2, units), BF16)] + [((model // 2, units // 2), BF16)] * 2 + [((8, units), F32), ((rows, model), F32)],
        (flags, grad_full, slope_2, hidden_turned, up_2, down_2),
        scalars=1,
        scratch=back_scratch,
    )
    down_mine, up_keep_0, *up_sends, up_sum_0, keep, send_0, send_1, send_2, send_3 = call(
        feed_back_mine_kernel,
        [((units, model), BF16), ((model // 2, units), BF16)] + [((model, units // 2), BF16)] * 2
        + [((8, units), F32), (half_row, F32)]
        + [((own // 4, model), BF16)] * 4,
        (
            flags, grad_full, active_0, slope_0, hidden_turned, up_weight, down_weight, running, *up_sends, grad_two,
        ),
        scalars=1,
        scratch=[pltpu.VMEM((rows, model), F32)] + back_scratch,
    )
    up_got = [swap_replica(up_sends[0], 1), swap_replica(up_sends[1], 2)]
    got = [swap_core(v) for v in (send_0, send_1, send_2, send_3)]
    grad_one, low_a, low_b = call(
        norm_one_back_kernel,
        [(half_row, F32), halves[0], ((own // 2 + BIAS_ROWS, model), BF16)],
        (keep, *got, normal_one, inverse_one, gain_one, vector_two),
        scratch=[pltpu.VMEM(half_row, BF16)] * 2 + [pltpu.VMEM((8, model), F32)],
    )
    low_other = [swap_core(low_a), swap_core(low_b)]


    def attend_back(low_a, qkv, turned, log_total, shard, up_sum):
        return call(
            attend_back_kernel,
            [((whole[0], LEFT), BF16), ((whole[0], model - LEFT), BF16), ((rows, 6 * LANES), BF16)],
            (
                flags, low_a, low_b, *low_other, up_sum,
                inputs, qkv, turned, log_total, shard,
            ),
            scalars=1,
            scratch=[
                pltpu.VMEM((rows, model), BF16), pltpu.VMEM((width // HEAD_DIM, rows, LANES), BF16),
                pltpu.VMEM((8, rows), F32), pltpu.VMEM((3 * width, rows), BF16),
                pltpu.VMEM((width // HEAD_DIM, rows, LANES), F32), pltpu.VMEM((width // HEAD_DIM, rows, LANES), F32),
            ],
        )

    left_theirs, right_theirs, plain_2 = attend_back(low_a, qkv_2, turned_2, log_2, pack_2, up_sum_2)

    left_theirs, right_theirs, low_a, down_chip, *up_got = tie(left_theirs, right_theirs, low_a, down_chip, *up_got)
    left_chip, right_chip = swap_chip(left_theirs), swap_chip(right_theirs)
    down_parts = [add(m, t) for m, t in zip(cut(down_mine), cut(down_chip))]
    up_theirs, up_mine = [
        add(keep_up, jnp.concatenate([got_up[here] for got_up in up_got], axis=1))
        for keep_up, here in ((up_keep_2, slice(0, model // 2)), (up_keep_0, slice(model // 2, model)))
    ]
    up_theirs, up_mine, low_a, *down_parts = tie(up_theirs, up_mine, low_a, *down_parts)
    down_got = swaps.scatter(down_parts)
    left_mine, right_mine, plain_0 = attend_back(low_a, qkv_0, turned_0, log_0, pack, up_sum_0)
    keep, send = call(
        tokens_kernel,
        [(half_row, F32), (half_row, BF16)],
        (flags, grad_one, plain_0, plain_2, pack, pack_2),
        scalars=1,
        scratch=[pltpu.VMEM((rows, model), F32)],
    )
    left_mine, keep, send, left_chip, *down_got = tie(left_mine, keep, send, left_chip, *down_got)
    left_parts = [add(m, t) for m, t in zip(cut(left_mine), cut(left_chip))]
    down_now = add(down_parts[0], *down_got)
    down_now, *left_parts = tie(down_now, *left_parts)
    left_got = swaps.scatter(left_parts)
    down_far = swaps.far(down_now, far_masks[0])
    right_chip, right_mine, down_far, up_theirs, *left_got = tie(right_chip, right_mine, down_far, up_theirs, *left_got)
    right_parts = [add(m, t) for m, t in zip(cut(right_mine), cut(right_chip))]
    left_now = add(left_parts[0], *left_got)
    down_now = add(down_now, down_far)
    for mask in far_masks[1:]:
        down_now = add(down_now, swaps.far(down_now, mask))
    left_now, down_now, up_theirs, *right_parts = tie(left_now, down_now, up_theirs, *right_parts)
    right_got = swaps.scatter(right_parts)
    up_chip = swap_chip(up_theirs)
    down_other = swap_replica(down_now, 2)
    up_chip, down_other, *right_got = tie(up_chip, down_other, *right_got)
    pack_now = jnp.concatenate([left_now, add(right_parts[0], *right_got)], axis=1)
    up_now, up_next = [add(m, t) for m, t in zip(cut_pair(up_mine), cut_pair(up_chip))]
    up_next = [up_next[:, : units // 2], up_next[:, units // 2 :]]
    pack_now, up_now, up_next[0], up_next[1], down_other = tie(pack_now, up_now, *up_next, down_other)
    pack_far = swaps.far(pack_now, far_masks[0])
    up_got = [swap_replica(up_next[0], 2), swap_replica(up_next[1], 1)]
    down_pair = jnp.concatenate([down_now, down_other], axis=0)
    down_other = swap_replica(down_pair, 1)
    pack_far, *up_got = tie(pack_far, *up_got)
    pack_now, up_now = add(pack_now, pack_far), add(up_now, jnp.concatenate(up_got, axis=1))
    for mask in far_masks[1:]:
        pack_now = add(pack_now, swaps.far(pack_now, mask))
    pack_now, up_now = tie(pack_now, up_now)
    pack_all = [pack_now] + swaps.gather(pack_now)
    up_far = swaps.far(up_now, far_masks[0])
    up_far, down_other, send = tie(up_far, down_other, send)
    up_now = add(up_now, up_far)
    for mask in far_masks[1:]:
        up_now = add(up_now, swaps.far(up_now, mask))
    up_now, late_flags, send = tie(up_now, flags, send)
    up_all = [up_now] + swaps.gather(up_now)
    (tokens_grad,) = call(last_kernel, [(half_row, F32)], (keep, swap_core(send)))
    first, second = cut_pair(down_pair), cut_pair(down_other)
    down_all = [first[0], second[0], first[1], second[1]]
    down_weight_grad = jnp.concatenate(swaps.placed(down_all), axis=0).astype(F32)
    up_weight_grad = jnp.concatenate(swaps.placed(up_all), axis=0).astype(F32)
    shard = [((width, model), F32)] * 4 + [((width,), F32)] * 2 + [((units,), F32)] + [((model,), F32)] * 6
    (
        query_grad, key_grad, value_grad, out_grad, query_bias_grad, value_bias_grad, up_bias_row, *vectors,
    ) = call(
        unpack_kernel, shard, (late_flags, *pack_all), scalars=1, scratch=[pltpu.VMEM((4, width + BIAS_ROWS, model), BF16)]
    )
    return (
        layer_output,
        tokens_grad,
        query_grad.T,
        query_bias_grad,
        key_grad.T,
        value_grad.T,
        value_bias_grad,
        out_grad,
        vectors[0],
        vectors[1],
        vectors[2],
        up_weight_grad,
        up_bias_row,
        down_weight_grad,
        vectors[5],
        vectors[3],
        vectors[4],
    )


def solution(mesh):
    placed = (
        P(("dp", "tensor"), None),
        P("dp", None),
        P(("dp", "tensor"), None),
        P(None, "tensor"),
        P("tensor"),
        P(None, "tensor"),
        P(None, "tensor"),
        P("tensor"),
        P("tensor", None),
        P(),
        P(),
        P(),
        P(None, "tensor"),
        P("tensor"),
        P("tensor", None),
        P(),
        P(),
        P(),
    )
    return jax.shard_map(
        functools.partial(body, mesh.shape["dp"]),
        mesh=mesh,
        in_specs=placed,
        out_specs=(
            P(("dp", "tensor"), None),
            P(("dp", "tensor"), None),
            P(None, "tensor"),
            P("tensor"),
            P(None, "tensor"),
            P(None, "tensor"),
            P("tensor"),
            P("tensor", None),
            P(),
            P(),
            P(),
            P(None, "tensor"),
            P("tensor"),
            P("tensor", None),
            P(),
            P(),
            P(),
        ),
        check_vma=False,
    )
```

```python
import functools

import jax
import jax.numpy as jnp
from jax import lax
from jax.experimental import pallas as pl
from jax.experimental.pallas import tpu as pltpu
from jax.sharding import PartitionSpec as P

HEAD_DIM = 64
MOST = 256
EPSILON = 1e-05
MASKED = -1e30
BLOCK = 256
STRIP = 64
LANES = 128
BIAS_ROWS = 16
LEFT = 512
VMEM_LIMIT = 16 * 1024 * 1024
PACK_LIMIT = 60 * 1024 * 1024
TAIL_SCALE = 0.425
TAIL = (
    0.23966740682492862,
    0.24201181237516,
    0.19964184258583956,
    0.2585875675603689,
    -0.10985333090134082,
    0.4147788772153898,
    -0.3173079260911745,
    0.07247363954140279,
)

BF16 = jnp.bfloat16
F32 = jnp.float32


def product(left_side, right_side):
    return jnp.dot(left_side, right_side, preferred_element_type=F32)


def rows_product(left_side, right_side):
    return lax.dot_general(
        left_side, right_side, (((0,), (0,)), ((), ())), preferred_element_type=F32
    )


def cols_product(left_side, right_side):
    return lax.dot_general(
        left_side, right_side, (((1,), (1,)), ((), ())), preferred_element_type=F32
    )


def normal_parts(z):
    size = jnp.abs(z)
    t = 1.0 / (1.0 + (TAIL_SCALE * 0.7071067811865476) * size)
    series = TAIL[-1]
    for factor in TAIL[-2::-1]:
        series = series * t + factor
    bell = jnp.exp(-0.5 * z * z)
    tail = (0.5 * bell) * (series * t)
    return jnp.where(z >= 0.0, 1.0 - tail, tail), bell * 0.3989422804014327


def call(kernel, outs, args, scalars=0, scratch=(), cost=1.0, far=()):
    specs = [pl.BlockSpec(memory_space=pltpu.SMEM)] * scalars
    specs += [pl.BlockSpec(memory_space=pltpu.VMEM)] * (len(args) + len(outs) - scalars)
    for i in far:
        specs[i] = pl.BlockSpec(memory_space=pl.ANY)
    outputs = pl.pallas_call(
        kernel,
        in_specs=specs[: len(args)],
        out_specs=specs[len(args) :],
        out_shape=[jax.ShapeDtypeStruct(shape, dtype) for shape, dtype in outs],
        scratch_shapes=list(scratch),
        compiler_params=pltpu.CompilerParams(vmem_limit_bytes=VMEM_LIMIT),
        cost_estimate=pl.CostEstimate(
            flops=0, bytes_accessed=0, transcendentals=0
        ),
    )(*args)
    return list(outputs)


def piece(index, size):
    return pl.ds(pl.multiple_of(index * size, 16), size)


def assemble(side, refs, out_ref):
    size, count = refs[0].shape[0], len(refs) // 2
    for i, ref in enumerate(refs):
        first = side if i < count else 1 - side
        out_ref[piece(first * count + i % count, size), :] = ref[...]


def row(ref):
    return ref[...].reshape(1, -1)


def join_parts(flags_ref, own_refs, other_refs, out_ref):
    for side, parts in ((flags_ref[1], own_refs), (1 - flags_ref[1], other_refs)):
        for i, part in enumerate(parts):
            size = out_ref.shape[0] // (2 * len(parts))
            out_ref[piece(side * len(parts) + i, size), :] = part[:size, :]


def join(flags_ref, own_ref, other_ref, out_ref):
    size = own_ref.shape[0]
    out_ref[piece(flags_ref[1], size), :] = own_ref[...]
    out_ref[piece(1 - flags_ref[1], size), :] = other_ref[...]


def pieces_kernel(
    flags_ref, query_b_ref, value_b_ref, up_b_ref, query_ref, key_ref, value_ref, out_w_ref, near_a, near_b, sems,
):
    weights = (query_ref, key_ref, value_ref, out_w_ref)
    width, model = query_ref.shape
    for side in range(2):

        @pl.when(flags_ref[0] == side)
        def load():
            for k, near in enumerate((near_a, near_b)):
                pltpu.make_async_copy(weights[2 * side + k], near.at[:width], sems.at[k]).start()

    blank = jnp.zeros((1, model - 2 * width), F32)
    rows = []
    for part in (row(up_b_ref), jnp.concatenate([row(query_b_ref), row(value_b_ref), blank], axis=1)):
        for _ in range(3):
            rows.append(part.astype(BF16).astype(F32))
            part = part - rows[-1]
    rows.append(jnp.zeros((BIAS_ROWS - 6, model), F32))
    near_a[width:, :] = jnp.concatenate(rows, axis=0).astype(BF16)
    for k, near in enumerate((near_a, near_b)):
        pltpu.make_async_copy(weights[k], near.at[:width], sems.at[k]).wait()


def pack_kernel(
    flags_ref, query_ref, key_ref, value_ref, out_w_ref, up_ref, down_ref,
    pack_ref, up_out, down_out, pack_near, up_near, down_near, sems,
):
    width = query_ref.shape[0]
    half = up_out.shape[0]
    loads = [(ref.at[piece(flags_ref[0], half)], near) for ref, near in ((up_ref, up_near), (down_ref, down_near))]
    weights = (query_ref, key_ref, value_ref, out_w_ref)
    loads += [(s, pack_near.at[i * width : (i + 1) * width]) for i, s in enumerate(weights)]
    copies = [pltpu.make_async_copy(a, b, sems.at[i]) for i, (a, b) in enumerate(loads)]
    for copy in copies:
        copy.start()
    for copy in copies:
        copy.wait()
    stores = ((up_near, up_out), (down_near, down_out), (pack_near, pack_ref))
    copies = [pltpu.make_async_copy(a, b, sems.at[6 + i]) for i, (a, b) in enumerate(stores)]
    for copy in copies:
        copy.start()
    for copy in copies:
        copy.wait()


def document_lanes(flags_ref, lengths_ref, rows):
    shape = (rows, LANES - HEAD_DIM)
    spot = lax.broadcasted_iota(jnp.int32, shape, 0)
    lane = lax.broadcasted_iota(jnp.int32, (1, shape[1]), 1)
    ends = 0
    begin_row, end_row = jnp.zeros_like(lane), jnp.zeros_like(lane)
    documents = lengths_ref.shape[1]
    for d in range(documents):
        begin_row = jnp.where(lane == d, ends, begin_row)
        ends = ends + lengths_ref[flags_ref[2], d]
        end_row = jnp.where(lane == d, ends, end_row)
    inside = (spot >= begin_row) & (spot < end_row)
    outside = jnp.where(lane < documents, MASKED, 0.0)
    return jnp.where(inside, 1.0, 0.0).astype(BF16), jnp.where(inside, 0.0, outside).astype(BF16)


def window(i, rows):
    return slice(max(i - 1, 0) * BLOCK, min(i + 2, rows // BLOCK) * BLOCK)


def attend_units(
    flags_ref, lengths_ref, x_ref, w_ref, biases, heads_ref, context_ref, turned_ref, log_ref, values_ref,
):
    rows, model = x_ref.shape
    width = context_ref.shape[1]
    heads = width // HEAD_DIM
    same, other = document_lanes(flags_ref, lengths_ref, rows)
    tails = (other, same, jnp.zeros_like(same))
    for i, bias in enumerate((biases[0], None, biases[1])):
        weights = w_ref[i * width : (i + 1) * width, :]
        for r in range(0, rows, 2 * BLOCK):
            here = slice(r, r + 2 * BLOCK)
            total = cols_product(x_ref[here, :], weights)
            if bias is not None:
                total = total + bias
            low = total.astype(BF16)
            if i == 0:
                low = low * BF16(HEAD_DIM**-0.5)
            for h in range(heads):
                part = low[:, h * HEAD_DIM : (h + 1) * HEAD_DIM]
                heads_ref[i * heads + h, here, :] = jnp.concatenate([part, tails[i][here, :]], axis=1)
            if i == 2:
                values_ref[:, here] = low.T
    for i in range(rows // BLOCK):
        here, seen = slice(i * BLOCK, (i + 1) * BLOCK), window(i, rows)
        for h in range(heads):
            part = slice(h * HEAD_DIM, (h + 1) * HEAD_DIM)
            queries = heads_ref[h, here, :]
            steps = range(seen.start, seen.stop, BLOCK)
            scores = [cols_product(heads_ref[heads + h, r : r + BLOCK, :], queries) for r in steps]
            top = functools.reduce(jnp.maximum, [jnp.max(s, axis=0, keepdims=True) for s in scores])
            total, context = 0.0, 0.0
            for r, score in zip(steps, scores):
                weights = jnp.exp(score - top)
                total = total + jnp.sum(weights, axis=0, keepdims=True)
                context = context + product(values_ref[part, r : r + BLOCK], weights.astype(BF16))
            turned_ref[part, here] = context * (1.0 / total)
            log_ref[h : h + 1, here] = top + jnp.log(total)
        context_ref[here, :] = turned_ref[:, here].T.astype(BF16)


def attend_kernel(
    flags_ref, lengths_ref, w_ref, query_b_ref, value_b_ref, tokens_ref, other_ref,
    x_ref, heads_ref, context_ref, turned_ref, log_ref, values_ref,
):
    join(flags_ref, tokens_ref, other_ref, x_ref)
    biases = (row(query_b_ref), row(value_b_ref))
    attend_units(
        flags_ref, lengths_ref, x_ref, w_ref, biases, heads_ref, context_ref, turned_ref, log_ref, values_ref
    )


def share(flags_ref, total_ref, keep_ref, *send_refs):
    size = keep_ref.shape[0]
    keep_ref[...] = total_ref[piece(flags_ref[1], size), :]
    part = size // len(send_refs)
    for i, send_ref in enumerate(send_refs):
        send_ref[...] = total_ref[piece((1 - flags_ref[1]) * len(send_refs) + i, part), :].astype(BF16)


def attend_last_kernel(
    flags_ref, lengths_ref, w_0, w_1, w_2, w_3, x_ref, before_ref, w_before,
    w_ref, heads_ref, turned_ref, log_ref, bias_ref, keep_ref, send_0, send_1, send_2, send_3,
    values_ref, context_ref, mix_ref,
):
    width = context_ref.shape[1]
    side = flags_ref[0] * 2
    for ref, spot in ((w_0, side), (w_1, side + 1), (w_2, 2 - side), (w_3, 3 - side)):
        w_ref[piece(spot, width), :] = ref[:width, :]
    parts = w_0[width : width + BIAS_ROWS, :].astype(F32)
    bias_ref[0:1, :] = parts[0:1] + parts[1:2] + parts[2:3]
    mixed = parts[3:4] + parts[4:5] + parts[5:6]
    biases = (mixed[:, :width], mixed[:, width : 2 * width])
    attend_units(
        flags_ref, lengths_ref, x_ref, w_ref, biases, heads_ref, context_ref, turned_ref, log_ref, values_ref
    )
    for r in range(0, x_ref.shape[0], BLOCK):
        here = slice(r, r + BLOCK)
        mix_ref[here, :] = product(before_ref[here, :], w_before[3 * width :, :]) + product(
            context_ref[here, :], w_ref[3 * width :, :]
        )
    share(flags_ref, mix_ref, keep_ref, send_0, send_1, send_2, send_3)


def strips(rows, step, sums=0, model=0):
    def one(i, carry):
        found = step(pl.ds(pl.multiple_of(i * STRIP, STRIP), STRIP))
        if not sums:
            return carry
        return tuple(c + jnp.sum(f.reshape(STRIP // 8, 8, model), axis=0) for c, f in zip(carry, found))

    first = tuple(jnp.zeros((8, model), F32) for _ in range(sums))
    total = lax.fori_loop(0, rows // STRIP, one, first if sums else 0, unroll=4)
    return [jnp.sum(t, axis=0, keepdims=True) for t in total] if sums else None


def norm_one_kernel(
    tokens_ref, keep_ref, got_0, got_1, got_2, got_3, out_b_ref, gain_ref, shift_ref,
    normal_ref, inverse_ref, hidden_0, hidden_1, hidden_2, hidden_3, got_ref, hidden_ref,
):
    part = got_0.shape[0]
    for i, got in enumerate((got_0, got_1, got_2, got_3)):
        got_ref[i * part : (i + 1) * part, :] = got[...]

    def step(here):
        values = tokens_ref[here, :].astype(F32) + keep_ref[here, :] + got_ref[here, :].astype(F32) + row(out_b_ref)
        centered = values - jnp.mean(values, axis=1, keepdims=True)
        inverse = lax.rsqrt(jnp.mean(centered * centered, axis=1, keepdims=True) + EPSILON)
        normal = centered * inverse
        normal_ref[here, :] = normal
        inverse_ref[here, :] = inverse
        hidden_ref[here, :] = (normal * row(gain_ref) + row(shift_ref)).astype(BF16)

    strips(tokens_ref.shape[0], step)
    for i, hidden in enumerate((hidden_0, hidden_1, hidden_2, hidden_3)):
        hidden[...] = hidden_ref[i * part : (i + 1) * part, :]


def feed_units(hidden_ref, up_ref, down_ref, bias, active_ref, slope_ref, sum_ref, before_ref):
    units = up_ref.shape[1]
    for u in range(0, units, BLOCK):
        for r in range(0, hidden_ref.shape[0], 2 * BLOCK):
            here = slice(r, r + 2 * BLOCK)
            pre_up = bias[:, u : u + BLOCK] + product(hidden_ref[here, :], up_ref[:, u : u + BLOCK])
            cumulative, density = normal_parts(pre_up)
            active = (pre_up * cumulative).astype(BF16)
            active_ref[u : u + BLOCK, here] = active.T
            slope_ref[here, u : u + BLOCK] = (cumulative + pre_up * density).astype(BF16)
            now = product(active, down_ref[u : u + BLOCK, :])
            if u:
                sum_ref[here, :] += now
            elif before_ref is not None:
                sum_ref[here, :] = before_ref[here, :] + now
            else:
                sum_ref[here, :] = now


def feed_kernel(flags_ref, *refs):
    own_refs, other_refs, refs = refs[:4], refs[4:8], refs[8:]
    up_ref, down_ref, bias_ref, hidden_ref, turned_ref, active_ref, slope_ref, sum_ref = refs
    join_parts(flags_ref, own_refs, other_refs, hidden_ref)
    turned_ref[...] = hidden_ref[...].T
    feed_units(hidden_ref, up_ref, down_ref, row(bias_ref), active_ref, slope_ref, sum_ref, None)


def feed_last_kernel(
    flags_ref, hidden_ref, up_a, up_b, up_c, down_a, down_b, down_c, bias_ref, before_ref,
    up_ref, down_ref, active_ref, slope_ref, keep_ref, send_ref, sum_ref,
):
    for (direct, *around), out in (((up_a, up_b, up_c), up_ref), ((down_a, down_b, down_c), down_ref)):
        half = direct.shape[0]
        out[piece(flags_ref[0], half), :] = direct[...]
        for i, ref in enumerate(around):
            out[piece((1 - flags_ref[0]) * 2 + i, half // 2), :] = ref[...]
    feed_units(hidden_ref, up_ref, down_ref, bias_ref[0:1, :], active_ref, slope_ref, sum_ref, before_ref)
    share(flags_ref, sum_ref, keep_ref, send_ref)


def norm_two_kernel(
    keep_ref, got_ref, normal_ref, gain_one_ref, shift_one_ref, down_b_ref, gain_ref, shift_ref, cotangent_ref,
    out_ref, grad_ref, low_ref, vector_ref,
):
    def step(here):
        values = keep_ref[here, :] + got_ref[here, :].astype(F32) + row(down_b_ref)
        values = values + (normal_ref[here, :] * row(gain_one_ref) + row(shift_one_ref))
        centered = values - jnp.mean(values, axis=1, keepdims=True)
        inverse = lax.rsqrt(jnp.mean(centered * centered, axis=1, keepdims=True) + EPSILON)
        normal = centered * inverse
        out_ref[here, :] = (normal * row(gain_ref) + row(shift_ref)).astype(BF16)
        upstream = cotangent_ref[here, :].astype(F32)
        scaled = upstream * row(gain_ref)
        first = jnp.mean(scaled, axis=1, keepdims=True)
        second = jnp.mean(scaled * normal, axis=1, keepdims=True)
        grad = inverse * (scaled - first - normal * second)
        grad_ref[here, :] = grad
        low_ref[here, :] = grad.astype(BF16)
        return upstream * normal, upstream, grad

    rows, model = keep_ref.shape
    vector_ref[...] = jnp.concatenate(strips(rows, step, 3, model) + [jnp.zeros((5, model), F32)], axis=0)


def quarters(flags_ref, size):
    return [pl.ds(pl.multiple_of(jnp.bitwise_xor(flags_ref[4], i) * size, 16), size) for i in range(4)]


def down_back_units(flags_ref, grad_ref, active_ref, down_grad_ref):
    quarter = active_ref.shape[0] // 4
    for i, where in enumerate(quarters(flags_ref, quarter)):
        value = product(active_ref[i * quarter : (i + 1) * quarter, :], grad_ref[...])
        down_grad_ref[where, :] = value.astype(BF16)


def down_back_kernel(flags_ref, own_ref, other_ref, active_ref, grad_ref, down_grad_ref):
    join(flags_ref, own_ref, other_ref, grad_ref)
    down_back_units(flags_ref, grad_ref, active_ref, down_grad_ref)


def feed_back_units(
    flags_ref, grad_ref, slope_ref, hidden_ref, up_ref, down_ref, before_ref, bias_grad_ref, sum_ref, turned_ref, grad_pre_ref,
):
    rows, model = grad_ref.shape
    units = slope_ref.shape[1]
    for u in range(0, units, BLOCK):
        here = slice(u, u + BLOCK)
        total = 0.0
        for r in range(0, rows, 2 * BLOCK):
            grad_active = cols_product(grad_ref[r : r + 2 * BLOCK, :], down_ref[here, :])
            grad_pre = (slope_ref[r : r + 2 * BLOCK, here].astype(F32) * grad_active).astype(BF16)
            grad_pre_ref[r : r + 2 * BLOCK, here] = grad_pre
            total = total + jnp.sum(grad_pre.astype(F32), axis=0, keepdims=True)
            bias_grad_ref[:, here] = jnp.concatenate([total, jnp.zeros((7, total.shape[1]), F32)], axis=0)
    for i, where in enumerate(quarters(flags_ref, model // 4)):
        value = product(hidden_ref[i * (model // 4) : (i + 1) * (model // 4), :], grad_pre_ref[...])
        turned_ref[where, :] = value.astype(BF16)
    for r in range(0, rows, BLOCK):
        value = cols_product(grad_pre_ref[r : r + BLOCK, :], up_ref[...])
        if before_ref is not None:
            value = value + before_ref[r : r + BLOCK, :]
        sum_ref[r : r + BLOCK, :] = value


def split(turned_ref, keep_ref, sends, first):
    quarter, half = turned_ref.shape[0] // 4, turned_ref.shape[1] // 2
    for columns, (stay, go), send in ((slice(0, half), ((0, 2), (1, 3)), 0), (slice(half, 2 * half), ((0, 1), (2, 3)), 1)):
        for i in range(2):
            there = slice(i * quarter, (i + 1) * quarter)
            keep_ref[there, columns] = turned_ref[stay[i] * quarter : (stay[i] + 1) * quarter, columns]
            there = slice(first + i * quarter, first + (i + 1) * quarter)
            sends[send][there, :] = turned_ref[go[i] * quarter : (go[i] + 1) * quarter, columns]


def feed_back_theirs_kernel(
    flags_ref, grad_ref, slope_ref, hidden_ref, up_ref, down_ref,
    keep_up, send_y, send_z, bias_grad_ref, sum_ref, turned_ref, grad_pre_ref,
):
    feed_back_units(
        flags_ref, grad_ref, slope_ref, hidden_ref, up_ref, down_ref, None, bias_grad_ref, sum_ref, turned_ref, grad_pre_ref
    )
    split(turned_ref, keep_up, (send_y, send_z), 0)


def feed_back_mine_kernel(
    flags_ref, grad_ref, active_ref, slope_ref, hidden_ref, up_ref, down_ref, before_ref,
    theirs_y, theirs_z, grad_two_ref, down_grad_ref, keep_up, send_y, send_z, bias_grad_ref, keep_ref, send_0, send_1, send_2, send_3, sum_ref, turned_ref, grad_pre_ref,
):
    down_back_units(flags_ref, grad_ref, active_ref, down_grad_ref)
    feed_back_units(
        flags_ref, grad_ref, slope_ref, hidden_ref, up_ref, down_ref, before_ref,
        bias_grad_ref, sum_ref, turned_ref, grad_pre_ref,
    )
    half = theirs_y.shape[0]
    send_y[:half, :] = theirs_y[...]
    send_z[:half, :] = theirs_z[...]
    split(turned_ref, keep_up, (send_y, send_z), half)
    share(flags_ref, sum_ref, keep_ref, send_0, send_1, send_2, send_3)
    keep_ref[...] += grad_two_ref[...]


def norm_one_back_kernel(
    keep_ref, got_0, got_1, got_2, got_3, normal_ref, inverse_ref, gain_ref, two_ref,
    grad_ref, low_a, low_b, got_ref, low_ref, vector_ref,
):
    part, half = got_0.shape[0], low_a.shape[0]
    for i, got in enumerate((got_0, got_1, got_2, got_3)):
        got_ref[i * part : (i + 1) * part, :] = got[...]

    def step(here):
        upstream, normal = keep_ref[here, :] + got_ref[here, :].astype(F32), normal_ref[here, :]
        scaled = upstream * row(gain_ref)
        first = jnp.mean(scaled, axis=1, keepdims=True)
        second = jnp.mean(scaled * normal, axis=1, keepdims=True)
        grad = inverse_ref[here, :] * (scaled - first - normal * second)
        grad_ref[here, :] = grad
        low_ref[here, :] = grad.astype(BF16)
        return grad, upstream * normal, upstream

    rows, model = keep_ref.shape
    vector_ref[...] = jnp.concatenate(
        strips(rows, step, 3, model) + [two_ref[0:3, :], jnp.zeros((2, model), F32)], axis=0
    )
    low_a[...] = low_ref[:half, :]
    low_b[:half, :] = low_ref[half:, :]
    blank = jnp.zeros((BIAS_ROWS - 8, model), F32)
    low_b[half:, :] = jnp.concatenate([vector_ref[...], blank], axis=0).astype(BF16)


def attend_back_kernel(
    flags_ref, own_a, own_b, other_a, other_b, up_sum_ref,
    x_ref, heads_ref, context_ref, log_ref, w_ref, left_ref, right_ref, plain_ref,
    grad_ref, grad_heads_ref, inner_ref, turned_ref, keys_ref, values_ref,
):
    rows, model = x_ref.shape
    width = context_ref.shape[0]
    heads = width // HEAD_DIM
    size = width + BIAS_ROWS
    half = own_a.shape[0]
    join_parts(flags_ref, (own_a, own_b), (other_a, other_b), grad_ref)
    blank = jnp.zeros((2 * BLOCK, LANES - HEAD_DIM), BF16)
    for r in range(0, rows, 2 * BLOCK):
        here = slice(r, r + 2 * BLOCK)
        low = cols_product(grad_ref[here, :], w_ref[3 * width :, :]).astype(BF16)
        turned = low.T.astype(F32) * context_ref[:, here]
        for h in range(heads):
            part = slice(h * HEAD_DIM, (h + 1) * HEAD_DIM)
            grad_heads_ref[h, here, :] = jnp.concatenate([low[:, part], blank], axis=1)
            inner_ref[h : h + 1, here] = jnp.sum(turned[part, :], axis=0, keepdims=True)
    keys_ref[...] = jnp.zeros_like(keys_ref)
    values_ref[...] = jnp.zeros_like(values_ref)
    for i in range(rows // BLOCK):
        here, seen = slice(i * BLOCK, (i + 1) * BLOCK), window(i, rows)
        for h in range(heads):
            queries, grads, key_rows = heads_ref[h, here, :], grad_heads_ref[h, here, :], heads_ref[heads + h, seen, :]
            probs = jnp.exp(cols_product(key_rows, queries) - log_ref[h : h + 1, here])
            grad_probs = cols_product(heads_ref[2 * heads + h, seen, :], grads)
            grad_scores = (probs * (grad_probs - inner_ref[h : h + 1, here])).astype(BF16)
            values_ref[h, seen, :] += product(probs.astype(BF16), grads)
            keys_ref[h, seen, :] += product(grad_scores, queries)
            grad_queries = rows_product(key_rows, grad_scores)[:HEAD_DIM, :] * (HEAD_DIM**-0.5)
            turned_ref[h * HEAD_DIM : (h + 1) * HEAD_DIM, here] = grad_queries.astype(BF16)
    for i, ref in ((1, keys_ref), (2, values_ref)):
        for h in range(heads):
            first = i * width + h * HEAD_DIM
            turned_ref[first : first + HEAD_DIM, :] = ref[h].T[:HEAD_DIM, :].astype(BF16)
    for i in range(3):
        plain_ref[:, i * 2 * LANES : i * 2 * LANES + width] = turned_ref[i * width : (i + 1) * width, :].T
    tops = [jnp.zeros((8, model), F32)] * 4
    for i in (0, 2):
        top = jnp.sum(plain_ref[:, i * 2 * LANES : i * 2 * LANES + width].astype(F32), axis=0, keepdims=True)
        top = jnp.concatenate([top, jnp.zeros((1, model - width), F32)], axis=1)
        tops[i] = jnp.concatenate([top, jnp.zeros((7, model), F32)], axis=0)
    tops[1] = up_sum_ref[...]
    vectors = [ref[half : half + BIAS_ROWS, :].astype(F32)[:8] for ref in (own_b, other_b)]
    tops[3] = vectors[0] + vectors[1]
    for i, here in enumerate(quarters(flags_ref, size)):
        if i < 3:
            grad = product(turned_ref[i * width : (i + 1) * width, :], x_ref[...])
        else:
            grad = product(context_ref[...].astype(BF16), grad_ref[...])
        blank = jnp.zeros((BIAS_ROWS - 8, model), F32)
        value = jnp.concatenate([grad, tops[i], blank], axis=0).astype(BF16)
        left_ref[here, :] = value[:, :LEFT]
        right_ref[here, :] = value[:, LEFT:]


def tokens_kernel(flags_ref, grad_ref, plain_0, plain_2, w_0, w_2, keep_ref, send_ref, sum_ref):
    rows, model = plain_0.shape[0], grad_ref.shape[1]
    width = w_0.shape[0] // 4
    for r in range(0, rows, BLOCK):
        total = 0.0
        for plain, w_ref in ((plain_0, w_0), (plain_2, w_2)):
            for i in range(3):
                total = total + product(
                    plain[r : r + BLOCK, i * 2 * LANES : i * 2 * LANES + width], w_ref[i * width : (i + 1) * width, :]
                )
        sum_ref[r : r + BLOCK, :] = total
    share(flags_ref, sum_ref, keep_ref, send_ref)
    keep_ref[...] += grad_ref[...]


def last_kernel(keep_ref, got_ref, out_ref):
    out_ref[...] = keep_ref[...] + got_ref[...].astype(F32)


def unpack_kernel(
    flags_ref, part_0, part_1, part_2, part_3,
    query_ref, key_ref, value_ref, out_w_ref, query_b_ref, value_b_ref, up_b_ref, *refs,
):
    vector_refs, parts = refs[:-1], refs[-1]
    for i, ref in enumerate((part_0, part_1, part_2, part_3)):
        parts[jnp.bitwise_xor(flags_ref[4], i)] = ref[...]
    width = query_ref.shape[0]
    for i, ref in enumerate((query_ref, key_ref, value_ref, out_w_ref)):
        ref[...] = parts[i, :width, :].astype(F32)
    tops = [parts[i, width : width + BIAS_ROWS, :].astype(F32) for i in range(4)]
    query_b_ref[...] = tops[0][0, :width]
    value_b_ref[...] = tops[2][0, :width]
    up_b_ref[...] = tops[1][0, :]
    for i, ref in enumerate(vector_refs):
        ref[...] = tops[3][i, :]


def tie(*arrays):
    return lax.optimization_barrier(arrays)


def add(*members):
    members = [m.astype(F32) for m in members]
    while len(members) > 1:
        members = [a + b for a, b in zip(members[::2], members[1::2])]
    return members[0].astype(BF16)


class Swaps:
    def __init__(self, dp_size, replica):
        self.dp_size, self.near = dp_size, replica & 3

    def core(self, values_in):
        return lax.ppermute(values_in, "tensor", [(i, i ^ 1) for i in range(4)])

    def chip(self, values_in):
        return lax.ppermute(values_in, "tensor", [(i, i ^ 2) for i in range(4)])

    def replica(self, values_in, mask):
        return lax.ppermute(values_in, "dp", [(i, i ^ mask) for i in range(self.dp_size)])

    def scatter(self, parts):
        got = {m: self.replica(parts[m], m) for m in (3, 1, 2)}
        return [got[m] for m in (1, 2, 3)]

    def far(self, value, mask):
        return self.replica(value, mask)

    def gather(self, value):
        got = {m: self.replica(value, m) for m in (3, 1, 2)}
        return [got[m] for m in (1, 2, 3)]

    @property
    def far_masks(self):
        return [1 << b for b in range(2, self.dp_size.bit_length() - 1)]

    def placed(self, members):
        return [lax.select_n(self.near, *[members[i ^ p] for p in range(4)]) for i in range(4)]


def cut_pair(value):
    half = value.shape[0] // 2
    return [value[:half], value[half:]]


def cut(value):
    size = value.shape[0] // 4
    return [value[i * size : (i + 1) * size] for i in range(4)]


def first_calls(
    flags, query_bias, value_bias, up_bias, query_weight, key_weight, value_weight, out_weight, up_weight, down_weight,
):
    model, width = query_weight.shape
    far, vmem = pl.BlockSpec(memory_space=pl.ANY), pl.BlockSpec(memory_space=pltpu.VMEM)
    smem = pl.BlockSpec(memory_space=pltpu.SMEM)
    params = dict(
        compiler_params=pltpu.CompilerParams(vmem_limit_bytes=PACK_LIMIT),
        cost_estimate=pl.CostEstimate(flops=0, bytes_accessed=0, transcendentals=0),
    )
    weights = (query_weight.T, key_weight.T, value_weight.T, out_weight)
    shapes = [(width + BIAS_ROWS, model), (width, model)]
    pieces = pl.pallas_call(
        pieces_kernel,
        in_specs=[smem] + [vmem] * 3 + [far] * 4,
        out_specs=[vmem] * 2,
        out_shape=[jax.ShapeDtypeStruct(s, BF16) for s in shapes],
        scratch_shapes=[pltpu.SemaphoreType.DMA((2,))],
        **params,
    )(flags, query_bias, value_bias, up_bias, *weights)
    pieces, weights = tie(pieces, weights)
    halves = [(w.shape[0] // 2, w.shape[1]) for w in (up_weight, down_weight)]
    outs = [(4 * width, model)] + halves
    rest = pl.pallas_call(
        pack_kernel,
        in_specs=[smem] + [far] * 6,
        out_specs=[far] * 3,
        out_shape=[jax.ShapeDtypeStruct(s, BF16) for s in outs],
        scratch_shapes=[pltpu.VMEM(s, BF16) for s in outs] + [pltpu.SemaphoreType.DMA((9,))],
        **params,
    )(flags, *weights, up_weight, down_weight)
    return [*pieces, *rest]


def body(
    dp_size,
    tokens,
    lengths,
    cotangent,
    query_weight,
    query_bias,
    key_weight,
    value_weight,
    value_bias,
    out_weight,
    out_bias,
    gain_one,
    shift_one,
    up_weight,
    up_bias,
    down_weight,
    down_bias,
    gain_two,
    shift_two,
):
    own, model = tokens.shape
    width = query_weight.shape[1]
    units = up_weight.shape[1]
    rows = 2 * own
    place = lax.axis_index("tensor")
    replica = lax.axis_index("dp")
    flags = [(replica ^ (replica >> 1)) & 1, place % 2, place // 2, place, replica & 3, (replica >> 1) & 1, replica & 1]
    flags = jnp.stack(flags).astype(jnp.int32)
    swaps = Swaps(dp_size, replica)
    swap_core, swap_chip, swap_replica = swaps.core, swaps.chip, swaps.replica
    far_masks = swaps.far_masks

    other_tokens = swap_core(tokens)
    pack_a, pack_b, pack, up_half, down_half = first_calls(
        flags, query_bias, value_bias, up_bias, query_weight, key_weight, value_weight, out_weight, up_weight, down_weight
    )
    whole, half_row = (4 * (width + BIAS_ROWS), model), (own, model)
    halves, fourths = [((own // 2, model), BF16)] * 2, [((own // 4, model), BF16)] * 4
    heads_shape = ((3 * width // HEAD_DIM, rows, LANES), BF16)
    values_scratch = pltpu.VMEM((width, rows), BF16)
    kept_shapes = [((width, rows), F32), ((8, rows), F32)]
    direct = [swap_chip(pack_a), swap_chip(pack_b)]
    up_direct, down_direct = swap_chip(up_half), swap_chip(down_half)

    inputs, qkv_0, context_0, turned_0, log_0 = call(
        attend_kernel,
        [((rows, model), BF16), heads_shape, ((rows, width), BF16)] + kept_shapes,
        (flags, lengths, pack, query_bias, value_bias, tokens, other_tokens),
        scalars=2,
        scratch=[values_scratch],
    )
    *direct, inputs = tie(*direct, inputs)
    around = [swap_replica(direct[0], 1), swap_replica(direct[1], 2)]
    *around, inputs = tie(*around, inputs)
    pack_2, qkv_2, turned_2, log_2, bias_2, keep, *sends = call(
        attend_last_kernel,
        [((4 * width, model), BF16), heads_shape] + kept_shapes + [((8, model), F32), (half_row, F32)] + fourths,
        (flags, lengths, *direct, *around, inputs, context_0, pack),
        scalars=2,
        scratch=[values_scratch, pltpu.VMEM((rows, width), BF16), pltpu.VMEM((rows, model), F32)],
    )
    *sends, up_direct = tie(*sends, up_direct)
    got = [swap_core(v) for v in sends]
    fourth = model // 4
    up_around = [swap_replica(up_direct[:fourth], 1), swap_replica(up_direct[fourth:], 2)]
    normal_one, inverse_one, *hidden = call(
        norm_one_kernel,
        [(half_row, F32), ((own, 1), F32)] + fourths,
        (tokens, keep, *got, out_bias, gain_one, shift_one),
        scratch=[pltpu.VMEM(half_row, BF16)] * 2,
    )
    other_hidden = [swap_core(v) for v in hidden]
    hidden[0], down_direct, *held = tie(hidden[0], down_direct, *other_hidden, *up_around)
    other_hidden, up_around = held[:4], held[4:]
    fourth = units // 4
    down_around = [swap_replica(down_direct[:fourth], 1), swap_replica(down_direct[fourth:], 2)]

    act_shapes = [((units, rows), BF16), ((rows, units), BF16)]
    hidden_full, hidden_turned, active_0, slope_0, before = call(
        feed_kernel,
        [((rows, model), BF16), ((model, rows), BF16)] + act_shapes + [((rows, model), F32)],
        (flags, *hidden, *other_hidden, up_weight, down_weight, up_bias),
        scalars=1,
    )
    before, *down_around = tie(before, *down_around)
    up_2, down_2, active_2, slope_2, keep, send = call(
        feed_last_kernel,
        [((model, units), BF16), ((units, model), BF16)] + act_shapes + [(half_row, F32), (half_row, BF16)],
        (flags, hidden_full, up_direct, *up_around, down_direct, *down_around, bias_2, before),
        scalars=1,
        scratch=[pltpu.VMEM((rows, model), F32)],
    )
    layer_output, grad_two, low_grad_two, vector_two = call(
        norm_two_kernel,
        [(half_row, BF16), (half_row, F32), (half_row, BF16), ((8, model), F32)],
        (
            keep, swap_core(send), normal_one, gain_one, shift_one, down_bias,
            gain_two, shift_two, cotangent,
        ),
    )

    back_scratch = [pltpu.VMEM((model, units), BF16), pltpu.VMEM((rows, units), BF16)]
    grad_full, down_theirs = call(
        down_back_kernel,
        [((rows, model), BF16), ((units, model), BF16)],
        (flags, low_grad_two, swap_core(low_grad_two), active_2),
        scalars=1,
    )
    down_theirs, grad_full = tie(down_theirs, grad_full)
    down_chip = swap_chip(down_theirs)
    up_keep_2, *up_sends, up_sum_2, running = call(
        feed_back_theirs_kernel,
        [((model // 2, units), BF16)] + [((model // 2, units // 2), BF16)] * 2 + [((8, units), F32), ((rows, model), F32)],
        (flags, grad_full, slope_2, hidden_turned, up_2, down_2),
        scalars=1,
        scratch=back_scratch,
    )
    down_mine, up_keep_0, *up_sends, up_sum_0, keep, send_0, send_1, send_2, send_3 = call(
        feed_back_mine_kernel,
        [((units, model), BF16), ((model // 2, units), BF16)] + [((model, units // 2), BF16)] * 2
        + [((8, units), F32), (half_row, F32)]
        + [((own // 4, model), BF16)] * 4,
        (
            flags, grad_full, active_0, slope_0, hidden_turned, up_weight, down_weight, running, *up_sends, grad_two,
        ),
        scalars=1,
        scratch=[pltpu.VMEM((rows, model), F32)] + back_scratch,
    )
    up_got = [swap_replica(up_sends[0], 1), swap_replica(up_sends[1], 2)]
    got = [swap_core(v) for v in (send_0, send_1, send_2, send_3)]
    grad_one, low_a, low_b = call(
        norm_one_back_kernel,
        [(half_row, F32), halves[0], ((own // 2 + BIAS_ROWS, model), BF16)],
        (keep, *got, normal_one, inverse_one, gain_one, vector_two),
        scratch=[pltpu.VMEM(half_row, BF16)] * 2 + [pltpu.VMEM((8, model), F32)],
    )
    low_other = [swap_core(low_a), swap_core(low_b)]


    def attend_back(low_a, qkv, turned, log_total, shard, up_sum):
        return call(
            attend_back_kernel,
            [((whole[0], LEFT), BF16), ((whole[0], model - LEFT), BF16), ((rows, 6 * LANES), BF16)],
            (
                flags, low_a, low_b, *low_other, up_sum,
                inputs, qkv, turned, log_total, shard,
            ),
            scalars=1,
            scratch=[
                pltpu.VMEM((rows, model), BF16), pltpu.VMEM((width // HEAD_DIM, rows, LANES), BF16),
                pltpu.VMEM((8, rows), F32), pltpu.VMEM((3 * width, rows), BF16),
                pltpu.VMEM((width // HEAD_DIM, rows, LANES), F32), pltpu.VMEM((width // HEAD_DIM, rows, LANES), F32),
            ],
        )

    left_theirs, right_theirs, plain_2 = attend_back(low_a, qkv_2, turned_2, log_2, pack_2, up_sum_2)

    left_theirs, right_theirs, low_a, down_chip, *up_got = tie(left_theirs, right_theirs, low_a, down_chip, *up_got)
    left_chip, right_chip = swap_chip(left_theirs), swap_chip(right_theirs)
    down_parts = [add(m, t) for m, t in zip(cut(down_mine), cut(down_chip))]
    up_theirs, up_mine = [
        add(keep_up, jnp.concatenate([got_up[here] for got_up in up_got], axis=1))
        for keep_up, here in ((up_keep_2, slice(0, model // 2)), (up_keep_0, slice(model // 2, model)))
    ]
    up_theirs, up_mine, low_a, *down_parts = tie(up_theirs, up_mine, low_a, *down_parts)
    down_got = swaps.scatter(down_parts)
    left_mine, right_mine, plain_0 = attend_back(low_a, qkv_0, turned_0, log_0, pack, up_sum_0)
    keep, send = call(
        tokens_kernel,
        [(half_row, F32), (half_row, BF16)],
        (flags, grad_one, plain_0, plain_2, pack, pack_2),
        scalars=1,
        scratch=[pltpu.VMEM((rows, model), F32)],
    )
    left_mine, keep, send, left_chip, *down_got = tie(left_mine, keep, send, left_chip, *down_got)
    left_parts = [add(m, t) for m, t in zip(cut(left_mine), cut(left_chip))]
    down_now = add(down_parts[0], *down_got)
    down_now, *left_parts = tie(down_now, *left_parts)
    left_got = swaps.scatter(left_parts)
    down_far = swaps.far(down_now, far_masks[0])
    right_chip, right_mine, down_far, up_theirs, *left_got = tie(right_chip, right_mine, down_far, up_theirs, *left_got)
    right_parts = [add(m, t) for m, t in zip(cut(right_mine), cut(right_chip))]
    left_now = add(left_parts[0], *left_got)
    down_now = add(down_now, down_far)
    for mask in far_masks[1:]:
        down_now = add(down_now, swaps.far(down_now, mask))
    left_now, down_now, up_theirs, *right_parts = tie(left_now, down_now, up_theirs, *right_parts)
    right_got = swaps.scatter(right_parts)
    up_chip = swap_chip(up_theirs)
    down_other = swap_replica(down_now, 2)
    up_chip, down_other, *right_got = tie(up_chip, down_other, *right_got)
    pack_now = jnp.concatenate([left_now, add(right_parts[0], *right_got)], axis=1)
    up_now, up_next = [add(m, t) for m, t in zip(cut_pair(up_mine), cut_pair(up_chip))]
    up_next = [up_next[:, : units // 2], up_next[:, units // 2 :]]
    pack_now, up_now, up_next[0], up_next[1], down_other = tie(pack_now, up_now, *up_next, down_other)
    pack_far = swaps.far(pack_now, far_masks[0])
    up_got = [swap_replica(up_next[0], 2), swap_replica(up_next[1], 1)]
    down_pair = jnp.concatenate([down_now, down_other], axis=0)
    down_other = swap_replica(down_pair, 1)
    pack_far, *up_got = tie(pack_far, *up_got)
    pack_now, up_now = add(pack_now, pack_far), add(up_now, jnp.concatenate(up_got, axis=1))
    for mask in far_masks[1:]:
        pack_now = add(pack_now, swaps.far(pack_now, mask))
    pack_now, up_now = tie(pack_now, up_now)
    pack_all = [pack_now] + swaps.gather(pack_now)
    up_far = swaps.far(up_now, far_masks[0])
    up_far, down_other, send = tie(up_far, down_other, send)
    up_now = add(up_now, up_far)
    for mask in far_masks[1:]:
        up_now = add(up_now, swaps.far(up_now, mask))
    up_now, late_flags, send = tie(up_now, flags, send)
    up_all = [up_now] + swaps.gather(up_now)
    (tokens_grad,) = call(last_kernel, [(half_row, F32)], (keep, swap_core(send)))
    first, second = cut_pair(down_pair), cut_pair(down_other)
    down_all = [first[0], second[0], first[1], second[1]]
    down_weight_grad = jnp.concatenate(swaps.placed(down_all), axis=0).astype(F32)
    up_weight_grad = jnp.concatenate(swaps.placed(up_all), axis=0).astype(F32)
    shard = [((width, model), F32)] * 4 + [((width,), F32)] * 2 + [((units,), F32)] + [((model,), F32)] * 6
    (
        query_grad, key_grad, value_grad, out_grad, query_bias_grad, value_bias_grad, up_bias_row, *vectors,
    ) = call(
        unpack_kernel, shard, (late_flags, *pack_all), scalars=1, scratch=[pltpu.VMEM((4, width + BIAS_ROWS, model), BF16)]
    )
    return (
        layer_output,
        tokens_grad,
        query_grad.T,
        query_bias_grad,
        key_grad.T,
        value_grad.T,
        value_bias_grad,
        out_grad,
        vectors[0],
        vectors[1],
        vectors[2],
        up_weight_grad,
        up_bias_row,
        down_weight_grad,
        vectors[5],
        vectors[3],
        vectors[4],
    )


def solution(mesh):
    placed = (
        P(("dp", "tensor"), None),
        P("dp", None),
        P(("dp", "tensor"), None),
        P(None, "tensor"),
        P("tensor"),
        P(None, "tensor"),
        P(None, "tensor"),
        P("tensor"),
        P("tensor", None),
        P(),
        P(),
        P(),
        P(None, "tensor"),
        P("tensor"),
        P("tensor", None),
        P(),
        P(),
        P(),
    )
    return jax.shard_map(
        functools.partial(body, mesh.shape["dp"]),
        mesh=mesh,
        in_specs=placed,
        out_specs=(
            P(("dp", "tensor"), None),
            P(("dp", "tensor"), None),
            P(None, "tensor"),
            P("tensor"),
            P(None, "tensor"),
            P(None, "tensor"),
            P("tensor"),
            P("tensor", None),
            P(),
            P(),
            P(),
            P(None, "tensor"),
            P("tensor"),
            P("tensor", None),
            P(),
            P(),
            P(),
        ),
        check_vma=False,
    )
```

```python
import functools

import jax
import jax.numpy as jnp
from jax import lax
from jax.experimental import pallas as pl
from jax.experimental.pallas import tpu as pltpu
from jax.sharding import PartitionSpec as P

HEAD_DIM = 64
MOST = 256
EPSILON = 1e-05
MASKED = -1e30
BLOCK = 256
STRIP = 64
LANES = 128
BIAS_ROWS = 16
LEFT = 512
VMEM_LIMIT = 16 * 1024 * 1024
PACK_LIMIT = 60 * 1024 * 1024
TAIL_SCALE = 0.425
TAIL = (
    0.23966740682492862,
    0.24201181237516,
    0.19964184258583956,
    0.2585875675603689,
    -0.10985333090134082,
    0.4147788772153898,
    -0.3173079260911745,
    0.07247363954140279,
)

BF16 = jnp.bfloat16
F32 = jnp.float32


def product(left_side, right_side):
    return jnp.dot(left_side, right_side, preferred_element_type=F32)


def rows_product(left_side, right_side):
    return lax.dot_general(
        left_side, right_side, (((0,), (0,)), ((), ())), preferred_element_type=F32
    )


def cols_product(left_side, right_side):
    return lax.dot_general(
        left_side, right_side, (((1,), (1,)), ((), ())), preferred_element_type=F32
    )


def normal_parts(z):
    size = jnp.abs(z)
    t = 1.0 / (1.0 + (TAIL_SCALE * 0.7071067811865476) * size)
    series = TAIL[-1]
    for factor in TAIL[-2::-1]:
        series = series * t + factor
    bell = jnp.exp(-0.5 * z * z)
    tail = (0.5 * bell) * (series * t)
    return jnp.where(z >= 0.0, 1.0 - tail, tail), bell * 0.3989422804014327


def call(kernel, outs, args, scalars=0, scratch=(), cost=1.0, far=()):
    specs = [pl.BlockSpec(memory_space=pltpu.SMEM)] * scalars
    specs += [pl.BlockSpec(memory_space=pltpu.VMEM)] * (len(args) + len(outs) - scalars)
    for i in far:
        specs[i] = pl.BlockSpec(memory_space=pl.ANY)
    outputs = pl.pallas_call(
        kernel,
        in_specs=specs[: len(args)],
        out_specs=specs[len(args) :],
        out_shape=[jax.ShapeDtypeStruct(shape, dtype) for shape, dtype in outs],
        scratch_shapes=list(scratch),
        compiler_params=pltpu.CompilerParams(vmem_limit_bytes=VMEM_LIMIT),
        cost_estimate=pl.CostEstimate(
            flops=0, bytes_accessed=0, transcendentals=0
        ),
    )(*args)
    return list(outputs)


def piece(index, size):
    return pl.ds(pl.multiple_of(index * size, 16), size)


def assemble(side, refs, out_ref):
    size, count = refs[0].shape[0], len(refs) // 2
    for i, ref in enumerate(refs):
        first = side if i < count else 1 - side
        out_ref[piece(first * count + i % count, size), :] = ref[...]


def row(ref):
    return ref[...].reshape(1, -1)


def join_parts(flags_ref, own_refs, other_refs, out_ref):
    for side, parts in ((flags_ref[1], own_refs), (1 - flags_ref[1], other_refs)):
        for i, part in enumerate(parts):
            size = out_ref.shape[0] // (2 * len(parts))
            out_ref[piece(side * len(parts) + i, size), :] = part[:size, :]


def join(flags_ref, own_ref, other_ref, out_ref):
    size = own_ref.shape[0]
    out_ref[piece(flags_ref[1], size), :] = own_ref[...]
    out_ref[piece(1 - flags_ref[1], size), :] = other_ref[...]


def pieces_kernel(
    flags_ref, query_b_ref, value_b_ref, up_b_ref, query_ref, key_ref, value_ref, out_w_ref, near_a, near_b, sems,
):
    weights = (query_ref, key_ref, value_ref, out_w_ref)
    width, model = query_ref.shape
    for side in range(2):

        @pl.when(flags_ref[0] == side)
        def load():
            for k, near in enumerate((near_a, near_b)):
                pltpu.make_async_copy(weights[2 * side + k], near.at[:width], sems.at[k]).start()

    blank = jnp.zeros((1, model - 2 * width), F32)
    rows = []
    for part in (row(up_b_ref), jnp.concatenate([row(query_b_ref), row(value_b_ref), blank], axis=1)):
        for _ in range(3):
            rows.append(part.astype(BF16).astype(F32))
            part = part - rows[-1]
    rows.append(jnp.zeros((BIAS_ROWS - 6, model), F32))
    near_a[width:, :] = jnp.concatenate(rows, axis=0).astype(BF16)
    for k, near in enumerate((near_a, near_b)):
        pltpu.make_async_copy(weights[k], near.at[:width], sems.at[k]).wait()


def pack_kernel(
    flags_ref, query_ref, key_ref, value_ref, out_w_ref, up_ref, down_ref,
    pack_ref, up_out, down_out, pack_near, up_near, down_near, sems,
):
    width = query_ref.shape[0]
    half = up_out.shape[0]
    loads = [(ref.at[piece(flags_ref[0], half)], near) for ref, near in ((up_ref, up_near), (down_ref, down_near))]
    weights = (query_ref, key_ref, value_ref, out_w_ref)
    loads += [(s, pack_near.at[i * width : (i + 1) * width]) for i, s in enumerate(weights)]
    copies = [pltpu.make_async_copy(a, b, sems.at[i]) for i, (a, b) in enumerate(loads)]
    for copy in copies:
        copy.start()
    for copy in copies:
        copy.wait()
    stores = ((up_near, up_out), (down_near, down_out), (pack_near, pack_ref))
    copies = [pltpu.make_async_copy(a, b, sems.at[6 + i]) for i, (a, b) in enumerate(stores)]
    for copy in copies:
        copy.start()
    for copy in copies:
        copy.wait()


def document_lanes(flags_ref, lengths_ref, rows):
    shape = (rows, LANES - HEAD_DIM)
    spot = lax.broadcasted_iota(jnp.int32, shape, 0)
    lane = lax.broadcasted_iota(jnp.int32, (1, shape[1]), 1)
    ends = 0
    begin_row, end_row = jnp.zeros_like(lane), jnp.zeros_like(lane)
    documents = lengths_ref.shape[1]
    for d in range(documents):
        begin_row = jnp.where(lane == d, ends, begin_row)
        ends = ends + lengths_ref[flags_ref[2], d]
        end_row = jnp.where(lane == d, ends, end_row)
    inside = (spot >= begin_row) & (spot < end_row)
    outside = jnp.where(lane < documents, MASKED, 0.0)
    return jnp.where(inside, 1.0, 0.0).astype(BF16), jnp.where(inside, 0.0, outside).astype(BF16)


def window(i, rows):
    return slice(max(i - 1, 0) * BLOCK, min(i + 2, rows // BLOCK) * BLOCK)


def attend_units(
    flags_ref, lengths_ref, x_ref, w_ref, biases, heads_ref, context_ref, turned_ref, log_ref, values_ref,
):
    rows, model = x_ref.shape
    width = context_ref.shape[1]
    heads = width // HEAD_DIM
    same, other = document_lanes(flags_ref, lengths_ref, rows)
    tails = (other, same, jnp.zeros_like(same))
    for i, bias in enumerate((biases[0], None, biases[1])):
        weights = w_ref[i * width : (i + 1) * width, :]
        for r in range(0, rows, 2 * BLOCK):
            here = slice(r, r + 2 * BLOCK)
            total = cols_product(x_ref[here, :], weights)
            if bias is not None:
                total = total + bias
            low = total.astype(BF16)
            if i == 0:
                low = low * BF16(HEAD_DIM**-0.5)
            for h in range(heads):
                part = low[:, h * HEAD_DIM : (h + 1) * HEAD_DIM]
                heads_ref[i * heads + h, here, :] = jnp.concatenate([part, tails[i][here, :]], axis=1)
            if i == 2:
                values_ref[:, here] = low.T
    for i in range(rows // BLOCK):
        here, seen = slice(i * BLOCK, (i + 1) * BLOCK), window(i, rows)
        for h in range(heads):
            part = slice(h * HEAD_DIM, (h + 1) * HEAD_DIM)
            queries = heads_ref[h, here, :]
            steps = range(seen.start, seen.stop, BLOCK)
            scores = [cols_product(heads_ref[heads + h, r : r + BLOCK, :], queries) for r in steps]
            top = functools.reduce(jnp.maximum, [jnp.max(s, axis=0, keepdims=True) for s in scores])
            total, context = 0.0, 0.0
            for r, score in zip(steps, scores):
                weights = jnp.exp(score - top)
                total = total + jnp.sum(weights, axis=0, keepdims=True)
                context = context + product(values_ref[part, r : r + BLOCK], weights.astype(BF16))
            turned_ref[part, here] = context * (1.0 / total)
            log_ref[h : h + 1, here] = top + jnp.log(total)
        context_ref[here, :] = turned_ref[:, here].T.astype(BF16)


def attend_kernel(
    flags_ref, lengths_ref, w_ref, query_b_ref, value_b_ref, tokens_ref, other_ref,
    x_ref, heads_ref, context_ref, turned_ref, log_ref, values_ref,
):
    join(flags_ref, tokens_ref, other_ref, x_ref)
    biases = (row(query_b_ref), row(value_b_ref))
    attend_units(
        flags_ref, lengths_ref, x_ref, w_ref, biases, heads_ref, context_ref, turned_ref, log_ref, values_ref
    )


def share(flags_ref, total_ref, keep_ref, *send_refs):
    size = keep_ref.shape[0]
    keep_ref[...] = total_ref[piece(flags_ref[1], size), :]
    part = size // len(send_refs)
    for i, send_ref in enumerate(send_refs):
        send_ref[...] = total_ref[piece((1 - flags_ref[1]) * len(send_refs) + i, part), :].astype(BF16)


def attend_last_kernel(
    flags_ref, lengths_ref, w_0, w_1, w_2, w_3, x_ref, before_ref, w_before,
    w_ref, heads_ref, turned_ref, log_ref, bias_ref, keep_ref, send_0, send_1, send_2, send_3,
    values_ref, context_ref, mix_ref,
):
    width = context_ref.shape[1]
    side = flags_ref[0] * 2
    for ref, spot in ((w_0, side), (w_1, side + 1), (w_2, 2 - side), (w_3, 3 - side)):
        w_ref[piece(spot, width), :] = ref[:width, :]
    parts = w_0[width : width + BIAS_ROWS, :].astype(F32)
    bias_ref[0:1, :] = parts[0:1] + parts[1:2] + parts[2:3]
    mixed = parts[3:4] + parts[4:5] + parts[5:6]
    biases = (mixed[:, :width], mixed[:, width : 2 * width])
    attend_units(
        flags_ref, lengths_ref, x_ref, w_ref, biases, heads_ref, context_ref, turned_ref, log_ref, values_ref
    )
    for r in range(0, x_ref.shape[0], BLOCK):
        here = slice(r, r + BLOCK)
        mix_ref[here, :] = product(before_ref[here, :], w_before[3 * width :, :]) + product(
            context_ref[here, :], w_ref[3 * width :, :]
        )
    share(flags_ref, mix_ref, keep_ref, send_0, send_1, send_2, send_3)


def strips(rows, step, sums=0, model=0):
    def one(i, carry):
        found = step(pl.ds(pl.multiple_of(i * STRIP, STRIP), STRIP))
        if not sums:
            return carry
        return tuple(c + jnp.sum(f.reshape(STRIP // 8, 8, model), axis=0) for c, f in zip(carry, found))

    first = tuple(jnp.zeros((8, model), F32) for _ in range(sums))
    total = lax.fori_loop(0, rows // STRIP, one, first if sums else 0, unroll=4)
    return [jnp.sum(t, axis=0, keepdims=True) for t in total] if sums else None


def norm_one_kernel(
    tokens_ref, keep_ref, got_0, got_1, got_2, got_3, out_b_ref, gain_ref, shift_ref,
    normal_ref, inverse_ref, hidden_0, hidden_1, hidden_2, hidden_3, got_ref, hidden_ref,
):
    part = got_0.shape[0]
    for i, got in enumerate((got_0, got_1, got_2, got_3)):
        got_ref[i * part : (i + 1) * part, :] = got[...]

    def step(here):
        values = tokens_ref[here, :].astype(F32) + keep_ref[here, :] + got_ref[here, :].astype(F32) + row(out_b_ref)
        centered = values - jnp.mean(values, axis=1, keepdims=True)
        inverse = lax.rsqrt(jnp.mean(centered * centered, axis=1, keepdims=True) + EPSILON)
        normal = centered * inverse
        normal_ref[here, :] = normal
        inverse_ref[here, :] = inverse
        hidden_ref[here, :] = (normal * row(gain_ref) + row(shift_ref)).astype(BF16)

    strips(tokens_ref.shape[0], step)
    for i, hidden in enumerate((hidden_0, hidden_1, hidden_2, hidden_3)):
        hidden[...] = hidden_ref[i * part : (i + 1) * part, :]


def feed_units(hidden_ref, up_ref, down_ref, bias, active_ref, slope_ref, sum_ref, before_ref):
    units = up_ref.shape[1]
    for u in range(0, units, BLOCK):
        for r in range(0, hidden_ref.shape[0], 2 * BLOCK):
            here = slice(r, r + 2 * BLOCK)
            pre_up = bias[:, u : u + BLOCK] + product(hidden_ref[here, :], up_ref[:, u : u + BLOCK])
            cumulative, density = normal_parts(pre_up)
            active = (pre_up * cumulative).astype(BF16)
            active_ref[u : u + BLOCK, here] = active.T
            slope_ref[here, u : u + BLOCK] = (cumulative + pre_up * density).astype(BF16)
            now = product(active, down_ref[u : u + BLOCK, :])
            if u:
                sum_ref[here, :] += now
            elif before_ref is not None:
                sum_ref[here, :] = before_ref[here, :] + now
            else:
                sum_ref[here, :] = now


def feed_kernel(flags_ref, *refs):
    own_refs, other_refs, refs = refs[:4], refs[4:8], refs[8:]
    up_ref, down_ref, bias_ref, hidden_ref, turned_ref, active_ref, slope_ref, sum_ref = refs
    join_parts(flags_ref, own_refs, other_refs, hidden_ref)
    turned_ref[...] = hidden_ref[...].T
    feed_units(hidden_ref, up_ref, down_ref, row(bias_ref), active_ref, slope_ref, sum_ref, None)


def feed_last_kernel(
    flags_ref, hidden_ref, up_a, up_b, up_c, down_a, down_b, down_c, bias_ref, before_ref,
    up_ref, down_ref, active_ref, slope_ref, keep_ref, send_ref, sum_ref,
):
    for (direct, *around), out in (((up_a, up_b, up_c), up_ref), ((down_a, down_b, down_c), down_ref)):
        half = direct.shape[0]
        out[piece(flags_ref[0], half), :] = direct[...]
        for i, ref in enumerate(around):
            out[piece((1 - flags_ref[0]) * 2 + i, half // 2), :] = ref[...]
    feed_units(hidden_ref, up_ref, down_ref, bias_ref[0:1, :], active_ref, slope_ref, sum_ref, before_ref)
    share(flags_ref, sum_ref, keep_ref, send_ref)


def norm_two_kernel(
    keep_ref, got_ref, normal_ref, gain_one_ref, shift_one_ref, down_b_ref, gain_ref, shift_ref, cotangent_ref,
    out_ref, grad_ref, low_ref, vector_ref,
):
    def step(here):
        values = keep_ref[here, :] + got_ref[here, :].astype(F32) + row(down_b_ref)
        values = values + (normal_ref[here, :] * row(gain_one_ref) + row(shift_one_ref))
        centered = values - jnp.mean(values, axis=1, keepdims=True)
        inverse = lax.rsqrt(jnp.mean(centered * centered, axis=1, keepdims=True) + EPSILON)
        normal = centered * inverse
        out_ref[here, :] = (normal * row(gain_ref) + row(shift_ref)).astype(BF16)
        upstream = cotangent_ref[here, :].astype(F32)
        scaled = upstream * row(gain_ref)
        first = jnp.mean(scaled, axis=1, keepdims=True)
        second = jnp.mean(scaled * normal, axis=1, keepdims=True)
        grad = inverse * (scaled - first - normal * second)
        grad_ref[here, :] = grad
        low_ref[here, :] = grad.astype(BF16)
        return upstream * normal, upstream, grad

    rows, model = keep_ref.shape
    vector_ref[...] = jnp.concatenate(strips(rows, step, 3, model) + [jnp.zeros((5, model), F32)], axis=0)


def quarters(flags_ref, size):
    return [pl.ds(pl.multiple_of(jnp.bitwise_xor(flags_ref[4], i) * size, 16), size) for i in range(4)]


def down_back_units(flags_ref, grad_ref, active_ref, down_grad_ref):
    quarter = active_ref.shape[0] // 4
    for i, where in enumerate(quarters(flags_ref, quarter)):
        value = product(active_ref[i * quarter : (i + 1) * quarter, :], grad_ref[...])
        down_grad_ref[where, :] = value.astype(BF16)


def down_back_kernel(flags_ref, own_ref, other_ref, active_ref, grad_ref, down_grad_ref):
    join(flags_ref, own_ref, other_ref, grad_ref)
    down_back_units(flags_ref, grad_ref, active_ref, down_grad_ref)


def feed_back_units(
    flags_ref, grad_ref, slope_ref, hidden_ref, up_ref, down_ref, before_ref, bias_grad_ref, sum_ref, turned_ref, grad_pre_ref,
):
    rows, model = grad_ref.shape
    units = slope_ref.shape[1]
    for u in range(0, units, BLOCK):
        here = slice(u, u + BLOCK)
        total = 0.0
        for r in range(0, rows, 2 * BLOCK):
            grad_active = cols_product(grad_ref[r : r + 2 * BLOCK, :], down_ref[here, :])
            grad_pre = (slope_ref[r : r + 2 * BLOCK, here].astype(F32) * grad_active).astype(BF16)
            grad_pre_ref[r : r + 2 * BLOCK, here] = grad_pre
            total = total + jnp.sum(grad_pre.astype(F32), axis=0, keepdims=True)
            bias_grad_ref[:, here] = jnp.concatenate([total, jnp.zeros((7, total.shape[1]), F32)], axis=0)
    for i, where in enumerate(quarters(flags_ref, model // 4)):
        value = product(hidden_ref[i * (model // 4) : (i + 1) * (model // 4), :], grad_pre_ref[...])
        turned_ref[where, :] = value.astype(BF16)
    for r in range(0, rows, BLOCK):
        value = cols_product(grad_pre_ref[r : r + BLOCK, :], up_ref[...])
        if before_ref is not None:
            value = value + before_ref[r : r + BLOCK, :]
        sum_ref[r : r + BLOCK, :] = value


def split(turned_ref, keep_ref, sends, first):
    quarter, half = turned_ref.shape[0] // 4, turned_ref.shape[1] // 2
    for columns, (stay, go), send in ((slice(0, half), ((0, 2), (1, 3)), 0), (slice(half, 2 * half), ((0, 1), (2, 3)), 1)):
        for i in range(2):
            there = slice(i * quarter, (i + 1) * quarter)
            keep_ref[there, columns] = turned_ref[stay[i] * quarter : (stay[i] + 1) * quarter, columns]
            there = slice(first + i * quarter, first + (i + 1) * quarter)
            sends[send][there, :] = turned_ref[go[i] * quarter : (go[i] + 1) * quarter, columns]


def feed_back_theirs_kernel(
    flags_ref, grad_ref, slope_ref, hidden_ref, up_ref, down_ref,
    keep_up, send_y, send_z, bias_grad_ref, sum_ref, turned_ref, grad_pre_ref,
):
    feed_back_units(
        flags_ref, grad_ref, slope_ref, hidden_ref, up_ref, down_ref, None, bias_grad_ref, sum_ref, turned_ref, grad_pre_ref
    )
    split(turned_ref, keep_up, (send_y, send_z), 0)


def feed_back_mine_kernel(
    flags_ref, grad_ref, active_ref, slope_ref, hidden_ref, up_ref, down_ref, before_ref,
    theirs_y, theirs_z, grad_two_ref, down_grad_ref, keep_up, send_y, send_z, bias_grad_ref, keep_ref, send_0, send_1, send_2, send_3, sum_ref, turned_ref, grad_pre_ref,
):
    down_back_units(flags_ref, grad_ref, active_ref, down_grad_ref)
    feed_back_units(
        flags_ref, grad_ref, slope_ref, hidden_ref, up_ref, down_ref, before_ref,
        bias_grad_ref, sum_ref, turned_ref, grad_pre_ref,
    )
    half = theirs_y.shape[0]
    send_y[:half, :] = theirs_y[...]
    send_z[:half, :] = theirs_z[...]
    split(turned_ref, keep_up, (send_y, send_z), half)
    share(flags_ref, sum_ref, keep_ref, send_0, send_1, send_2, send_3)
    keep_ref[...] += grad_two_ref[...]


def norm_one_back_kernel(
    keep_ref, got_0, got_1, got_2, got_3, normal_ref, inverse_ref, gain_ref, two_ref,
    grad_ref, low_a, low_b, got_ref, low_ref, vector_ref,
):
    part, half = got_0.shape[0], low_a.shape[0]
    for i, got in enumerate((got_0, got_1, got_2, got_3)):
        got_ref[i * part : (i + 1) * part, :] = got[...]

    def step(here):
        upstream, normal = keep_ref[here, :] + got_ref[here, :].astype(F32), normal_ref[here, :]
        scaled = upstream * row(gain_ref)
        first = jnp.mean(scaled, axis=1, keepdims=True)
        second = jnp.mean(scaled * normal, axis=1, keepdims=True)
        grad = inverse_ref[here, :] * (scaled - first - normal * second)
        grad_ref[here, :] = grad
        low_ref[here, :] = grad.astype(BF16)
        return grad, upstream * normal, upstream

    rows, model = keep_ref.shape
    vector_ref[...] = jnp.concatenate(
        strips(rows, step, 3, model) + [two_ref[0:3, :], jnp.zeros((2, model), F32)], axis=0
    )
    low_a[...] = low_ref[:half, :]
    low_b[:half, :] = low_ref[half:, :]
    blank = jnp.zeros((BIAS_ROWS - 8, model), F32)
    low_b[half:, :] = jnp.concatenate([vector_ref[...], blank], axis=0).astype(BF16)


def attend_back_kernel(
    flags_ref, own_a, own_b, other_a, other_b, up_sum_ref,
    x_ref, heads_ref, context_ref, log_ref, w_ref, left_ref, right_ref, plain_ref,
    grad_ref, grad_heads_ref, inner_ref, turned_ref, keys_ref, values_ref,
):
    rows, model = x_ref.shape
    width = context_ref.shape[0]
    heads = width // HEAD_DIM
    size = width + BIAS_ROWS
    half = own_a.shape[0]
    join_parts(flags_ref, (own_a, own_b), (other_a, other_b), grad_ref)
    blank = jnp.zeros((2 * BLOCK, LANES - HEAD_DIM), BF16)
    for r in range(0, rows, 2 * BLOCK):
        here = slice(r, r + 2 * BLOCK)
        low = cols_product(grad_ref[here, :], w_ref[3 * width :, :]).astype(BF16)
        turned = low.T.astype(F32) * context_ref[:, here]
        for h in range(heads):
            part = slice(h * HEAD_DIM, (h + 1) * HEAD_DIM)
            grad_heads_ref[h, here, :] = jnp.concatenate([low[:, part], blank], axis=1)
            inner_ref[h : h + 1, here] = jnp.sum(turned[part, :], axis=0, keepdims=True)
    keys_ref[...] = jnp.zeros_like(keys_ref)
    values_ref[...] = jnp.zeros_like(values_ref)
    for i in range(rows // BLOCK):
        here, seen = slice(i * BLOCK, (i + 1) * BLOCK), window(i, rows)
        for h in range(heads):
            queries, grads, key_rows = heads_ref[h, here, :], grad_heads_ref[h, here, :], heads_ref[heads + h, seen, :]
            probs = jnp.exp(cols_product(key_rows, queries) - log_ref[h : h + 1, here])
            grad_probs = cols_product(heads_ref[2 * heads + h, seen, :], grads)
            grad_scores = (probs * (grad_probs - inner_ref[h : h + 1, here])).astype(BF16)
            values_ref[h, seen, :] += product(probs.astype(BF16), grads)
            keys_ref[h, seen, :] += product(grad_scores, queries)
            grad_queries = rows_product(key_rows, grad_scores)[:HEAD_DIM, :] * (HEAD_DIM**-0.5)
            turned_ref[h * HEAD_DIM : (h + 1) * HEAD_DIM, here] = grad_queries.astype(BF16)
    for i, ref in ((1, keys_ref), (2, values_ref)):
        for h in range(heads):
            first = i * width + h * HEAD_DIM
            turned_ref[first : first + HEAD_DIM, :] = ref[h].T[:HEAD_DIM, :].astype(BF16)
    for i in range(3):
        plain_ref[:, i * 2 * LANES : i * 2 * LANES + width] = turned_ref[i * width : (i + 1) * width, :].T
    tops = [jnp.zeros((8, model), F32)] * 4
    for i in (0, 2):
        top = jnp.sum(plain_ref[:, i * 2 * LANES : i * 2 * LANES + width].astype(F32), axis=0, keepdims=True)
        top = jnp.concatenate([top, jnp.zeros((1, model - width), F32)], axis=1)
        tops[i] = jnp.concatenate([top, jnp.zeros((7, model), F32)], axis=0)
    tops[1] = up_sum_ref[...]
    vectors = [ref[half : half + BIAS_ROWS, :].astype(F32)[:8] for ref in (own_b, other_b)]
    tops[3] = vectors[0] + vectors[1]
    for i, here in enumerate(quarters(flags_ref, size)):
        if i < 3:
            grad = product(turned_ref[i * width : (i + 1) * width, :], x_ref[...])
        else:
            grad = product(context_ref[...].astype(BF16), grad_ref[...])
        blank = jnp.zeros((BIAS_ROWS - 8, model), F32)
        value = jnp.concatenate([grad, tops[i], blank], axis=0).astype(BF16)
        left_ref[here, :] = value[:, :LEFT]
        right_ref[here, :] = value[:, LEFT:]


def tokens_kernel(flags_ref, grad_ref, plain_0, plain_2, w_0, w_2, keep_ref, send_ref, sum_ref):
    rows, model = plain_0.shape[0], grad_ref.shape[1]
    width = w_0.shape[0] // 4
    for r in range(0, rows, BLOCK):
        total = 0.0
        for plain, w_ref in ((plain_0, w_0), (plain_2, w_2)):
            for i in range(3):
                total = total + product(
                    plain[r : r + BLOCK, i * 2 * LANES : i * 2 * LANES + width], w_ref[i * width : (i + 1) * width, :]
                )
        sum_ref[r : r + BLOCK, :] = total
    share(flags_ref, sum_ref, keep_ref, send_ref)
    keep_ref[...] += grad_ref[...]


def last_kernel(keep_ref, got_ref, out_ref):
    out_ref[...] = keep_ref[...] + got_ref[...].astype(F32)


def unpack_kernel(
    flags_ref, part_0, part_1, part_2, part_3,
    query_ref, key_ref, value_ref, out_w_ref, query_b_ref, value_b_ref, up_b_ref, *refs,
):
    vector_refs, parts = refs[:-1], refs[-1]
    for i, ref in enumerate((part_0, part_1, part_2, part_3)):
        parts[jnp.bitwise_xor(flags_ref[4], i)] = ref[...]
    width = query_ref.shape[0]
    for i, ref in enumerate((query_ref, key_ref, value_ref, out_w_ref)):
        ref[...] = parts[i, :width, :].astype(F32)
    tops = [parts[i, width : width + BIAS_ROWS, :].astype(F32) for i in range(4)]
    query_b_ref[...] = tops[0][0, :width]
    value_b_ref[...] = tops[2][0, :width]
    up_b_ref[...] = tops[1][0, :]
    for i, ref in enumerate(vector_refs):
        ref[...] = tops[3][i, :]


def tie(*arrays):
    return lax.optimization_barrier(arrays)


def add(*members):
    members = [m.astype(F32) for m in members]
    while len(members) > 1:
        members = [a + b for a, b in zip(members[::2], members[1::2])]
    return members[0].astype(BF16)


class Swaps:
    def __init__(self, dp_size, replica):
        self.dp_size, self.near = dp_size, replica & 3

    def core(self, values_in):
        return lax.ppermute(values_in, "tensor", [(i, i ^ 1) for i in range(4)])

    def chip(self, values_in):
        return lax.ppermute(values_in, "tensor", [(i, i ^ 2) for i in range(4)])

    def replica(self, values_in, mask):
        return lax.ppermute(values_in, "dp", [(i, i ^ mask) for i in range(self.dp_size)])

    def scatter(self, parts):
        got = {m: self.replica(parts[m], m) for m in (3, 1, 2)}
        return [got[m] for m in (1, 2, 3)]

    def far(self, value, mask):
        return self.replica(value, mask)

    def gather(self, value):
        got = {m: self.replica(value, m) for m in (3, 1, 2)}
        return [got[m] for m in (1, 2, 3)]

    @property
    def far_masks(self):
        return [1 << b for b in range(2, self.dp_size.bit_length() - 1)]

    def placed(self, members):
        return [lax.select_n(self.near, *[members[i ^ p] for p in range(4)]) for i in range(4)]


def cut_pair(value):
    half = value.shape[0] // 2
    return [value[:half], value[half:]]


def cut(value):
    size = value.shape[0] // 4
    return [value[i * size : (i + 1) * size] for i in range(4)]


def first_calls(
    flags, query_bias, value_bias, up_bias, query_weight, key_weight, value_weight, out_weight, up_weight, down_weight,
):
    model, width = query_weight.shape
    far, vmem = pl.BlockSpec(memory_space=pl.ANY), pl.BlockSpec(memory_space=pltpu.VMEM)
    smem = pl.BlockSpec(memory_space=pltpu.SMEM)
    params = dict(
        compiler_params=pltpu.CompilerParams(vmem_limit_bytes=PACK_LIMIT),
        cost_estimate=pl.CostEstimate(flops=0, bytes_accessed=0, transcendentals=0),
    )
    weights = (query_weight.T, key_weight.T, value_weight.T, out_weight)
    shapes = [(width + BIAS_ROWS, model), (width, model)]
    pieces = pl.pallas_call(
        pieces_kernel,
        in_specs=[smem] + [vmem] * 3 + [far] * 4,
        out_specs=[vmem] * 2,
        out_shape=[jax.ShapeDtypeStruct(s, BF16) for s in shapes],
        scratch_shapes=[pltpu.SemaphoreType.DMA((2,))],
        **params,
    )(flags, query_bias, value_bias, up_bias, *weights)
    pieces, weights = tie(pieces, weights)
    halves = [(w.shape[0] // 2, w.shape[1]) for w in (up_weight, down_weight)]
    outs = [(4 * width, model)] + halves
    rest = pl.pallas_call(
        pack_kernel,
        in_specs=[smem] + [far] * 6,
        out_specs=[far] * 3,
        out_shape=[jax.ShapeDtypeStruct(s, BF16) for s in outs],
        scratch_shapes=[pltpu.VMEM(s, BF16) for s in outs] + [pltpu.SemaphoreType.DMA((9,))],
        **params,
    )(flags, *weights, up_weight, down_weight)
    return [*pieces, *rest]


def body(
    dp_size,
    tokens,
    lengths,
    cotangent,
    query_weight,
    query_bias,
    key_weight,
    value_weight,
    value_bias,
    out_weight,
    out_bias,
    gain_one,
    shift_one,
    up_weight,
    up_bias,
    down_weight,
    down_bias,
    gain_two,
    shift_two,
):
    own, model = tokens.shape
    width = query_weight.shape[1]
    units = up_weight.shape[1]
    rows = 2 * own
    place = lax.axis_index("tensor")
    replica = lax.axis_index("dp")
    flags = [(replica ^ (replica >> 1)) & 1, place % 2, place // 2, place, replica & 3, (replica >> 1) & 1, replica & 1]
    flags = jnp.stack(flags).astype(jnp.int32)
    swaps = Swaps(dp_size, replica)
    swap_core, swap_chip, swap_replica = swaps.core, swaps.chip, swaps.replica
    far_masks = swaps.far_masks

    other_tokens = swap_core(tokens)
    pack_a, pack_b, pack, up_half, down_half = first_calls(
        flags, query_bias, value_bias, up_bias, query_weight, key_weight, value_weight, out_weight, up_weight, down_weight
    )
    whole, half_row = (4 * (width + BIAS_ROWS), model), (own, model)
    halves, fourths = [((own // 2, model), BF16)] * 2, [((own // 4, model), BF16)] * 4
    heads_shape = ((3 * width // HEAD_DIM, rows, LANES), BF16)
    values_scratch = pltpu.VMEM((width, rows), BF16)
    kept_shapes = [((width, rows), F32), ((8, rows), F32)]
    direct = [swap_chip(pack_a), swap_chip(pack_b)]
    up_direct, down_direct = swap_chip(up_half), swap_chip(down_half)

    inputs, qkv_0, context_0, turned_0, log_0 = call(
        attend_kernel,
        [((rows, model), BF16), heads_shape, ((rows, width), BF16)] + kept_shapes,
        (flags, lengths, pack, query_bias, value_bias, tokens, other_tokens),
        scalars=2,
        scratch=[values_scratch],
    )
    *direct, inputs = tie(*direct, inputs)
    around = [swap_replica(direct[0], 1), swap_replica(direct[1], 2)]
    *around, inputs = tie(*around, inputs)
    pack_2, qkv_2, turned_2, log_2, bias_2, keep, *sends = call(
        attend_last_kernel,
        [((4 * width, model), BF16), heads_shape] + kept_shapes + [((8, model), F32), (half_row, F32)] + fourths,
        (flags, lengths, *direct, *around, inputs, context_0, pack),
        scalars=2,
        scratch=[values_scratch, pltpu.VMEM((rows, width), BF16), pltpu.VMEM((rows, model), F32)],
    )
    *sends, up_direct = tie(*sends, up_direct)
    got = [swap_core(v) for v in sends]
    fourth = model // 4
    up_around = [swap_replica(up_direct[:fourth], 1), swap_replica(up_direct[fourth:], 2)]
    normal_one, inverse_one, *hidden = call(
        norm_one_kernel,
        [(half_row, F32), ((own, 1), F32)] + fourths,
        (tokens, keep, *got, out_bias, gain_one, shift_one),
        scratch=[pltpu.VMEM(half_row, BF16)] * 2,
    )
    other_hidden = [swap_core(v) for v in hidden]
    hidden[0], down_direct, *held = tie(hidden[0], down_direct, *other_hidden, *up_around)
    other_hidden, up_around = held[:4], held[4:]
    fourth = units // 4
    down_around = [swap_replica(down_direct[:fourth], 1), swap_replica(down_direct[fourth:], 2)]

    act_shapes = [((units, rows), BF16), ((rows, units), BF16)]
    hidden_full, hidden_turned, active_0, slope_0, before = call(
        feed_kernel,
        [((rows, model), BF16), ((model, rows), BF16)] + act_shapes + [((rows, model), F32)],
        (flags, *hidden, *other_hidden, up_weight, down_weight, up_bias),
        scalars=1,
    )
    before, *down_around = tie(before, *down_around)
    up_2, down_2, active_2, slope_2, keep, send = call(
        feed_last_kernel,
        [((model, units), BF16), ((units, model), BF16)] + act_shapes + [(half_row, F32), (half_row, BF16)],
        (flags, hidden_full, up_direct, *up_around, down_direct, *down_around, bias_2, before),
        scalars=1,
        scratch=[pltpu.VMEM((rows, model), F32)],
    )
    layer_output, grad_two, low_grad_two, vector_two = call(
        norm_two_kernel,
        [(half_row, BF16), (half_row, F32), (half_row, BF16), ((8, model), F32)],
        (
            keep, swap_core(send), normal_one, gain_one, shift_one, down_bias,
            gain_two, shift_two, cotangent,
        ),
    )

    back_scratch = [pltpu.VMEM((model, units), BF16), pltpu.VMEM((rows, units), BF16)]
    grad_full, down_theirs = call(
        down_back_kernel,
        [((rows, model), BF16), ((units, model), BF16)],
        (flags, low_grad_two, swap_core(low_grad_two), active_2),
        scalars=1,
    )
    down_theirs, grad_full = tie(down_theirs, grad_full)
    down_chip = swap_chip(down_theirs)
    up_keep_2, *up_sends, up_sum_2, running = call(
        feed_back_theirs_kernel,
        [((model // 2, units), BF16)] + [((model // 2, units // 2), BF16)] * 2 + [((8, units), F32), ((rows, model), F32)],
        (flags, grad_full, slope_2, hidden_turned, up_2, down_2),
        scalars=1,
        scratch=back_scratch,
    )
    down_mine, up_keep_0, *up_sends, up_sum_0, keep, send_0, send_1, send_2, send_3 = call(
        feed_back_mine_kernel,
        [((units, model), BF16), ((model // 2, units), BF16)] + [((model, units // 2), BF16)] * 2
        + [((8, units), F32), (half_row, F32)]
        + [((own // 4, model), BF16)] * 4,
        (
            flags, grad_full, active_0, slope_0, hidden_turned, up_weight, down_weight, running, *up_sends, grad_two,
        ),
        scalars=1,
        scratch=[pltpu.VMEM((rows, model), F32)] + back_scratch,
    )
    up_got = [swap_replica(up_sends[0], 1), swap_replica(up_sends[1], 2)]
    got = [swap_core(v) for v in (send_0, send_1, send_2, send_3)]
    grad_one, low_a, low_b = call(
        norm_one_back_kernel,
        [(half_row, F32), halves[0], ((own // 2 + BIAS_ROWS, model), BF16)],
        (keep, *got, normal_one, inverse_one, gain_one, vector_two),
        scratch=[pltpu.VMEM(half_row, BF16)] * 2 + [pltpu.VMEM((8, model), F32)],
    )
    low_other = [swap_core(low_a), swap_core(low_b)]


    def attend_back(low_a, qkv, turned, log_total, shard, up_sum):
        return call(
            attend_back_kernel,
            [((whole[0], LEFT), BF16), ((whole[0], model - LEFT), BF16), ((rows, 6 * LANES), BF16)],
            (
                flags, low_a, low_b, *low_other, up_sum,
                inputs, qkv, turned, log_total, shard,
            ),
            scalars=1,
            scratch=[
                pltpu.VMEM((rows, model), BF16), pltpu.VMEM((width // HEAD_DIM, rows, LANES), BF16),
                pltpu.VMEM((8, rows), F32), pltpu.VMEM((3 * width, rows), BF16),
                pltpu.VMEM((width // HEAD_DIM, rows, LANES), F32), pltpu.VMEM((width // HEAD_DIM, rows, LANES), F32),
            ],
        )

    left_theirs, right_theirs, plain_2 = attend_back(low_a, qkv_2, turned_2, log_2, pack_2, up_sum_2)

    left_theirs, right_theirs, low_a, down_chip, *up_got = tie(left_theirs, right_theirs, low_a, down_chip, *up_got)
    left_chip, right_chip = swap_chip(left_theirs), swap_chip(right_theirs)
    down_parts = [add(m, t) for m, t in zip(cut(down_mine), cut(down_chip))]
    up_theirs, up_mine = [
        add(keep_up, jnp.concatenate([got_up[here] for got_up in up_got], axis=1))
        for keep_up, here in ((up_keep_2, slice(0, model // 2)), (up_keep_0, slice(model // 2, model)))
    ]
    up_theirs, up_mine, low_a, *down_parts = tie(up_theirs, up_mine, low_a, *down_parts)
    down_got = swaps.scatter(down_parts)
    left_mine, right_mine, plain_0 = attend_back(low_a, qkv_0, turned_0, log_0, pack, up_sum_0)
    keep, send = call(
        tokens_kernel,
        [(half_row, F32), (half_row, BF16)],
        (flags, grad_one, plain_0, plain_2, pack, pack_2),
        scalars=1,
        scratch=[pltpu.VMEM((rows, model), F32)],
    )
    left_mine, keep, send, left_chip, *down_got = tie(left_mine, keep, send, left_chip, *down_got)
    left_parts = [add(m, t) for m, t in zip(cut(left_mine), cut(left_chip))]
    down_now = add(down_parts[0], *down_got)
    down_now, *left_parts = tie(down_now, *left_parts)
    left_got = swaps.scatter(left_parts)
    down_far = swaps.far(down_now, far_masks[0])
    right_chip, right_mine, down_far, up_theirs, *left_got = tie(right_chip, right_mine, down_far, up_theirs, *left_got)
    right_parts = [add(m, t) for m, t in zip(cut(right_mine), cut(right_chip))]
    left_now = add(left_parts[0], *left_got)
    down_now = add(down_now, down_far)
    for mask in far_masks[1:]:
        down_now = add(down_now, swaps.far(down_now, mask))
    left_now, down_now, up_theirs, *right_parts = tie(left_now, down_now, up_theirs, *right_parts)
    right_got = swaps.scatter(right_parts)
    up_chip = swap_chip(up_theirs)
    left_far = swaps.far(left_now, far_masks[0])
    up_chip, left_far, *right_got = tie(up_chip, left_far, *right_got)
    right_now, left_now = add(right_parts[0], *right_got), add(left_now, left_far)
    up_now, up_next = [add(m, t) for m, t in zip(cut_pair(up_mine), cut_pair(up_chip))]
    up_next = [up_next[:, : units // 2], up_next[:, units // 2 :]]
    right_now, left_now, up_now, up_next[0], up_next[1], down_now = tie(right_now, left_now, up_now, *up_next, down_now)
    right_far = swaps.far(right_now, far_masks[0])
    down_other = swap_replica(down_now, 2)
    up_got = [swap_replica(up_next[0], 2), swap_replica(up_next[1], 1)]
    right_far, down_other, *up_got = tie(right_far, down_other, *up_got)
    right_now, up_now = add(right_now, right_far), add(up_now, jnp.concatenate(up_got, axis=1))
    down_pair = jnp.concatenate([down_now, down_other], axis=0)
    pack_now = jnp.concatenate([left_now, right_now], axis=1)
    for mask in far_masks[1:]:
        pack_now = add(pack_now, swaps.far(pack_now, mask))
    pack_now, up_now, down_pair = tie(pack_now, up_now, down_pair)
    pack_all = [pack_now] + swaps.gather(pack_now)
    down_other = swap_replica(down_pair, 1)
    up_far = swaps.far(up_now, far_masks[0])
    up_far, down_other, send = tie(up_far, down_other, send)
    up_now = add(up_now, up_far)
    for mask in far_masks[1:]:
        up_now = add(up_now, swaps.far(up_now, mask))
    up_now, late_flags, send = tie(up_now, flags, send)
    up_all = [up_now] + swaps.gather(up_now)
    (tokens_grad,) = call(last_kernel, [(half_row, F32)], (keep, swap_core(send)))
    first, second = cut_pair(down_pair), cut_pair(down_other)
    down_all = [first[0], second[0], first[1], second[1]]
    down_weight_grad = jnp.concatenate(swaps.placed(down_all), axis=0).astype(F32)
    up_weight_grad = jnp.concatenate(swaps.placed(up_all), axis=0).astype(F32)
    shard = [((width, model), F32)] * 4 + [((width,), F32)] * 2 + [((units,), F32)] + [((model,), F32)] * 6
    (
        query_grad, key_grad, value_grad, out_grad, query_bias_grad, value_bias_grad, up_bias_row, *vectors,
    ) = call(
        unpack_kernel, shard, (late_flags, *pack_all), scalars=1, scratch=[pltpu.VMEM((4, width + BIAS_ROWS, model), BF16)]
    )
    return (
        layer_output,
        tokens_grad,
        query_grad.T,
        query_bias_grad,
        key_grad.T,
        value_grad.T,
        value_bias_grad,
        out_grad,
        vectors[0],
        vectors[1],
        vectors[2],
        up_weight_grad,
        up_bias_row,
        down_weight_grad,
        vectors[5],
        vectors[3],
        vectors[4],
    )


def solution(mesh):
    placed = (
        P(("dp", "tensor"), None),
        P("dp", None),
        P(("dp", "tensor"), None),
        P(None, "tensor"),
        P("tensor"),
        P(None, "tensor"),
        P(None, "tensor"),
        P("tensor"),
        P("tensor", None),
        P(),
        P(),
        P(),
        P(None, "tensor"),
        P("tensor"),
        P("tensor", None),
        P(),
        P(),
        P(),
    )
    return jax.shard_map(
        functools.partial(body, mesh.shape["dp"]),
        mesh=mesh,
        in_specs=placed,
        out_specs=(
            P(("dp", "tensor"), None),
            P(("dp", "tensor"), None),
            P(None, "tensor"),
            P("tensor"),
            P(None, "tensor"),
            P(None, "tensor"),
            P("tensor"),
            P("tensor", None),
            P(),
            P(),
            P(),
            P(None, "tensor"),
            P("tensor"),
            P("tensor", None),
            P(),
            P(),
            P(),
        ),
        check_vma=False,
    )
```
